32 devices in a mesh: groups: 2 (over y), gx: 4 (over z), gy: 2 (over x), gz: 2 (over core).
Axes of the slice: x: 2, y: 2, z: 4, core: 2. Of those that a mesh axis runs over, the one named last changes fastest.
Arguments:
- state: float32 [64, 128, 512], P(('groups', 'gx'), 'gy', 'gz'), parts along dimension 0, may hold values from -6 to 6
- conduct: float32 [32, 128, 512], P('gx', 'gy', 'gz'), may hold values from 0.3 to 3
- sink: float32 [64, 128, 512], P(('groups', 'gx'), 'gy', 'gz'), parts along dimension 0, may hold values from 0.3 to 3
- labels: int32 [64, 128, 512], P(('groups', 'gx'), 'gy', 'gz'), parts along dimension 0, may hold values from 0 to 3
- cotangent: float32 [64, 128, 512], P(('groups', 'gx'), 'gy', 'gz'), parts along dimension 0, may hold values from -6 to 6
Outputs:
- grad_state: float32 [64, 128, 512], P(('groups', 'gx'), 'gy', 'gz'), parts along dimension 0
- grad_sink: float32 [64, 128, 512], P(('groups', 'gx'), 'gy', 'gz'), parts along dimension 0
The draws below stay inside these ranges and needn't reach their ends.
There are 2 independent parts, one for each index of `groups`. The reference program is written for one: setup_inputs(seed, part) draws one part's arguments, and reference() takes and returns one part's arrays. A program takes and returns all parts, laid end to end along the dimension named above; an argument that names none is the same for every part. Nothing has to cross between parts.
Inputs may be any that keep to these rules, and one draw needn't show every extreme that they name: `labels`: each cell's class as in the meaning.
All inputs are finite; a program needn't handle non-finite values.
Results may differ from the reference program's by a relative error of at most 0.00002.
Values sent between devices are 32-bit elements; how exact they have to be, the bound alone decides.
No kernel may reach another device: no remote copies, remote signals or barrier semaphores. Data moves between devices by JAX's collectives and lax.ppermute only.
A program may use at most 64 MiB of HBM per device.

```python
import math
import jax
import jax.numpy as jnp

NX = 32
NY = 128
NZ = 512


def with_ends(entries, stream_key, low, top_value):
    shape = entries.shape
    spot = [jax.random.randint(jax.random.fold_in(stream_key, axis), (), 0, shape[axis]) for axis in range(len(shape))]
    entries = entries.at[tuple(spot)].set(low)
    longest = shape.index(max(shape))
    spot[longest] = (spot[longest] + 1) % shape[longest]
    return entries.at[tuple(spot)].set(top_value)


def steps_of(stream_key, dims, shards, smallest, largest):
    loudness, own = 1.0, jax.random.fold_in(stream_key, 6)
    for axis_at, blocks in shards:
        draws = jnp.exp(jax.random.uniform(jax.random.fold_in(own, axis_at), (blocks,), jnp.float32, smallest / len(shards), largest / len(shards)))
        loudness = loudness * jnp.repeat(draws, dims[axis_at] // blocks).reshape([-1 if axis == axis_at else 1 for axis in range(len(dims))])
    return loudness


def scatter_about(key, shape, deviation, bound, cuts=(), kind=jnp.bfloat16):
    entries = deviation * jax.random.normal(key, shape, jnp.float32)
    if cuts:
        entries = entries * steps_of(key, shape, cuts, -0.22, 0.18)
    return jnp.clip(entries, -bound, bound).astype(kind)


def setup_inputs(seed: int = 0, part: int = 0) -> dict:
    key_list = jax.random.split(jax.random.key(seed), 6)
    own_keys = jax.random.split(jax.random.fold_in(key_list[5], part), 6)
    state = scatter_about(own_keys[0], (NX, NY, NZ), 1.0, 6.0, ((0, 4), (1, 2), (2, 2)), jnp.float32)
    conduct = jnp.clip(jnp.exp(math.log(3.0) - 2.3025851 * jax.random.uniform(key_list[1], (NX, NY, NZ), jnp.float32) ** steps_of(key_list[1], (NX, NY, NZ), ((0, 4), (1, 2), (2, 2)), -0.2, 0.2)), 0.3, 3.0)
    sink = jnp.clip(jnp.exp(math.log(3.0) - 2.3025851 * jax.random.uniform(own_keys[2], (NX, NY, NZ), jnp.float32) ** steps_of(own_keys[2], (NX, NY, NZ), ((0, 4), (1, 2), (2, 2)), -0.2, 0.2)), 0.3, 3.0)
    labels = with_ends(jax.random.randint(own_keys[3], (NX, NY, NZ), 0, 4), jax.random.fold_in(own_keys[3], 1), 0, 3).astype(jnp.int32)
    cotangent = scatter_about(own_keys[4], (NX, NY, NZ), 1.0, 6.0, ((0, 4), (1, 2), (2, 2)), jnp.float32)
    return {"state": state, "conduct": conduct, "sink": sink, "labels": labels, "cotangent": cotangent}


velocity = 0.5
time_step = 0.06

def window(array, axis, offset):
    index = []
    for which in range(3):
        if which == axis:
            if offset == 0:
                index.append(slice(0, -2))
            elif offset == 1:
                index.append(slice(1, -1))
            else:
                index.append(slice(2, None))
        else:
            index.append(slice(1, -1))
    return array[tuple(index)]

def diffuse(padded, conduct_pad):
    centre = window(padded, 0, 1)
    middle = window(conduct_pad, 0, 1)
    total = jnp.zeros_like(centre)
    for axis in range(3):
        for offset in (2, 0):
            total = total + 0.5 * (middle + window(conduct_pad, axis, offset)) * (window(padded, axis, offset) - centre)
    return total

def rates(padded, conduct_pad, fluid, capacity, sink_term):
    centre = window(padded, 0, 1)
    advect = -velocity * fluid * (centre - window(padded, 0, 0))
    source = -sink_term * jnp.tanh(centre)
    return (diffuse(padded, conduct_pad) + advect + source) / capacity

def wrap_pad(field):
    looped = jnp.pad(field, ((1, 1), (0, 0), (0, 0)), mode='wrap')
    return jnp.pad(looped, ((0, 0), (1, 1), (1, 1)))

def reference(state, conduct, sink, labels, cotangent):
    fluid = (labels <= 1).astype(jnp.float32)
    solid = (labels >= 2).astype(jnp.float32)
    interface = jnp.logical_or(labels == 1, labels == 2).astype(jnp.float32)
    capacity = 1.0 + solid
    sink_term = sink * interface
    conduct_pad = wrap_pad(conduct)

    def advance(start, term):

        def rate(field):
            return rates(wrap_pad(field), conduct_pad, fluid, capacity, term)
        first = start + time_step * rate(start)
        second = 0.75 * start + 0.25 * (first + time_step * rate(first))
        return start / 3.0 + 2.0 / 3.0 * (second + time_step * rate(second))
    final, pull = jax.vjp(advance, state, sink_term)
    grad_state, grad_term = pull(cotangent)
    return (grad_state, grad_term * interface)
```

```python
import functools

import jax
import jax.numpy as jnp
from jax import lax
from jax.experimental import pallas as pl
from jax.experimental.pallas import tpu as pltpu
from jax.sharding import PartitionSpec as P

VMEM = pltpu.VMEM
time_step = 0.06
HALO = 4
TILE = 8
S, C, T, F, K = range(5)


def call(kernel, outs, *ins, keep=True):
    space = VMEM if keep else jax.ShapeDtypeStruct
    return pl.pallas_call(
        kernel,
        out_shape=[space(shape, jnp.float32) for shape in outs],
        in_specs=[pl.BlockSpec(memory_space=VMEM)] * len(ins),
        out_specs=[pl.BlockSpec(memory_space=VMEM)] * len(outs),
        compiler_params=pltpu.CompilerParams(vmem_limit_bytes=8 * 1024 * 1024),
    )(*[pltpu.with_memory_space_constraint(x, VMEM) for x in ins])


def half_fluid(labels):
    return jnp.where(labels <= 1, 0.5, 0.0)


def touching(labels):
    return jnp.logical_or(labels == 1, labels == 2)


def rows_of(shape):
    return lax.broadcasted_iota(jnp.int32, shape, 0)


def lanes_of(shape):
    return lax.broadcasted_iota(jnp.int32, shape, 1)


def down_rows(before, here):
    return pltpu.roll(jnp.where(rows_of(here.shape) == TILE - 1, before, here), 1, 0)


def up_rows(here, after):
    return pltpu.roll(jnp.where(rows_of(here.shape) == 0, after, here), TILE - 1, 0)


def down_lanes(here):
    return pltpu.roll(here, 1, 1)


def up_lanes(here):
    return pltpu.roll(here, here.shape[1] - 1, 1)


def across(ky, kz, v):
    count = len(v)
    py = [a * b for a, b in zip(ky, v)]
    out = []
    for t in range(count):
        before, after = (t - 1) % count, (t + 1) % count
        total = ky[t] * down_rows(v[before], v[t]) + up_rows(py[t], py[after])
        pz = kz[t] * v[t]
        out.append(total + (kz[t] * down_lanes(v[t]) + up_lanes(pz)))
    return out


def tiles(main, ghost):
    count = main.shape[0] // TILE
    return [main[t * TILE : (t + 1) * TILE] for t in range(count)] + [ghost[...]]


def split(ref):
    return [ref[t * TILE : (t + 1) * TILE] for t in range(ref.shape[0] // TILE)]


def put(ref, values):
    for t, value in enumerate(values):
        ref[t * TILE : (t + 1) * TILE] = value


def pack_inputs(state, conduct, sink, labels, cotangent, up, down, trade):
    core = lax.axis_index("gz")
    count = state.shape[0]
    half = count // 2
    for out, plane in ((up, count - 1), (down, 0)):
        out[S] = state[plane]
        out[C] = conduct[plane]
        out[T] = cotangent[plane]
        out[F] = half_fluid(labels[plane])
    first = (1 - core) * half
    for i in range(half):
        trade[S, i] = state[first + i]
        trade[C, i] = conduct[first + i]
        trade[T, i] = cotangent[first + i]
        trade[F, i] = half_fluid(labels[first + i])
        trade[K, i] = jnp.where(touching(labels[first + i]), sink[first + i], 0.0)


def gather_planes(two, state, conduct, sink, labels, cotangent, traded, block, *rims):
    core = lax.axis_index("gz")
    half, wide = traded.shape[1], traded.shape[3]
    mine = pl.ds(pl.multiple_of(core * wide, 128), wide)
    other = pl.ds(pl.multiple_of((1 - core) * wide, 128), wide)
    first = core * half
    for i in range(half):
        block[S, i, :, mine] = state[first + i]
        block[C, i, :, mine] = conduct[first + i]
        block[T, i, :, mine] = cotangent[first + i]
        block[F, i, :, mine] = half_fluid(labels[first + i])
        block[K, i, :, mine] = jnp.where(touching(labels[first + i]), sink[first + i], 0.0)
        for j in range(5):
            block[j, i, :, other] = traded[j, i]
    ny = block.shape[2]
    for j in range(5):
        for k in range(half // 2):
            even_low, odd_low = block[j, 2 * k, 0:TILE], block[j, 2 * k + 1, 0:TILE]
            even_high, odd_high = block[j, 2 * k, ny - TILE : ny], block[j, 2 * k + 1, ny - TILE : ny]
            upper = rows_of(even_low.shape) < HALO
            low = jnp.where(upper, even_low, pltpu.roll(odd_low, HALO, 0))
            high = jnp.where(upper, pltpu.roll(even_high, HALO, 0), odd_high)
            if two:
                rims[0][j, k] = jnp.where(lax.axis_index("gy") == 0, high, low)
            else:
                rims[0][j, k] = low
                rims[1][j, k] = high


def prepare(two, count_y, block, *refs):
    rims, (ghost, kx, ky, kz, diag, part, back, off, on) = refs[: 1 if two else 2], refs[1 if two else 2 :]
    half = block.shape[1]
    place = lax.axis_index("gy")
    core = lax.axis_index("gz")
    has_low, has_high = place > 0, place < count_y - 1
    for j in range(5):
        for k in range(half // 2):
            above = jnp.where(has_high, rims[0][j, k], 0.0)
            below = jnp.where(has_low, rims[0 if two else 1][j, k], 0.0)
            upper = rows_of(above.shape) < HALO
            ghost[j, 2 * k] = jnp.where(upper, above, pltpu.roll(below, HALO, 0))
            ghost[j, 2 * k + 1] = jnp.where(upper, pltpu.roll(above, HALO, 0), below)
    own = lambda j, i: tiles(block.at[j, i], ghost.at[j, i])
    count = block.shape[2] // TILE + 1
    for i in range(half):
        c = own(C, i)
        rows, lanes = rows_of(c[0].shape), lanes_of(c[0].shape)
        for t in range(count):
            before, after = c[(t - 1) % count], c[(t + 1) % count]
            here = c[t] * (0.5 * time_step)
            low = here + down_rows(before, c[t]) * (0.5 * time_step)
            high = here + up_rows(c[t], after) * (0.5 * time_step)
            left = here + jnp.where(lanes == 0, 0.0, down_lanes(c[t])) * (0.5 * time_step)
            right = here + jnp.where(lanes == lanes.shape[1] - 1, 0.0, up_lanes(c[t])) * (0.5 * time_step)
            total = (low + high) + (left + right) + time_step * own(F, i)[t]
            if i > 0:
                face = here + own(C, i - 1)[t] * (0.5 * time_step)
                kx[i - 1, t * TILE : (t + 1) * TILE] = face
                total = total + face
            if i < half - 1:
                total = total + (here + own(C, i + 1)[t] * (0.5 * time_step))
            diag[i, t * TILE : (t + 1) * TILE] = total
            if t == 0:
                low = jnp.where(jnp.logical_and(rows == 0, jnp.logical_not(has_low)), 0.0, low)
            if t == count - 1:
                low = jnp.where(jnp.logical_and(rows == 0, jnp.logical_not(has_high)), 0.0, low)
            ky[i, t * TILE : (t + 1) * TILE] = low
            kz[i, t * TILE : (t + 1) * TILE] = jnp.where(lanes == 0, 0.0, left)
    for i in range(half):
        s, f, k, c = own(S, i), own(F, i), own(K, i), own(T, i)
        y, z, d = split(ky.at[i]), split(kz.at[i]), split(diag.at[i])
        b = [c[t] * (0.5 + f[t]) for t in range(count)]
        ahead = across(y, z, s)
        behind = across(y, z, b)
        for t in range(count):
            at = slice(t * TILE, (t + 1) * TILE)
            go = ahead[t] - d[t] * s[t]
            come = behind[t] - d[t] * b[t]
            if i > 0:
                go = go + (kx[i - 1, at] + time_step * f[t]) * own(S, i - 1)[t]
                low_b = own(T, i - 1)[t] * (0.5 + own(F, i - 1)[t])
                come = come + kx[i - 1, at] * low_b
            if i < half - 1:
                go = go + kx[i, at] * own(S, i + 1)[t]
                high_f = own(F, i + 1)[t]
                come = come + (kx[i, at] + time_step * high_f) * (own(T, i + 1)[t] * (0.5 + high_f))
            go = go - time_step * k[t] * jnp.tanh(s[t])
            part[i, at] = s[t] + (0.5 + f[t]) * go
            back[i, at] = c[t] + come
    ny = block.shape[2]
    outer = core * (half - 1)
    inner = (1 - core) * (half - 1)
    off[0 : ny + TILE] = part[outer]
    for j in range(4):
        off[ny + (j + 1) * TILE : ny + (j + 2) * TILE] = ghost[j, outer]
        on[j, 0:ny] = block[j, inner]
        on[j, ny : ny + TILE] = ghost[j, inner]
    on[4] = part[inner]


def choose_half(up, down, out):
    core = lax.axis_index("gz")
    out[...] = jnp.where(core == 0, down[...], up[...])


def middle(block, ghost, kx, ky, kz, diag, part, back, up, down, passed, off, on, *refs):
    first, second, sa, b2, fa, edge, full, off2, on2, side = refs
    core = lax.axis_index("gz")
    half, ny = block.shape[1], block.shape[2]
    wide = up.shape[2]
    count = ny // TILE + 1
    last = half - 1
    own = lambda j, i: tiles(block.at[j, i], ghost.at[j, i])
    near = core
    far = 1 - core
    for j in range(4):
        side[j, near, 0:ny, 0:wide] = jnp.where(core == 0, up[j], passed[j])
        side[j, near, 0:ny, wide : 2 * wide] = jnp.where(core == 0, passed[j], down[j])
        side[j, near, ny : ny + TILE] = off[ny + (j + 1) * TILE : ny + (j + 2) * TILE]
        side[j, far] = on[j]
    side[4, near] = off[0 : ny + TILE]
    side[4, far] = on[4]
    scale = 0.5 * time_step
    for t in range(count):
        at = slice(t * TILE, (t + 1) * TILE)
        low_c, high_c = side[C, 0, at], side[C, 1, at]
        low = (own(C, 0)[t] + low_c) * scale
        high = (own(C, last)[t] + high_c) * scale
        edge[0, at] = low
        edge[1, at] = high
        for i in range(half):
            d = diag[i, at]
            if i == 0:
                d = d + low
            if i == last:
                d = d + high
            full[i, at] = d
        s0, s1 = own(S, 0)[t], own(S, last)[t]
        f0, f1 = own(F, 0)[t], own(F, last)[t]
        sl, sh = side[S, 0, at], side[S, 1, at]
        fl, fh = side[F, 0, at], side[F, 1, at]
        first[0, at] = side[4, 0, at] + (0.5 + fl) * low * (s0 - sl)
        first[1, at] = part[0, at] + (0.5 + f0) * ((low + time_step * f0) * sl - low * s0)
        for i in range(1, last):
            first[i + 1, at] = part[i, at]
        first[last + 1, at] = part[last, at] + (0.5 + f1) * high * (sh - s1)
        first[last + 2, at] = side[4, 1, at] + (0.5 + fh) * ((high + time_step * fh) * s1 - high * sh)
    for i in range(half):
        v, f, k, s, c = split(first.at[i + 1]), own(F, i), own(K, i), own(S, i), own(T, i)
        flow = across(split(ky.at[i]), split(kz.at[i]), v)
        for t in range(count):
            at = slice(t * TILE, (t + 1) * TILE)
            low = edge[0, at] if i == 0 else kx[i - 1, at]
            high = edge[1, at] if i == last else kx[i, at]
            rc = 0.5 + f[t]
            sink = time_step * k[t]
            rate = flow[t] + (low + time_step * f[t]) * first[i, at] + high * first[i + 2, at] - full[i, at] * v[t] - sink * jnp.tanh(v[t])
            value = 0.75 * s[t] + 0.25 * (v[t] + rc * rate)
            hot = jnp.tanh(value)
            second[i, at] = hot
            b = c[t] * rc
            total = back[i, at] - sink * (1.0 - hot * hot) * b
            if i == 0:
                total = total + low * (side[T, 0, at] * (0.5 + side[F, 0, at]) - b)
            if i == last:
                high_f = side[F, 1, at]
                total = total + ((high + time_step * high_f) * (side[T, 1, at] * (0.5 + high_f)) - high * b)
            total = total * (2.0 / 3.0)
            sa[i, at] = total
            b2[i, at] = total * rc
    for i in range(half):
        v, b, f, k = split(first.at[i + 1]), split(b2.at[i]), own(F, i), own(K, i)
        flow = across(split(ky.at[i]), split(kz.at[i]), b)
        for t in range(count):
            at = slice(t * TILE, (t + 1) * TILE)
            hot = jnp.tanh(v[t])
            total = sa[i, at] + flow[t] - full[i, at] * b[t] - time_step * k[t] * (1.0 - hot * hot) * b[t]
            if i > 0:
                total = total + kx[i - 1, at] * b2[i - 1, at]
            if i < last:
                total = total + (kx[i, at] + time_step * own(F, i + 1)[t]) * b2[i + 1, at]
            fa[i, at] = 0.25 * total
    outer, inner = core * last, (1 - core) * last
    for out, plane in ((off2, outer), (on2, inner)):
        out[0 : ny + TILE] = b2[plane]
        out[ny + TILE : 2 * ny + TILE] = fa[plane, 0:ny]


def finish(block, kx, ky, kz, first, second, sa, b2, fa, edge, full, side, ghost, off2, on2, keep, give, b3, fixed):
    core = lax.axis_index("gz")
    half, ny = block.shape[1], block.shape[2]
    wide = keep.shape[3]
    count = ny // TILE + 1
    last = half - 1
    own = lambda j, i: tiles(block.at[j, i], ghost.at[j, i])
    low_is_off = core == 0
    for t in range(count):
        at = slice(t * TILE, (t + 1) * TILE)
        off_b, on_b = off2[at], on2[at]
        low_b, high_b = jnp.where(low_is_off, off_b, on_b), jnp.where(low_is_off, on_b, off_b)
        low, high = edge[0, at], edge[1, at]
        fh = side[F, 1, at]
        f0, f1 = own(F, 0)[t], own(F, last)[t]
        fixed[0, at] = fa[0, at] + 0.25 * low * low_b
        for i in range(1, last):
            fixed[i, at] = fa[i, at]
        fixed[last, at] = fa[last, at] + 0.25 * (high + time_step * fh) * high_b
        for i in range(half):
            b3[i + 1, at] = fixed[i, at] * (0.5 + own(F, i)[t])
        if t < count - 1:
            at2 = slice(ny + (t + 1) * TILE, ny + (t + 2) * TILE)
            off_p, on_p = off2[at2], on2[at2]
            low_p, high_p = jnp.where(low_is_off, off_p, on_p), jnp.where(low_is_off, on_p, off_p)
            b3[0, at] = (low_p + 0.25 * (low + time_step * f0) * b2[0, at]) * (0.5 + side[F, 0, at])
            b3[half + 1, at] = (high_p + 0.25 * high * b2[last, at]) * (0.5 + fh)
    for i in range(half):
        b, f, k = split(b3.at[i + 1]), own(F, i), own(K, i)
        s, c = own(S, i), own(T, i)
        flow = across(split(ky.at[i]), split(kz.at[i]), b)
        for t in range(count - 1):
            at = slice(t * TILE, (t + 1) * TILE)
            low = edge[0, at] if i == 0 else kx[i - 1, at]
            if i == last:
                high = edge[1, at] + time_step * side[F, 1, at]
            else:
                high = kx[i, at] + time_step * own(F, i + 1)[t]
            hot = jnp.tanh(s[t])
            total = flow[t] + low * b3[i, at] + high * b3[i + 2, at] - full[i, at] * b[t]
            total = total - time_step * k[t] * (1.0 - hot * hot) * b[t]
            total = total + fixed[i, at] + 0.75 * sa[i, at] + c[t] * (1.0 / 3.0)
            term = (2.0 / 3.0) * second[i, at] * c[t] + 0.25 * jnp.tanh(first[i + 1, at]) * sa[i, at] + hot * fixed[i, at]
            term = -time_step * (0.5 + f[t]) * term
            for which, value in ((0, total), (1, term)):
                left, right = value[:, :wide], value[:, wide:]
                keep[which, i, at] = jnp.where(core == 0, left, right)
                give[which, i, at] = jnp.where(core == 0, right, left)


def assemble(labels, keep, got, grad_state, grad_sink):
    core = lax.axis_index("gz")
    half = keep.shape[1]
    mine, other = core * half, (1 - core) * half
    for start, source in ((mine, keep), (other, got)):
        for i in range(half):
            grad_state[start + i] = source[0, i]
            grad_sink[start + i] = jnp.where(touching(labels[start + i]), source[1, i], 0.0)


def on_device(state, conduct, sink, labels, cotangent):
    count, ny, nz = state.shape
    half, wide, rows = count // 2, 2 * nz, ny + TILE
    count_x, count_y = lax.axis_size("gx"), lax.axis_size("gy")
    assert lax.axis_size("gz") == 2 and count % 4 == 0 and ny % TILE == 0
    two = count_y == 2
    ahead = [(i, (i + 1) % count_x) for i in range(count_x)]
    behind = [(b, a) for a, b in ahead]
    cores = [(0, 1), (1, 0)]
    chips = [(2 * i + 1, (2 * i + 2) % (2 * count_x)) for i in range(count_x)]
    chips = chips + [(b, a) for a, b in chips]

    def swap_cores(x):
        return lax.ppermute(x, "gz", cores)

    def swap_chips(x):
        return lax.ppermute(x, ("gx", "gz"), chips)

    inputs = (state, conduct, sink, labels, cotangent)
    plane = (4, ny, nz)
    up, down, trade = call(pack_inputs, [plane, plane, (5, half, ny, nz)], *inputs)
    up = lax.ppermute(up, "gx", ahead)
    down = lax.ppermute(down, "gx", behind)
    traded = swap_cores(trade)
    rim = (5, half // 2, TILE, wide)
    block, *rims = call(
        functools.partial(gather_planes, two), [(5, half, ny, wide)] + [rim] * (1 if two else 2), *inputs, traded
    )
    if two:
        rims = [lax.ppermute(rims[0], "gy", [(0, 1), (1, 0)])]
    else:
        forward = [(i, (i + 1) % count_y) for i in range(count_y)]
        backward = [(b, a) for a, b in forward]
        rims = [lax.ppermute(rims[0], "gy", backward), lax.ppermute(rims[1], "gy", forward)]
    own = (half, rows, wide)
    ghost, kx, ky, kz, diag, part, back, off, on = call(
        functools.partial(prepare, two, count_y),
        [(5, half, TILE, wide), (half - 1, rows, wide), own, own, own, own, own, (rows + 4 * TILE, wide), (5, rows, wide)],
        block,
        *rims,
    )
    off, on = swap_chips(off), swap_cores(on)
    (passed,) = call(choose_half, [plane], up, down)
    passed = swap_cores(passed)
    ends = (rows + ny, wide)
    first, second, sa, b2, fa, edge, full, off2, on2, side = call(
        middle,
        [(half + 2, rows, wide), own, own, own, own, (2, rows, wide), own, ends, ends, (5, 2, rows, wide)],
        block, ghost, kx, ky, kz, diag, part, back, up, down, passed, off, on,
    )
    off2, on2 = swap_chips(off2), swap_cores(on2)
    quarter = (2, half, ny, nz)
    keep, give, _, _ = call(
        finish,
        [quarter, quarter, (half + 2, rows, wide), own],
        block, kx, ky, kz, first, second, sa, b2, fa, edge, full, side, ghost, off2, on2,
    )
    got = swap_cores(give)
    grad_state, grad_sink = call(assemble, [state.shape, state.shape], labels, keep, got, keep=False)
    return (grad_state, grad_sink)


def solution(mesh):
    block = P(("groups", "gx"), "gy", "gz")
    in_specs = (block, P("gx", "gy", "gz"), block, block, block)
    return jax.shard_map(on_device, mesh=mesh, in_specs=in_specs, out_specs=(block, block), check_vma=False)
```

```python
import functools

import jax
import jax.numpy as jnp
from jax import lax
from jax.experimental import pallas as pl
from jax.experimental.pallas import tpu as pltpu
from jax.sharding import PartitionSpec as P

VMEM = pltpu.VMEM
HBM = pltpu.HBM
time_step = 0.06
scale = 0.5 * time_step
HALO = 4
TILE = 8
PIECES = 2
S, C, T, F, K = range(5)


def call(kernel, outs, *ins, keep=True, given=VMEM, scratch=()):
    space = VMEM if keep else jax.ShapeDtypeStruct
    block = pl.BlockSpec(memory_space=VMEM if given is VMEM else pl.ANY)
    return pl.pallas_call(
        kernel,
        out_shape=[space(shape, jnp.float32) for shape in outs],
        in_specs=[block] * len(ins),
        out_specs=[pl.BlockSpec(memory_space=VMEM)] * len(outs),
        scratch_shapes=list(scratch),
        compiler_params=pltpu.CompilerParams(vmem_limit_bytes=8 * 1024 * 1024),
        cost_estimate=pl.CostEstimate(flops=1024, bytes_accessed=1024, transcendentals=0),
    )(*[pltpu.with_memory_space_constraint(x, given) for x in ins])


def half_fluid(labels):
    return jnp.where(labels <= 1, 0.5, 0.0)


def touching(labels):
    return jnp.logical_or(labels == 1, labels == 2)


def rows_of(value):
    return lax.broadcasted_iota(jnp.int32, value.shape, 0)


def lanes_of(value):
    return lax.broadcasted_iota(jnp.int32, value.shape, 1)


def down_rows(before, here):
    return pltpu.roll(jnp.where(rows_of(here) == TILE - 1, before, here), 1, 0)


def up_rows(here, after):
    return pltpu.roll(jnp.where(rows_of(here) == 0, after, here), TILE - 1, 0)


def down_lanes(here):
    return pltpu.roll(here, 1, 1)


def up_lanes(here):
    return pltpu.roll(here, here.shape[1] - 1, 1)


def at(t):
    return slice(t * TILE, (t + 1) * TILE)


class Tiles:
    def __init__(self, *places):
        self.places = places

    def __getitem__(self, t):
        ref, slot = self.places[t % len(self.places)]
        return ref[at(slot)]

    def __setitem__(self, t, value):
        ref, slot = self.places[t]
        ref[at(slot)] = value

    def __len__(self):
        return len(self.places)


def whole(ref):
    return Tiles(*[(ref, t) for t in range(ref.shape[0] // TILE)])


def with_ghost(main, ghost):
    return Tiles(*[(main, t) for t in range(main.shape[0] // TILE)], (ghost, 0))


def mid_and_rim(mid, rim):
    return Tiles((rim, 0), *[(mid, t) for t in range(mid.shape[0] // TILE)], (rim, 1), (rim, 2))


class Across:
    def __init__(self, ky, kz, v):
        self.ky, self.kz, self.v = ky, kz, v
        self.known = {}

    def product(self, t):
        t = t % len(self.v)
        if t not in self.known:
            self.known[t] = self.ky[t] * self.v[t]
        return self.known[t]

    def __getitem__(self, t):
        here, kz = self.v[t], self.kz[t]
        along_y = self.ky[t] * down_rows(self.v[t - 1], here) + up_rows(self.product(t), self.product(t + 1))
        return along_y + (kz * down_lanes(here) + up_lanes(kz * here))


class Made:
    def __init__(self, values):
        self.values = values

    def __getitem__(self, t):
        return self.values[t % len(self.values)]

    def __len__(self):
        return len(self.values)


def sides_along_z(c, here):
    lanes = lanes_of(c)
    left = here + jnp.where(lanes == 0, 0.0, down_lanes(c)) * scale
    right = here + jnp.where(lanes == lanes.shape[1] - 1, 0.0, up_lanes(c)) * scale
    return left, right


def load_all(pairs, sems):
    copies = [pltpu.make_async_copy(a, b, sems.at[i]) for i, (a, b) in enumerate(pairs)]
    for copy in copies:
        copy.start()
    return copies


def load_planes(inputs, start, out, kinds, drains, sems):
    state, conduct, sink, labels, cotangent = inputs
    part = pl.ds(start, out.shape[1])
    pairs = [(labels.at[part], kinds), (sink.at[part], drains), (state.at[part], out.at[S])]
    return load_all(pairs + [(conduct.at[part], out.at[C]), (cotangent.at[part], out.at[T])], sems)


def fill_planes(out, kinds, drains):
    for i in range(out.shape[1]):
        out[F, i] = half_fluid(kinds[i])
        out[K, i] = jnp.where(touching(kinds[i]), drains[i], 0.0)


def pack_inputs(state, conduct, sink, labels, cotangent, up, down, trade, kinds, drains, ends, sems, plane_sems):
    count = state.shape[0]
    pairs = []
    for which, (out, plane) in enumerate(((up, count - 1), (down, 0))):
        pairs += [(state.at[plane], out.at[S]), (conduct.at[plane], out.at[C]), (cotangent.at[plane], out.at[T])]
        pairs += [(labels.at[plane], ends.at[which])]
    copies = load_all(pairs, plane_sems)
    start = (1 - lax.axis_index("gz")) * (count - trade.shape[1])
    copies += load_planes((state, conduct, sink, labels, cotangent), start, trade, kinds, drains, sems)
    for copy in copies:
        copy.wait()
    up[F] = half_fluid(ends[0])
    down[F] = half_fluid(ends[1])
    fill_planes(trade, kinds, drains)


def own_planes(state, conduct, sink, labels, cotangent, mine, kinds, drains, sems):
    start = lax.axis_index("gz") * (state.shape[0] - mine.shape[1])
    for copy in load_planes((state, conduct, sink, labels, cotangent), start, mine, kinds, drains, sems):
        copy.wait()
    fill_planes(mine, kinds, drains)


def pack_rims(two, planes, outs):
    for k in range(0, len(planes), 2):
        even, odd = planes[k], planes[min(k + 1, len(planes) - 1)]
        ny = even.shape[0]
        low_even, high_even = even[0:TILE], even[ny - TILE : ny]
        low_odd, high_odd = odd[0:TILE], odd[ny - TILE : ny]
        upper = rows_of(low_even) < HALO
        low = jnp.where(upper, low_even, pltpu.roll(low_odd, HALO, 0))
        high = jnp.where(upper, pltpu.roll(high_even, HALO, 0), high_odd)
        per = outs[0].shape[0]
        piece, slot = k // 2 // per, k // 2 % per
        if two:
            outs[piece][slot] = jnp.where(lax.axis_index("gy") == 0, high, low)
        else:
            outs[2 * piece][slot] = low
            outs[2 * piece + 1][slot] = high


def unpack_rims(two, count_y, rims, planes):
    place = lax.axis_index("gy")
    for k in range(0, len(planes), 2):
        per = rims[0].shape[0]
        piece, slot = k // 2 // per, k // 2 % per
        above = jnp.where(place < count_y - 1, rims[piece if two else 2 * piece][slot], 0.0)
        below = jnp.where(place > 0, rims[piece if two else 2 * piece + 1][slot], 0.0)
        upper = rows_of(above) < HALO
        planes[k][...] = jnp.where(upper, above, pltpu.roll(below, HALO, 0))
        if k + 1 < len(planes):
            planes[k + 1][...] = jnp.where(upper, pltpu.roll(above, HALO, 0), below)


def gather_planes(mine, traded, block, near):
    core = lax.axis_index("gz")
    half, narrow = block.shape[1], mine.shape[3]
    own = pl.ds(pl.multiple_of(core * narrow, 128), narrow)
    other = pl.ds(pl.multiple_of((1 - core) * narrow, 128), narrow)
    start = 2 * core
    beside = (1 - core) * half + core
    beyond = (1 - core) * (half + 1)
    for j in range(5):
        for i in range(half):
            block[j, i, :, own] = mine[j, start + i]
            block[j, i, :, other] = traded[j, start + i]
        near[j, :, own] = mine[j, beside]
        near[j, :, other] = traded[j, beside]
        if j in (S, C):
            near[5 + j, :, own] = mine[j, beyond]
            near[5 + j, :, other] = traded[j, beyond]


def rim_planes(block, near):
    return [block.at[j, i] for j in range(5) for i in range(block.shape[1])] + [near.at[j] for j in range(7)]


def pack_along_y(two, block, near, *rims):
    pack_rims(two, rim_planes(block, near), rims)


class Lazy:
    def __init__(self, count, make):
        self.count, self.make, self.known = count, make, {}

    def __getitem__(self, t):
        t = t % self.count
        if t not in self.known:
            self.known[t] = self.make(t)
        return self.known[t]

    def __len__(self):
        return self.count


def prepare(todo, count_y, block, near, ghost, near_ghost, kx, ky_out, kz_out, diag, part, back, one):
    place = lax.axis_index("gy")
    core = lax.axis_index("gz")
    half, ny = block.shape[1], block.shape[2]
    count, last = ny // TILE + 1, half - 1

    def own(j, i):
        if ghost is None:
            return Tiles(*[(block.at[j, i], t) for t in range(count - 1)], (None, 0))
        return with_ghost(block.at[j, i], ghost.at[j, i])

    def next_to(j):
        if ghost is None:
            return Tiles(*[(near.at[j], t) for t in range(count - 1)], (None, 0))
        return with_ghost(near.at[j], near_ghost.at[j])

    def faces_along_y(c):
        def make(t):
            value = (c[t] + down_rows(c[t - 1], c[t])) * scale
            if t == 0:
                value = jnp.where(jnp.logical_and(rows_of(value) == 0, place == 0), 0.0, value)
            if t == count - 1:
                value = jnp.where(jnp.logical_and(rows_of(value) == 0, place == count_y - 1), 0.0, value)
            return value

        return Lazy(count, make)

    def own_weight(c, f, t):
        here = c[t] * scale
        left, right = sides_along_z(c[t], here)
        low, high = down_rows(c[t - 1], c[t]), up_rows(c[t], c[t + 1])
        return left, (2.0 * here + (low + high) * scale) + (left + right) + time_step * f[t]

    for i in range(half):
        s, c, a, f, k = (own(j, i) for j in (S, C, T, F, K))
        ky, kz = faces_along_y(c), {}
        for t in todo:
            left, weight = own_weight(c, f, t)
            kz[t] = jnp.where(lanes_of(left) == 0, 0.0, left)
            slot = at(todo.index(t))
            if i > 0:
                face = (c[t] + own(C, i - 1)[t]) * scale
                kx[i - 1, slot] = face
                weight = weight + face
            if i < last:
                weight = weight + (c[t] + own(C, i + 1)[t]) * scale
            diag[i, slot] = weight
            ky_out[i, slot] = ky[t]
            kz_out[i, slot] = kz[t]
        scaled = Lazy(count, lambda t, a=a, f=f: a[t] * (0.5 + f[t]))
        ahead = Across(ky, kz, s)
        behind = Across(ky, kz, scaled)
        for t in todo:
            slot = at(todo.index(t))
            d, b = diag[i, slot], scaled[t]
            go = ahead[t] - d * s[t] - time_step * k[t] * jnp.tanh(s[t])
            come = behind[t] - d * b
            if i > 0:
                go = go + (kx[i - 1, slot] + time_step * f[t]) * own(S, i - 1)[t]
                come = come + kx[i - 1, slot] * (own(T, i - 1)[t] * (0.5 + own(F, i - 1)[t]))
            if i < last:
                face, high_f = (c[t] + own(C, i + 1)[t]) * scale, own(F, i + 1)[t]
                go = go + face * own(S, i + 1)[t]
                come = come + (face + time_step * high_f) * (own(T, i + 1)[t] * (0.5 + high_f))
            part[i, slot] = s[t] + (0.5 + f[t]) * go
            back[i, slot] = a[t] + come
    s, c, f, k = (next_to(j) for j in (S, C, F, K))
    kz = {}
    for t in todo:
        left, _ = own_weight(c, f, t)
        kz[t] = jnp.where(lanes_of(left) == 0, 0.0, left)
    ahead = Across(faces_along_y(c), kz, s)
    is_low = core == 0
    for t in todo:
        _, weight = own_weight(c, f, t)
        c_own = jnp.where(is_low, own(C, last)[t], own(C, 0)[t])
        s_own = jnp.where(is_low, own(S, last)[t], own(S, 0)[t])
        face_own, face_far = (c[t] + c_own) * scale, (c[t] + next_to(5 + C)[t]) * scale
        wind = time_step * f[t]
        go = ahead[t] - (weight + face_own + face_far) * s[t] - time_step * k[t] * jnp.tanh(s[t])
        go = go + (face_own + jnp.where(is_low, wind, 0.0)) * s_own
        go = go + (face_far + jnp.where(is_low, 0.0, wind)) * next_to(5 + S)[t]
        one[at(todo.index(t))] = s[t] + (0.5 + f[t]) * go


def prepare_mid(count_y, block, near, *outs):
    prepare(list(range(1, block.shape[2] // TILE - 1)), count_y, block, near, None, None, *outs)


def prepare_rim(two, count_y, block, near, *refs):
    rims, (ghost, near_ghost, *outs) = refs[: PIECES * (1 if two else 2)], refs[PIECES * (1 if two else 2) :]
    count = block.shape[2] // TILE
    unpack_rims(two, count_y, rims, rim_planes(ghost, near_ghost))
    prepare([0, count - 1, count], count_y, block, near, ghost, near_ghost, *outs)


def pack_pair(place, a, b):
    upper = rows_of(a) < HALO
    turned_a, turned_b = pltpu.roll(a, HALO, 0), pltpu.roll(b, HALO, 0)
    return jnp.where(upper, jnp.where(place == 0, a, turned_a), jnp.where(place == 0, turned_b, b))


def unpack_pair(place, both):
    upper = rows_of(both) < HALO
    turned = pltpu.roll(both, HALO, 0)
    valid = upper == (place == 0)
    a = jnp.where(place == 0, both, turned)
    b = jnp.where(place == 0, turned, both)
    return jnp.where(valid, a, 0.0), jnp.where(valid, b, 0.0)


def pack_off(two, ghost, part_mid, part_rim, off):
    place = lax.axis_index("gy")
    outer = lax.axis_index("gz") * (ghost.shape[1] - 1)
    part = mid_and_rim(part_mid.at[outer], part_rim.at[outer])
    for t in range(len(part)):
        off[at(t)] = part[t]
    for j in range(0, 4, 2):
        a, b = ghost[j, outer], ghost[j + 1, outer]
        if two:
            off[at(len(part) + j // 2)] = pack_pair(place, a, b)
        else:
            off[at(len(part) + j)] = a
            off[at(len(part) + j + 1)] = b


def choose_half(up, down, *refs):
    for j in range(4):
        refs[j - 4][...] = jnp.where(lax.axis_index("gz") == 0, down[j], up[j])


def coefficients(refs):
    mids, rims = refs[:6], refs[7:13]
    return [lambda i, m=m, r=r: mid_and_rim(m.at[i], r.at[i]) for m, r in zip(mids, rims)]


def middle(two, block, ghost, near, near_ghost, up, down, *refs):
    passed, off, refs = refs[:4], refs[4], refs[5:]
    kx, ky, kz, diag, part, back = coefficients(refs[:14])
    side, edge, add, first, known, linear, adjoint, sa, b2, hot2, inward = refs[14:]
    core = lax.axis_index("gz")
    place = lax.axis_index("gy")
    half, ny, narrow = block.shape[1], block.shape[2], up.shape[2]
    count, last = ny // TILE, half - 1
    own = lambda j, i: with_ghost(block.at[j, i], ghost.at[j, i])
    outside, inside = core, 1 - core
    for j in range(4):
        side[j, outside, 0:ny, 0:narrow] = jnp.where(core == 0, up[j], passed[j][...])
        side[j, outside, 0:ny, narrow : 2 * narrow] = jnp.where(core == 0, passed[j][...], down[j])
        side[j, inside, 0:ny] = near[j]
        side[j, inside, ny : ny + TILE] = near_ghost[j]
    for j in range(0, 4, 2):
        if two:
            a, b = unpack_pair(place, off[at(count + 1 + j // 2)])
        else:
            a, b = off[at(count + 1 + j)], off[at(count + 2 + j)]
        side[j, outside, ny : ny + TILE] = a
        side[j + 1, outside, ny : ny + TILE] = b
    for which, i in ((0, 0), (1, last)):
        s, f, c = own(S, i), own(F, i), own(C, i)
        s_out, c_out, f_out = (whole(side.at[j, which]) for j in (S, C, F))
        for t in range(count + 1):
            face = (c[t] + c_out[t]) * scale
            edge[which, at(t)] = face
            v, beyond = s[t], s_out[t]
            if which == 0:
                inner_add = (face + time_step * f[t]) * beyond - face * v
                outer_add = face * (v - beyond)
            else:
                inner_add = face * (beyond - v)
                outer_add = (face + time_step * f_out[t]) * v - face * beyond
            first[i, at(t)] = part(i)[t] + (0.5 + f[t]) * inner_add
            add[which, at(t)] = (0.5 + f_out[t]) * outer_add
    for i in range(1, last):
        for t in range(count + 1):
            first[i, at(t)] = part(i)[t]
    for i in range(half):
        v, f, k, s, a = whole(first.at[i]), own(F, i), own(K, i), own(S, i), own(T, i)
        flow = Across(ky(i), kz(i), v)
        for t in range(count + 1):
            rc = 0.5 + f[t]
            sink = time_step * k[t]
            hot1 = jnp.tanh(v[t])
            full = diag(i)[t]
            if i == 0:
                full = full + edge[0, at(t)]
            if i == last:
                full = full + edge[1, at(t)]
            adjoint[i, at(t)] = full + sink * (1.0 - hot1 * hot1)
            rate = flow[t] - full * v[t] - sink * hot1
            if i > 0:
                rate = rate + (kx(i - 1)[t] + time_step * f[t]) * first[i - 1, at(t)]
            if i < last:
                rate = rate + kx(i)[t] * first[i + 1, at(t)]
            value = 0.75 * s[t] + 0.25 * (v[t] + rc * rate)
            b = a[t] * rc
            total = back(i)[t]
            if i == 0:
                total = total + edge[0, at(t)] * (side[T, 0, at(t)] * (0.5 + side[F, 0, at(t)]) - b)
            if i == last:
                high, high_f = edge[1, at(t)], side[F, 1, at(t)]
                total = total + ((high + time_step * high_f) * (side[T, 1, at(t)] * (0.5 + high_f)) - high * b)
            if i == 0 or i == last:
                which = 0 if i == 0 else 1
                known[which, at(t)] = value
                linear[which, at(t)] = total
            else:
                hot = jnp.tanh(value)
                hot2[i, at(t)] = hot
                total = (2.0 / 3.0) * (total - sink * (1.0 - hot * hot) * b)
                sa[i, at(t)] = total
                b2[i, at(t)] = total * rc
    for t in range(count + 1):
        inward[0, at(t)] = (kx(0)[t] + time_step * own(F, 1)[t]) * b2[1, at(t)]
        inward[1, at(t)] = kx(last - 1)[t] * b2[last - 1, at(t)]


def outward(block, ghost, one_mid, one_rim, side, edge, add, known, linear, adjoint, inward, off, *refs):
    ky_mid, kz_mid, ky_rim, kz_rim, hot2, sa, b2, fa, off2, on2 = refs
    core = lax.axis_index("gz")
    half, ny = block.shape[1], block.shape[2]
    count, last = ny // TILE, half - 1
    own = lambda j, i: with_ghost(block.at[j, i], ghost.at[j, i])
    for which, i in ((0, 0), (1, last)):
        f, k, a = own(F, i), own(K, i), own(T, i)
        mine = core == which
        for t in range(count + 1):
            one = jnp.where(mine, off[at(t)] + add[which, at(t)], mid_and_rim(one_mid, one_rim)[t])
            face = edge[which, at(t)]
            if which == 0:
                face = face + time_step * f[t]
            rc = 0.5 + f[t]
            hot = jnp.tanh(known[which, at(t)] + 0.25 * rc * face * one)
            total = (2.0 / 3.0) * (linear[which, at(t)] - time_step * k[t] * (1.0 - hot * hot) * (a[t] * rc))
            hot2[which, at(t)] = hot
            sa[which, at(t)] = total
            b2[which, at(t)] = total * rc
        b = whole(b2.at[which])
        flow = Across(mid_and_rim(ky_mid.at[i], ky_rim.at[i]), mid_and_rim(kz_mid.at[i], kz_rim.at[i]), b)
        for t in range(count + 1):
            total = sa[which, at(t)] + flow[t] - adjoint[i, at(t)] * b[t] + inward[which, at(t)]
            fa[which, at(t)] = 0.25 * total
    for out, which in ((off2, core), (on2, 1 - core)):
        out[0 : ny + TILE] = b2[which]
        out[ny + TILE : 2 * ny + TILE] = fa[which, 0:ny]


def inner(block, ghost, edge, side, first, adjoint, sa_in, b2_in, hot2_in, sa_out, b2_out, hot2_out, fa_out, *refs):
    kx, ky, kz, diag, _, _ = coefficients(refs[:14])
    value, term, adjoint0, hot0, fa, b3 = refs[14:]
    half, ny = block.shape[1], block.shape[2]
    count, last = ny // TILE, half - 1
    own = lambda j, i: with_ghost(block.at[j, i], ghost.at[j, i])
    pick = lambda i, inside, outside: inside.at[i] if 0 < i < last else outside.at[0 if i == 0 else 1]
    sa = lambda i: whole(pick(i, sa_in, sa_out))
    b2 = lambda i: whole(pick(i, b2_in, b2_out))
    hot2 = lambda i: whole(pick(i, hot2_in, hot2_out))
    for i in range(half):
        f = own(F, i)
        flow = Across(ky(i), kz(i), b2(i))
        for t in range(count + 1):
            if 0 < i < last:
                total = sa(i)[t] + flow[t] - adjoint[i, at(t)] * b2(i)[t]
                total = total + kx(i - 1)[t] * b2(i - 1)[t] + (kx(i)[t] + time_step * own(F, i + 1)[t]) * b2(i + 1)[t]
                total = 0.25 * total
            else:
                total = fa_out[0 if i == 0 else 1, at(t)]
            fa[i, at(t)] = total
            b3[i, at(t)] = total * (0.5 + f[t])
    for i in range(half):
        s, f, k, a = own(S, i), own(F, i), own(K, i), own(T, i)
        b = whole(b3.at[i])
        flow = Across(ky(i), kz(i), b)
        for t in range(count):
            hot = jnp.tanh(s[t])
            full = diag(i)[t]
            if i == 0:
                full = full + edge[0, at(t)]
            if i == last:
                full = full + edge[1, at(t)]
            full = full + time_step * k[t] * (1.0 - hot * hot)
            total = flow[t] - full * b[t] + fa[i, at(t)] + 0.75 * sa(i)[t] + a[t] * (1.0 / 3.0)
            if i > 0:
                total = total + kx(i - 1)[t] * b3[i - 1, at(t)]
            if i < last:
                total = total + (kx(i)[t] + time_step * own(F, i + 1)[t]) * b3[i + 1, at(t)]
            value[i, at(t)] = total
            first_hot = jnp.tanh(first[i, at(t)])
            total = (2.0 / 3.0) * hot2(i)[t] * a[t] + 0.25 * first_hot * sa(i)[t] + hot * fa[i, at(t)]
            term[i, at(t)] = -time_step * (0.5 + f[t]) * total
            if i == 0 or i == last:
                which = 0 if i == 0 else 1
                adjoint0[which, at(t)] = full
                hot0[which, at(t)] = -time_step * (0.5 + f[t]) * hot


def finish(block, ghost, edge, side, b2_out, value, term, adjoint0, hot0, off2, on2, *refs):
    kx_mid, ky_mid, kz_mid, kx_rim, ky_rim, kz_rim, keep, give, late = refs
    core = lax.axis_index("gz")
    half, ny, narrow = block.shape[1], block.shape[2], keep.shape[3]
    count, last = ny // TILE, half - 1
    own = lambda j, i: with_ghost(block.at[j, i], ghost.at[j, i])
    both = lambda mid, rim: lambda i: mid_and_rim(mid.at[i], rim.at[i])
    kx, ky, kz = both(kx_mid, kx_rim), both(ky_mid, ky_rim), both(kz_mid, kz_rim)
    gains = {}
    for which, i in ((0, 0), (1, last)):
        mine = core == which
        f = own(F, i)
        for t in range(count + 1):
            face = edge[which, at(t)]
            if which == 1:
                face = face + time_step * side[F, 1, at(t)]
            gain = 0.25 * face * jnp.where(mine, off2[at(t)], on2[at(t)])
            late[which, at(t)] = gain * (0.5 + f[t])
            gains[which, t] = gain

    def write(i, t, total, term):
        for which, whole_row in ((0, total), (1, term)):
            left, right = whole_row[:, :narrow], whole_row[:, narrow:]
            keep[which, i, at(t)] = jnp.where(core == 0, left, right)
            give[which, i, at(t)] = jnp.where(core == 0, right, left)

    for i in range(half):
        for which in range(2):
            if i == which * last:
                flow = Across(ky(i), kz(i), whole(late.at[which]))
        for t in range(count):
            total, sink = value[i, at(t)], term[i, at(t)]
            for which in range(2):
                if i == which * last:
                    mine = core == which
                    slot = slice(ny + (t + 1) * TILE, ny + (t + 2) * TILE)
                    beyond = jnp.where(mine, off2[slot], on2[slot])
                    face, f_out = edge[which, at(t)], side[F, which, at(t)]
                    into, out_of = face, face
                    if which == 0:
                        out_of = out_of + time_step * own(F, 0)[t]
                    else:
                        into = into + time_step * f_out
                    beyond = (beyond + 0.25 * out_of * b2_out[which, at(t)]) * (0.5 + f_out)
                    total = total + gains[which, t] + flow[t] - adjoint0[which, at(t)] * late[which, at(t)] + into * beyond
                    sink = sink + hot0[which, at(t)] * gains[which, t]
            if i == 1:
                total = total + kx(0)[t] * late[0, at(t)]
            if i == last - 1:
                total = total + (kx(last - 1)[t] + time_step * own(F, last)[t]) * late[1, at(t)]
            write(i, t, total, sink)


def assemble(labels, keep, got, grad_state, grad_sink):
    core = lax.axis_index("gz")
    half = keep.shape[1]
    mine, other = core * half, (1 - core) * half
    for start, source in ((mine, keep), (other, got)):
        for i in range(half):
            grad_state[start + i] = source[0, i]
            grad_sink[start + i] = jnp.where(touching(labels[start + i]), source[1, i], 0.0)


def on_device(state, conduct, sink, labels, cotangent):
    count, ny, nz = state.shape
    half, wide, rows = count // 2, 2 * nz, ny + TILE
    count_x, count_y = lax.axis_size("gx"), lax.axis_size("gy")
    assert lax.axis_size("gz") == 2 and half >= 3 and ny % TILE == 0 and ny >= 3 * TILE
    two = count_y == 2
    ahead = [(i, (i + 1) % count_x) for i in range(count_x)]
    behind = [(b, a) for a, b in ahead]
    chips = [(2 * i + 1, (2 * i + 2) % (2 * count_x)) for i in range(count_x)]
    chips = chips + [(b, a) for a, b in chips]

    def swap_cores(x):
        return lax.ppermute(x, "gz", [(0, 1), (1, 0)])

    def swap_chips(x):
        return lax.ppermute(x, ("gx", "gz"), chips)

    def along_y(rims):
        forward = [(i, (i + 1) % count_y) for i in range(count_y)]
        backward = [(b, a) for a, b in forward]
        routes = [forward] if two else [backward, forward]
        return [lax.ppermute(rim, "gy", routes[i % len(routes)]) for i, rim in enumerate(rims)]

    ways = 1 if two else 2
    inputs = (state, conduct, sink, labels, cotangent)
    plane, span = (4, ny, nz), (5, half + 2, ny, nz)
    kinds = pltpu.VMEM((half + 2, ny, nz), jnp.int32)
    drains = pltpu.VMEM((half + 2, ny, nz), jnp.float32)
    sems = lambda many: pltpu.SemaphoreType.DMA((many,))
    up, down, trade = call(
        pack_inputs, [plane, plane, span], *inputs, given=HBM,
        scratch=[kinds, drains, pltpu.VMEM((2, ny, nz), jnp.int32), sems(5), sems(8)],
    )
    up = lax.ppermute(up, "gx", ahead)
    down = lax.ppermute(down, "gx", behind)
    traded = swap_cores(trade)
    (mine,) = call(own_planes, [span], *inputs, given=HBM, scratch=[kinds, drains, sems(5)])
    block, near = call(gather_planes, [(5, half, ny, wide), (7, ny, wide)], mine, traded)
    per = -(-((5 * half + 8) // 2) // PIECES)
    rims = call(functools.partial(pack_along_y, two), [(per, TILE, wide)] * (ways * PIECES), block, near)
    rims = along_y(rims)
    split = lambda r: [(half - 1, r, wide)] + [(half, r, wide)] * 5 + [(r, wide)]
    mids = call(functools.partial(prepare_mid, count_y), split(ny - 2 * TILE), block, near)
    ghost, near_ghost, *edges = call(
        functools.partial(prepare_rim, two, count_y),
        [(5, half, TILE, wide), (7, TILE, wide)] + split(3 * TILE), block, near, *rims,
    )
    (off,) = call(functools.partial(pack_off, two), [(rows + (2 if two else 4) * TILE, wide)], ghost, mids[4], edges[4])
    passed = call(choose_half, [(ny, nz)] * 4, up, down, *rims)
    passed = [swap_cores(x) for x in passed]
    off = swap_chips(off)
    own, outer = (half, rows, wide), (2, rows, wide)
    side, edge, add, first, known, linear, adjoint, sa, b2, hot2, inward = call(
        functools.partial(middle, two),
        [(4, 2, rows, wide), outer, outer, own, outer, outer, own, own, own, own, outer],
        block, ghost, near, near_ghost, up, down, *passed, off, *mids, *edges,
    )
    ends = (rows + ny, wide)
    hot2_out, sa_out, b2_out, fa_out, off2, on2 = call(
        outward, [outer] * 4 + [ends] * 2,
        block, ghost, mids[6], edges[6], side, edge, add, known, linear, adjoint, inward, off,
        mids[1], mids[2], edges[1], edges[2],
    )
    off2, on2 = swap_chips(off2), swap_cores(on2)
    main = lambda planes: (planes, ny, wide)
    value, term, adjoint0, hot0, _, _ = call(
        inner, [main(half), main(half), main(2), main(2), own, own],
        block, ghost, edge, side, first, adjoint, sa, b2, hot2, sa_out, b2_out, hot2_out, fa_out, *mids, *edges,
    )
    quarter = (2, half, ny, nz)
    keep, give, _ = call(
        finish, [quarter, quarter, outer],
        block, ghost, edge, side, b2_out, value, term, adjoint0, hot0, off2, on2, *mids[:3], *edges[:3],
    )
    got = swap_cores(give)
    grad_state, grad_sink = call(assemble, [state.shape, state.shape], labels, keep, got, keep=False)
    return (grad_state, grad_sink)


def solution(mesh):
    block = P(("groups", "gx"), "gy", "gz")
    in_specs = (block, P("gx", "gy", "gz"), block, block, block)
    return jax.shard_map(on_device, mesh=mesh, in_specs=in_specs, out_specs=(block, block), check_vma=False)
```

```python
import functools

import jax
import jax.numpy as jnp
from jax import lax
from jax.experimental import pallas as pl
from jax.experimental.pallas import tpu as pltpu
from jax.sharding import PartitionSpec as P

VMEM = pltpu.VMEM
HBM = pltpu.HBM
time_step = 0.06
scale = 0.5 * time_step
HALO = 4
TILE = 8
RETURNS = 3
S, C, T, F, K = range(5)


def call(kernel, outs, *ins, keep=True, given=VMEM, scratch=()):
    space = VMEM if keep else jax.ShapeDtypeStruct
    block = pl.BlockSpec(memory_space=VMEM if given is VMEM else pl.ANY)
    return pl.pallas_call(
        kernel,
        out_shape=[space(shape, jnp.float32) for shape in outs],
        in_specs=[block] * len(ins),
        out_specs=[pl.BlockSpec(memory_space=VMEM)] * len(outs),
        scratch_shapes=list(scratch),
        compiler_params=pltpu.CompilerParams(vmem_limit_bytes=8 * 1024 * 1024),
        cost_estimate=pl.CostEstimate(flops=1024, bytes_accessed=1024, transcendentals=0),
    )(*[pltpu.with_memory_space_constraint(x, given) for x in ins])


def half_fluid(labels):
    return jnp.where(labels <= 1, 0.5, 0.0)


def touching(labels):
    return jnp.logical_or(labels == 1, labels == 2)


def rows_of(value):
    return lax.broadcasted_iota(jnp.int32, value.shape, 0)


def lanes_of(value):
    return lax.broadcasted_iota(jnp.int32, value.shape, 1)


def down_rows(before, here):
    return pltpu.roll(jnp.where(rows_of(here) == TILE - 1, before, here), 1, 0)


def up_rows(here, after):
    return pltpu.roll(jnp.where(rows_of(here) == 0, after, here), TILE - 1, 0)


def down_lanes(here):
    return pltpu.roll(here, 1, 1)


def up_lanes(here):
    return pltpu.roll(here, here.shape[1] - 1, 1)


def at(t):
    return slice(t * TILE, (t + 1) * TILE)


class Tiles:
    def __init__(self, *places):
        self.places = places

    def __getitem__(self, t):
        ref, slot = self.places[t % len(self.places)]
        return ref[at(slot)]

    def __setitem__(self, t, value):
        ref, slot = self.places[t]
        ref[at(slot)] = value

    def __len__(self):
        return len(self.places)


def whole(ref):
    return Tiles(*[(ref, t) for t in range(ref.shape[0] // TILE)])


def with_ghost(main, ghost):
    return Tiles(*[(main, t) for t in range(main.shape[0] // TILE)], (ghost, 0))


def mid_and_rim(mid, rim):
    return Tiles((rim, 0), *[(mid, t) for t in range(mid.shape[0] // TILE)], (rim, 1), (rim, 2))


class Across:
    def __init__(self, ky, kz, v):
        self.ky, self.kz, self.v = ky, kz, v
        self.known = {}

    def product(self, t):
        t = t % len(self.v)
        if t not in self.known:
            self.known[t] = self.ky[t] * self.v[t]
        return self.known[t]

    def __getitem__(self, t):
        here, kz = self.v[t], self.kz[t]
        along_y = self.ky[t] * down_rows(self.v[t - 1], here) + up_rows(self.product(t), self.product(t + 1))
        return along_y + (kz * down_lanes(here) + up_lanes(kz * here))


class Made:
    def __init__(self, values):
        self.values = values

    def __getitem__(self, t):
        return self.values[t % len(self.values)]

    def __len__(self):
        return len(self.values)


def sides_along_z(c, here):
    lanes = lanes_of(c)
    left = here + jnp.where(lanes == 0, 0.0, down_lanes(c)) * scale
    right = here + jnp.where(lanes == lanes.shape[1] - 1, 0.0, up_lanes(c)) * scale
    return left, right


def load_all(pairs, sems):
    copies = [pltpu.make_async_copy(a, b, sems.at[i]) for i, (a, b) in enumerate(pairs)]
    for copy in copies:
        copy.start()
    return copies


def load_planes(inputs, start, out, kinds, drains, sems):
    state, conduct, sink, labels, cotangent = inputs
    part = pl.ds(start, out.shape[1])
    pairs = [(labels.at[part], kinds), (sink.at[part], drains), (state.at[part], out.at[S])]
    return load_all(pairs + [(conduct.at[part], out.at[C]), (cotangent.at[part], out.at[T])], sems)


def fill_planes(out, kinds, drains):
    for i in range(out.shape[1]):
        out[F, i] = half_fluid(kinds[i])
        out[K, i] = jnp.where(touching(kinds[i]), drains[i], 0.0)


def pack_inputs(state, conduct, sink, labels, cotangent, up, down, trade, kinds, drains, ends, sems, plane_sems):
    count = state.shape[0]
    pairs = []
    for which, (out, plane) in enumerate(((up, count - 1), (down, 0))):
        pairs += [(state.at[plane], out.at[S]), (conduct.at[plane], out.at[C]), (cotangent.at[plane], out.at[T])]
        pairs += [(labels.at[plane], ends.at[which])]
    copies = load_all(pairs, plane_sems)
    start = (1 - lax.axis_index("gz")) * (count - trade.shape[1])
    copies += load_planes((state, conduct, sink, labels, cotangent), start, trade, kinds, drains, sems)
    for copy in copies:
        copy.wait()
    up[F] = half_fluid(ends[0])
    down[F] = half_fluid(ends[1])
    fill_planes(trade, kinds, drains)


def own_planes(state, conduct, sink, labels, cotangent, mine, kinds, drains, sems):
    start = lax.axis_index("gz") * (state.shape[0] - mine.shape[1])
    for copy in load_planes((state, conduct, sink, labels, cotangent), start, mine, kinds, drains, sems):
        copy.wait()
    fill_planes(mine, kinds, drains)


def pack_rims(two, planes, outs):
    for k in range(0, len(planes), 2):
        even, odd = planes[k], planes[min(k + 1, len(planes) - 1)]
        ny = even.shape[0]
        low_even, high_even = even[0:TILE], even[ny - TILE : ny]
        low_odd, high_odd = odd[0:TILE], odd[ny - TILE : ny]
        upper = rows_of(low_even) < HALO
        low = jnp.where(upper, low_even, pltpu.roll(low_odd, HALO, 0))
        high = jnp.where(upper, pltpu.roll(high_even, HALO, 0), high_odd)
        if two:
            outs[0][k // 2] = jnp.where(lax.axis_index("gy") == 0, high, low)
        else:
            outs[0][k // 2] = low
            outs[1][k // 2] = high


def unpack_rims(two, count_y, rims, planes):
    place = lax.axis_index("gy")
    for k in range(0, len(planes), 2):
        above = jnp.where(place < count_y - 1, rims[0][k // 2], 0.0)
        below = jnp.where(place > 0, rims[0 if two else 1][k // 2], 0.0)
        upper = rows_of(above) < HALO
        planes[k][...] = jnp.where(upper, above, pltpu.roll(below, HALO, 0))
        if k + 1 < len(planes):
            planes[k + 1][...] = jnp.where(upper, pltpu.roll(above, HALO, 0), below)


def gather_planes(mine, traded, block, near):
    core = lax.axis_index("gz")
    half, narrow = block.shape[1], mine.shape[3]
    own = pl.ds(pl.multiple_of(core * narrow, 128), narrow)
    other = pl.ds(pl.multiple_of((1 - core) * narrow, 128), narrow)
    start = 2 * core
    beside = (1 - core) * half + core
    beyond = (1 - core) * (half + 1)
    for j in range(5):
        for i in range(half):
            block[j, i, :, own] = mine[j, start + i]
            block[j, i, :, other] = traded[j, start + i]
        near[j, :, own] = mine[j, beside]
        near[j, :, other] = traded[j, beside]
        if j in (S, C):
            near[5 + j, :, own] = mine[j, beyond]
            near[5 + j, :, other] = traded[j, beyond]


def rim_planes(block, near):
    half = block.shape[1]
    core = lax.axis_index("gz")
    inward = lambda i: core * (half - 1) + i * (1 - 2 * core)
    early = [block.at[j, inward(0)] for j in range(5)] + [block.at[j, inward(1)] for j in (S, C)]
    late = [block.at[j, inward(1)] for j in (T, F, K)] + [block.at[j, inward(i)] for i in range(2, half) for j in range(5)]
    return early, late + [near.at[j] for j in range(7)]


def pack_along_y(two, block, near, *rims):
    early, late = rim_planes(block, near)
    ways = 1 if two else 2
    pack_rims(two, early, rims[:ways])
    pack_rims(two, late, rims[ways:])


class Lazy:
    def __init__(self, count, make):
        self.count, self.make, self.known = count, make, {}

    def __getitem__(self, t):
        t = t % self.count
        if t not in self.known:
            self.known[t] = self.make(t)
        return self.known[t]

    def __len__(self):
        return self.count


def prepare(todo, count_y, block, near, ghost, near_ghost, kx, ky_out, kz_out, diag, part, back, one):
    place = lax.axis_index("gy")
    core = lax.axis_index("gz")
    half, ny = block.shape[1], block.shape[2]
    count, last = ny // TILE + 1, half - 1

    def own(j, i):
        if ghost is None:
            return Tiles(*[(block.at[j, i], t) for t in range(count - 1)], (None, 0))
        return with_ghost(block.at[j, i], ghost.at[j, i])

    def next_to(j):
        if ghost is None:
            return Tiles(*[(near.at[j], t) for t in range(count - 1)], (None, 0))
        return with_ghost(near.at[j], near_ghost.at[j])

    def faces_along_y(c):
        def make(t):
            value = (c[t] + down_rows(c[t - 1], c[t])) * scale
            if t == 0:
                value = jnp.where(jnp.logical_and(rows_of(value) == 0, place == 0), 0.0, value)
            if t == count - 1:
                value = jnp.where(jnp.logical_and(rows_of(value) == 0, place == count_y - 1), 0.0, value)
            return value

        return Lazy(count, make)

    def own_weight(c, f, t):
        here = c[t] * scale
        left, right = sides_along_z(c[t], here)
        low, high = down_rows(c[t - 1], c[t]), up_rows(c[t], c[t + 1])
        return left, (2.0 * here + (low + high) * scale) + (left + right) + time_step * f[t]

    for i in range(half):
        s, c, a, f, k = (own(j, i) for j in (S, C, T, F, K))
        ky, kz = faces_along_y(c), {}
        for t in todo:
            left, weight = own_weight(c, f, t)
            kz[t] = jnp.where(lanes_of(left) == 0, 0.0, left)
            slot = at(todo.index(t))
            if i > 0:
                face = (c[t] + own(C, i - 1)[t]) * scale
                kx[i - 1, slot] = face
                weight = weight + face
            if i < last:
                weight = weight + (c[t] + own(C, i + 1)[t]) * scale
            diag[i, slot] = weight
            ky_out[i, slot] = ky[t]
            kz_out[i, slot] = kz[t]
        scaled = Lazy(count, lambda t, a=a, f=f: a[t] * (0.5 + f[t]))
        ahead = Across(ky, kz, s)
        behind = Across(ky, kz, scaled)
        for t in todo:
            slot = at(todo.index(t))
            d, b = diag[i, slot], scaled[t]
            go = ahead[t] - d * s[t] - time_step * k[t] * jnp.tanh(s[t])
            come = behind[t] - d * b
            if i > 0:
                go = go + (kx[i - 1, slot] + time_step * f[t]) * own(S, i - 1)[t]
                come = come + kx[i - 1, slot] * (own(T, i - 1)[t] * (0.5 + own(F, i - 1)[t]))
            if i < last:
                face, high_f = (c[t] + own(C, i + 1)[t]) * scale, own(F, i + 1)[t]
                go = go + face * own(S, i + 1)[t]
                come = come + (face + time_step * high_f) * (own(T, i + 1)[t] * (0.5 + high_f))
            part[i, slot] = s[t] + (0.5 + f[t]) * go
            back[i, slot] = a[t] + come
    s, c, f, k = (next_to(j) for j in (S, C, F, K))
    kz = {}
    for t in todo:
        left, _ = own_weight(c, f, t)
        kz[t] = jnp.where(lanes_of(left) == 0, 0.0, left)
    ahead = Across(faces_along_y(c), kz, s)
    is_low = core == 0
    for t in todo:
        _, weight = own_weight(c, f, t)
        c_own = jnp.where(is_low, own(C, last)[t], own(C, 0)[t])
        s_own = jnp.where(is_low, own(S, last)[t], own(S, 0)[t])
        face_own, face_far = (c[t] + c_own) * scale, (c[t] + next_to(5 + C)[t]) * scale
        wind = time_step * f[t]
        go = ahead[t] - (weight + face_own + face_far) * s[t] - time_step * k[t] * jnp.tanh(s[t])
        go = go + (face_own + jnp.where(is_low, wind, 0.0)) * s_own
        go = go + (face_far + jnp.where(is_low, 0.0, wind)) * next_to(5 + S)[t]
        one[at(todo.index(t))] = s[t] + (0.5 + f[t]) * go


def prepare_mid(count_y, block, near, *outs):
    prepare(list(range(1, block.shape[2] // TILE - 1)), count_y, block, near, None, None, *outs)


def prepare_rim(two, count_y, block, near, *refs):
    ways = 1 if two else 2
    rims, (ghost, near_ghost, *outs) = refs[: 2 * ways], refs[2 * ways :]
    count = block.shape[2] // TILE
    early, late = rim_planes(ghost, near_ghost)
    unpack_rims(two, count_y, rims[:ways], early)
    unpack_rims(two, count_y, rims[ways:], late)
    prepare([0, count - 1, count], count_y, block, near, ghost, near_ghost, *outs)


def pack_pair(place, a, b):
    upper = rows_of(a) < HALO
    turned_a, turned_b = pltpu.roll(a, HALO, 0), pltpu.roll(b, HALO, 0)
    return jnp.where(upper, jnp.where(place == 0, a, turned_a), jnp.where(place == 0, turned_b, b))


def unpack_pair(place, both):
    upper = rows_of(both) < HALO
    turned = pltpu.roll(both, HALO, 0)
    valid = upper == (place == 0)
    a = jnp.where(place == 0, both, turned)
    b = jnp.where(place == 0, turned, both)
    return jnp.where(valid, a, 0.0), jnp.where(valid, b, 0.0)


def pack_off(two, count_y, block, part_mid, *refs):
    ways = 1 if two else 2
    rims, (off, ghost) = refs[:ways], refs[ways:]
    place = lax.axis_index("gy")
    core = lax.axis_index("gz")
    last = block.shape[1] - 1
    outer = core * last
    inside = outer + 1 - 2 * core
    unpack_rims(two, count_y, rims, [ghost.at[j] for j in range(7)])
    s, c, f, k = (with_ghost(block.at[j, outer], ghost.at[j]) for j in (S, C, F, K))
    s_in, c_in = (with_ghost(block.at[j, inside], ghost.at[5 + j]) for j in (S, C))
    count = len(s)

    def face_along_y(t):
        value = (c[t] + down_rows(c[t - 1], c[t])) * scale
        if t == 0:
            value = jnp.where(jnp.logical_and(rows_of(value) == 0, place == 0), 0.0, value)
        if t == count - 1:
            value = jnp.where(jnp.logical_and(rows_of(value) == 0, place == count_y - 1), 0.0, value)
        return value

    todo, kz, weight = (0, count - 2, count - 1), {}, {}
    for t in todo:
        here = c[t] * scale
        left, right = sides_along_z(c[t], here)
        kz[t] = jnp.where(lanes_of(left) == 0, 0.0, left)
        low, high = down_rows(c[t - 1], c[t]), up_rows(c[t], c[t + 1])
        weight[t] = (2.0 * here + (low + high) * scale) + (left + right) + time_step * f[t]
    flow = Across(Lazy(count, face_along_y), kz, s)
    for t in range(count):
        if t in todo:
            face = (c[t] + c_in[t]) * scale
            go = flow[t] - (weight[t] + face) * s[t] - time_step * k[t] * jnp.tanh(s[t])
            go = go + (face + jnp.where(core == 0, 0.0, time_step) * f[t]) * s_in[t]
            off[at(t)] = s[t] + (0.5 + f[t]) * go
        else:
            off[at(t)] = part_mid[outer, at(t - 1)]
    for j in range(0, 4, 2):
        if two:
            off[at(count + j // 2)] = pack_pair(place, ghost[j], ghost[j + 1])
        else:
            off[at(count + j)] = ghost[j]
            off[at(count + j + 1)] = ghost[j + 1]


def choose_half(up, down, *refs):
    for j in range(4):
        refs[j - 4][...] = jnp.where(lax.axis_index("gz") == 0, down[j], up[j])


def coefficients(refs):
    mids, rims = refs[:6], refs[7:13]
    return [lambda i, m=m, r=r: mid_and_rim(m.at[i], r.at[i]) for m, r in zip(mids, rims)]


def middle(two, block, ghost, near, near_ghost, up, down, *refs):
    passed, off, refs = refs[:4], refs[4], refs[5:]
    kx, ky, kz, diag, part, back = coefficients(refs[:14])
    side, edge, add, first, known, linear, adjoint, sa, b2, hot2, inward = refs[14:]
    core = lax.axis_index("gz")
    place = lax.axis_index("gy")
    half, ny, narrow = block.shape[1], block.shape[2], up.shape[2]
    count, last = ny // TILE, half - 1
    own = lambda j, i: with_ghost(block.at[j, i], ghost.at[j, i])
    outside, inside = core, 1 - core
    for j in range(4):
        side[j, outside, 0:ny, 0:narrow] = jnp.where(core == 0, up[j], passed[j][...])
        side[j, outside, 0:ny, narrow : 2 * narrow] = jnp.where(core == 0, passed[j][...], down[j])
        side[j, inside, 0:ny] = near[j]
        side[j, inside, ny : ny + TILE] = near_ghost[j]
    for j in range(0, 4, 2):
        if two:
            a, b = unpack_pair(place, off[at(count + 1 + j // 2)])
        else:
            a, b = off[at(count + 1 + j)], off[at(count + 2 + j)]
        side[j, outside, ny : ny + TILE] = a
        side[j + 1, outside, ny : ny + TILE] = b
    for which, i in ((0, 0), (1, last)):
        s, f, c = own(S, i), own(F, i), own(C, i)
        s_out, c_out, f_out = (whole(side.at[j, which]) for j in (S, C, F))
        for t in range(count + 1):
            face = (c[t] + c_out[t]) * scale
            edge[which, at(t)] = face
            v, beyond = s[t], s_out[t]
            if which == 0:
                inner_add = (face + time_step * f[t]) * beyond - face * v
                outer_add = face * (v - beyond)
            else:
                inner_add = face * (beyond - v)
                outer_add = (face + time_step * f_out[t]) * v - face * beyond
            first[i, at(t)] = part(i)[t] + (0.5 + f[t]) * inner_add
            add[which, at(t)] = (0.5 + f_out[t]) * outer_add
    for i in range(1, last):
        for t in range(count + 1):
            first[i, at(t)] = part(i)[t]
    for i in range(half):
        v, f, k, s, a = whole(first.at[i]), own(F, i), own(K, i), own(S, i), own(T, i)
        flow = Across(ky(i), kz(i), v)
        for t in range(count + 1):
            rc = 0.5 + f[t]
            sink = time_step * k[t]
            hot1 = jnp.tanh(v[t])
            full = diag(i)[t]
            if i == 0:
                full = full + edge[0, at(t)]
            if i == last:
                full = full + edge[1, at(t)]
            adjoint[i, at(t)] = full + sink * (1.0 - hot1 * hot1)
            rate = flow[t] - full * v[t] - sink * hot1
            if i > 0:
                rate = rate + (kx(i - 1)[t] + time_step * f[t]) * first[i - 1, at(t)]
            if i < last:
                rate = rate + kx(i)[t] * first[i + 1, at(t)]
            value = 0.75 * s[t] + 0.25 * (v[t] + rc * rate)
            b = a[t] * rc
            total = back(i)[t]
            if i == 0:
                total = total + edge[0, at(t)] * (side[T, 0, at(t)] * (0.5 + side[F, 0, at(t)]) - b)
            if i == last:
                high, high_f = edge[1, at(t)], side[F, 1, at(t)]
                total = total + ((high + time_step * high_f) * (side[T, 1, at(t)] * (0.5 + high_f)) - high * b)
            if i == 0 or i == last:
                which = 0 if i == 0 else 1
                known[which, at(t)] = value
                linear[which, at(t)] = total
            else:
                hot = jnp.tanh(value)
                hot2[i, at(t)] = hot
                total = (2.0 / 3.0) * (total - sink * (1.0 - hot * hot) * b)
                sa[i, at(t)] = total
                b2[i, at(t)] = total * rc
    for t in range(count + 1):
        inward[0, at(t)] = (kx(0)[t] + time_step * own(F, 1)[t]) * b2[1, at(t)]
        inward[1, at(t)] = kx(last - 1)[t] * b2[last - 1, at(t)]


def outward(block, ghost, one_mid, one_rim, edge, add, known, linear, off, hot2, sa, b2, off_b, on_b):
    core = lax.axis_index("gz")
    half, ny = block.shape[1], block.shape[2]
    count, last = ny // TILE, half - 1
    own = lambda j, i: with_ghost(block.at[j, i], ghost.at[j, i])
    for which, i in ((0, 0), (1, last)):
        f, k, a = own(F, i), own(K, i), own(T, i)
        mine = core == which
        for t in range(count + 1):
            one = jnp.where(mine, off[at(t)] + add[which, at(t)], mid_and_rim(one_mid, one_rim)[t])
            face = edge[which, at(t)]
            if which == 0:
                face = face + time_step * f[t]
            rc = 0.5 + f[t]
            hot = jnp.tanh(known[which, at(t)] + 0.25 * rc * face * one)
            total = (2.0 / 3.0) * (linear[which, at(t)] - time_step * k[t] * (1.0 - hot * hot) * (a[t] * rc))
            hot2[which, at(t)] = hot
            sa[which, at(t)] = total
            b2[which, at(t)] = total * rc
    off_b[...] = b2[core]
    on_b[...] = b2[1 - core]


def outward_first(ky_mid, kz_mid, ky_rim, kz_rim, adjoint, inward, sa, b2, fa, off_p, on_p):
    core = lax.axis_index("gz")
    half, ny = adjoint.shape[0], off_p.shape[0]
    for which, i in ((0, 0), (1, half - 1)):
        b = whole(b2.at[which])
        flow = Across(mid_and_rim(ky_mid.at[i], ky_rim.at[i]), mid_and_rim(kz_mid.at[i], kz_rim.at[i]), b)
        for t in range(len(b)):
            total = sa[which, at(t)] + flow[t] - adjoint[i, at(t)] * b[t] + inward[which, at(t)]
            fa[which, at(t)] = 0.25 * total
    off_p[...] = fa[core, 0:ny]
    on_p[...] = fa[1 - core, 0:ny]


def inner(block, ghost, edge, side, first, adjoint, sa_in, b2_in, hot2_in, sa_out, b2_out, hot2_out, fa_out, *refs):
    kx, ky, kz, diag, _, _ = coefficients(refs[:14])
    value, term, adjoint0, hot0, fa, b3 = refs[14:]
    half, ny = block.shape[1], block.shape[2]
    count, last = ny // TILE, half - 1
    own = lambda j, i: with_ghost(block.at[j, i], ghost.at[j, i])
    pick = lambda i, inside, outside: inside.at[i] if 0 < i < last else outside.at[0 if i == 0 else 1]
    sa = lambda i: whole(pick(i, sa_in, sa_out))
    b2 = lambda i: whole(pick(i, b2_in, b2_out))
    hot2 = lambda i: whole(pick(i, hot2_in, hot2_out))
    for i in range(half):
        f = own(F, i)
        flow = Across(ky(i), kz(i), b2(i))
        for t in range(count + 1):
            if 0 < i < last:
                total = sa(i)[t] + flow[t] - adjoint[i, at(t)] * b2(i)[t]
                total = total + kx(i - 1)[t] * b2(i - 1)[t] + (kx(i)[t] + time_step * own(F, i + 1)[t]) * b2(i + 1)[t]
                total = 0.25 * total
            else:
                total = fa_out[0 if i == 0 else 1, at(t)]
            fa[i, at(t)] = total
            b3[i, at(t)] = total * (0.5 + f[t])
    for i in range(half):
        s, f, k, a = own(S, i), own(F, i), own(K, i), own(T, i)
        b = whole(b3.at[i])
        flow = Across(ky(i), kz(i), b)
        for t in range(count):
            hot = jnp.tanh(s[t])
            full = diag(i)[t]
            if i == 0:
                full = full + edge[0, at(t)]
            if i == last:
                full = full + edge[1, at(t)]
            full = full + time_step * k[t] * (1.0 - hot * hot)
            total = flow[t] - full * b[t] + fa[i, at(t)] + 0.75 * sa(i)[t] + a[t] * (1.0 / 3.0)
            if i > 0:
                total = total + kx(i - 1)[t] * b3[i - 1, at(t)]
            if i < last:
                total = total + (kx(i)[t] + time_step * own(F, i + 1)[t]) * b3[i + 1, at(t)]
            value[i, at(t)] = total
            first_hot = jnp.tanh(first[i, at(t)])
            total = (2.0 / 3.0) * hot2(i)[t] * a[t] + 0.25 * first_hot * sa(i)[t] + hot * fa[i, at(t)]
            term[i, at(t)] = -time_step * (0.5 + f[t]) * total
            if i == 0 or i == last:
                which = 0 if i == 0 else 1
                adjoint0[which, at(t)] = full
                hot0[which, at(t)] = -time_step * (0.5 + f[t]) * hot


class Pieces:
    def __init__(self, refs):
        self.refs, self.size = refs, refs[0].shape[0]

    def __getitem__(self, place):
        return self.refs[place // self.size][place % self.size]

    def __setitem__(self, place, value):
        self.refs[place[0] // self.size][place[0] % self.size, place[1]] = value


def halves(core, value):
    narrow = value.shape[1] // 2
    left, right = value[:, :narrow], value[:, narrow:]
    return jnp.where(core == 0, left, right), jnp.where(core == 0, right, left)


def finish(block, ghost, edge, side, b2_out, value, term, adjoint0, hot0, off_b, on_b, *refs):
    kx_mid, ky_mid, kz_mid, kx_rim, ky_rim, kz_rim, keep, *pieces, rest, late = refs
    give = Pieces(pieces)
    core = lax.axis_index("gz")
    half, ny = block.shape[1], block.shape[2]
    count, last = ny // TILE, half - 1
    own = lambda j, i: with_ghost(block.at[j, i], ghost.at[j, i])
    both = lambda mid, rim: lambda i: mid_and_rim(mid.at[i], rim.at[i])
    kx, ky, kz = both(kx_mid, kx_rim), both(ky_mid, ky_rim), both(kz_mid, kz_rim)
    gains = {}
    for which, i in ((0, 0), (1, last)):
        mine = core == which
        f = own(F, i)
        for t in range(count + 1):
            face = edge[which, at(t)]
            if which == 1:
                face = face + time_step * side[F, 1, at(t)]
            gain = 0.25 * face * jnp.where(mine, off_b[at(t)], on_b[at(t)])
            late[which, at(t)] = gain * (0.5 + f[t])
            gains[which, t] = gain
    for which, i in ((0, 0), (1, last)):
        flow = Across(ky(i), kz(i), whole(late.at[which]))
        for t in range(count):
            face, f_out = edge[which, at(t)], side[F, which, at(t)]
            into, out_of = face, face
            if which == 0:
                out_of = out_of + time_step * own(F, 0)[t]
            else:
                into = into + time_step * f_out
            total = value[i, at(t)] + gains[which, t] + flow[t] - adjoint0[which, at(t)] * late[which, at(t)]
            rest[which, at(t)] = total + into * (0.25 * out_of * b2_out[which, at(t)]) * (0.5 + f_out)
            keep[i, at(t)], give[i, at(t)] = halves(core, term[i, at(t)] + hot0[which, at(t)] * gains[which, t])
    for i in range(1, last):
        for t in range(count):
            total = value[i, at(t)]
            if i == 1:
                total = total + kx(0)[t] * late[0, at(t)]
            if i == last - 1:
                total = total + (kx(last - 1)[t] + time_step * own(F, last)[t]) * late[1, at(t)]
            keep[half + i - 1, at(t)], give[half + i - 1, at(t)] = halves(core, total)
            keep[i, at(t)], give[i, at(t)] = halves(core, term[i, at(t)])


def finish_outer(edge, side, rest, off_p, on_p, keep, give):
    core = lax.axis_index("gz")
    for which in range(2):
        mine = core == which
        for t in range(rest.shape[1] // TILE):
            face, f_out = edge[which, at(t)], side[F, which, at(t)]
            if which == 1:
                face = face + time_step * f_out
            total = rest[which, at(t)] + face * (0.5 + f_out) * jnp.where(mine, off_p[at(t)], on_p[at(t)])
            keep[which, at(t)], give[which, at(t)] = halves(core, total)


def assemble(labels, keep, keep_outer, got_outer, *refs):
    *pieces, grad_state, grad_sink = refs
    got = Pieces(pieces)
    core = lax.axis_index("gz")
    half = grad_state.shape[0] // 2
    for start, source, outer in ((core * half, keep, keep_outer), ((1 - core) * half, got, got_outer)):
        grad_state[start] = outer[0]
        grad_state[start + half - 1] = outer[1]
        for i in range(1, half - 1):
            grad_state[start + i] = source[half + i - 1]
        for i in range(half):
            grad_sink[start + i] = jnp.where(touching(labels[start + i]), source[i], 0.0)


def on_device(state, conduct, sink, labels, cotangent):
    count, ny, nz = state.shape
    half, wide, rows = count // 2, 2 * nz, ny + TILE
    count_x, count_y = lax.axis_size("gx"), lax.axis_size("gy")
    assert lax.axis_size("gz") == 2 and half >= 3 and ny % TILE == 0 and ny >= 3 * TILE
    two = count_y == 2
    ahead = [(i, (i + 1) % count_x) for i in range(count_x)]
    behind = [(b, a) for a, b in ahead]
    chips = [(2 * i + 1, (2 * i + 2) % (2 * count_x)) for i in range(count_x)]
    chips = chips + [(b, a) for a, b in chips]

    def swap_cores(x):
        return lax.ppermute(x, "gz", [(0, 1), (1, 0)])

    def swap_chips(x):
        return lax.ppermute(x, ("gx", "gz"), chips)

    def along_y(rims):
        forward = [(i, (i + 1) % count_y) for i in range(count_y)]
        backward = [(b, a) for a, b in forward]
        routes = [forward] if two else [backward, forward]
        return [lax.ppermute(rim, "gy", routes[i % len(routes)]) for i, rim in enumerate(rims)]

    ways = 1 if two else 2
    inputs = (state, conduct, sink, labels, cotangent)
    plane, span = (4, ny, nz), (5, half + 2, ny, nz)
    kinds = pltpu.VMEM((half + 2, ny, nz), jnp.int32)
    drains = pltpu.VMEM((half + 2, ny, nz), jnp.float32)
    sems = lambda many: pltpu.SemaphoreType.DMA((many,))
    up, down, trade = call(
        pack_inputs, [plane, plane, span], *inputs, given=HBM,
        scratch=[kinds, drains, pltpu.VMEM((2, ny, nz), jnp.int32), sems(5), sems(8)],
    )
    up = lax.ppermute(up, "gx", ahead)
    down = lax.ppermute(down, "gx", behind)
    traded = swap_cores(trade)
    (mine,) = call(own_planes, [span], *inputs, given=HBM, scratch=[kinds, drains, sems(5)])
    block, near = call(gather_planes, [(5, half, ny, wide), (7, ny, wide)], mine, traded)
    sizes = [4, (5 * half + 1) // 2]
    rims = call(functools.partial(pack_along_y, two), [(n, TILE, wide) for n in sizes for _ in range(ways)], block, near)
    rims = along_y(rims)
    split = lambda r: [(half - 1, r, wide)] + [(half, r, wide)] * 5 + [(r, wide)]
    mids = call(functools.partial(prepare_mid, count_y), split(ny - 2 * TILE), block, near)
    ghost, near_ghost, *edges = call(
        functools.partial(prepare_rim, two, count_y),
        [(5, half, TILE, wide), (7, TILE, wide)] + split(3 * TILE), block, near, *rims,
    )
    off, _ = call(
        functools.partial(pack_off, two, count_y), [(rows + (2 if two else 4) * TILE, wide), (7, TILE, wide)],
        block, mids[4], *rims[:ways],
    )
    passed = call(choose_half, [(ny, nz)] * 4, up, down, *rims)
    passed = [swap_cores(x) for x in passed]
    off = swap_chips(off)
    own, outer = (half, rows, wide), (2, rows, wide)
    side, edge, add, first, known, linear, adjoint, sa, b2, hot2, inward = call(
        functools.partial(middle, two),
        [(4, 2, rows, wide), outer, outer, own, outer, outer, own, own, own, own, outer],
        block, ghost, near, near_ghost, up, down, *passed, off, *mids, *edges,
    )
    ends, mains = (rows, wide), (ny, wide)
    hot2_out, sa_out, b2_out, off_b, on_b = call(
        outward, [outer] * 3 + [ends] * 2, block, ghost, mids[6], edges[6], edge, add, known, linear, off
    )
    off_b, on_b = swap_chips(off_b), swap_cores(on_b)
    fa_out, off_p, on_p = call(
        outward_first, [outer] + [mains] * 2, mids[1], mids[2], edges[1], edges[2], adjoint, inward, sa_out, b2_out
    )
    off_p, on_p = swap_chips(off_p), swap_cores(on_p)
    main = lambda planes: (planes, ny, wide)
    value, term, adjoint0, hot0, _, _ = call(
        inner, [main(half), main(half), main(2), main(2), own, own],
        block, ghost, edge, side, first, adjoint, sa, b2, hot2, sa_out, b2_out, hot2_out, fa_out, *mids, *edges,
    )
    most = (2 * half - 2, ny, nz)
    pieces = RETURNS if most[0] % RETURNS == 0 else 1
    keep, *give, rest, _ = call(
        finish, [most] + [(most[0] // pieces, ny, nz)] * pieces + [main(2), outer],
        block, ghost, edge, side, b2_out, value, term, adjoint0, hot0, off_b, on_b, *mids[:3], *edges[:3],
    )
    got = [swap_cores(x) for x in give]
    keep_outer, give_outer = call(finish_outer, [(2, ny, nz)] * 2, edge, side, rest, off_p, on_p)
    got_outer = swap_cores(give_outer)
    grad_state, grad_sink = call(
        assemble, [state.shape, state.shape], labels, keep, keep_outer, got_outer, *got, keep=False
    )
    return (grad_state, grad_sink)


def solution(mesh):
    block = P(("groups", "gx"), "gy", "gz")
    in_specs = (block, P("gx", "gy", "gz"), block, block, block)
    return jax.shard_map(on_device, mesh=mesh, in_specs=in_specs, out_specs=(block, block), check_vma=False)
```

```python
import functools

import jax
import jax.numpy as jnp
from jax import lax
from jax.experimental import pallas as pl
from jax.experimental.pallas import tpu as pltpu
from jax.sharding import PartitionSpec as P

VMEM = pltpu.VMEM
HBM = pltpu.HBM
time_step = 0.06
scale = 0.5 * time_step
HALO = 4
TILE = 8
RETURNS = 3
FLOPS = 100000000000
S, C, T, F, K = range(5)


def call(kernel, outs, *ins, keep=True, given=VMEM, scratch=(), flops=1024):
    space = VMEM if keep else jax.ShapeDtypeStruct
    block = pl.BlockSpec(memory_space=VMEM if given is VMEM else pl.ANY)
    return pl.pallas_call(
        kernel,
        out_shape=[space(shape, jnp.float32) for shape in outs],
        in_specs=[block] * len(ins),
        out_specs=[pl.BlockSpec(memory_space=VMEM)] * len(outs),
        scratch_shapes=list(scratch),
        compiler_params=pltpu.CompilerParams(vmem_limit_bytes=8 * 1024 * 1024),
        cost_estimate=pl.CostEstimate(flops=flops, bytes_accessed=1024, transcendentals=0),
    )(*[pltpu.with_memory_space_constraint(x, given) for x in ins])


def half_fluid(labels):
    return jnp.where(labels <= 1, 0.5, 0.0)


def touching(labels):
    return jnp.logical_or(labels == 1, labels == 2)


def rows_of(value):
    return lax.broadcasted_iota(jnp.int32, value.shape, 0)


def lanes_of(value):
    return lax.broadcasted_iota(jnp.int32, value.shape, 1)


def down_rows(before, here):
    return pltpu.roll(jnp.where(rows_of(here) == TILE - 1, before, here), 1, 0)


def up_rows(here, after):
    return pltpu.roll(jnp.where(rows_of(here) == 0, after, here), TILE - 1, 0)


def down_lanes(here):
    return pltpu.roll(here, 1, 1)


def up_lanes(here):
    return pltpu.roll(here, here.shape[1] - 1, 1)


def at(t):
    return slice(t * TILE, (t + 1) * TILE)


class Tiles:
    def __init__(self, *places):
        self.places = places

    def __getitem__(self, t):
        ref, slot = self.places[t % len(self.places)]
        return ref[at(slot)]

    def __setitem__(self, t, value):
        ref, slot = self.places[t]
        ref[at(slot)] = value

    def __len__(self):
        return len(self.places)


def whole(ref):
    return Tiles(*[(ref, t) for t in range(ref.shape[0] // TILE)])


def with_ghost(main, ghost):
    return Tiles(*[(main, t) for t in range(main.shape[0] // TILE)], (ghost, 0))


def mid_and_rim(mid, rim):
    return Tiles((rim, 0), *[(mid, t) for t in range(mid.shape[0] // TILE)], (rim, 1), (rim, 2))


class Across:
    def __init__(self, ky, kz, v):
        self.ky, self.kz, self.v = ky, kz, v
        self.known = {}

    def product(self, t):
        t = t % len(self.v)
        if t not in self.known:
            self.known[t] = self.ky[t] * self.v[t]
        return self.known[t]

    def __getitem__(self, t):
        here, kz = self.v[t], self.kz[t]
        along_y = self.ky[t] * down_rows(self.v[t - 1], here) + up_rows(self.product(t), self.product(t + 1))
        return along_y + (kz * down_lanes(here) + up_lanes(kz * here))


class Made:
    def __init__(self, values):
        self.values = values

    def __getitem__(self, t):
        return self.values[t % len(self.values)]

    def __len__(self):
        return len(self.values)


def sides_along_z(c, here):
    lanes = lanes_of(c)
    left = here + jnp.where(lanes == 0, 0.0, down_lanes(c)) * scale
    right = here + jnp.where(lanes == lanes.shape[1] - 1, 0.0, up_lanes(c)) * scale
    return left, right


def load_all(pairs, sems):
    copies = [pltpu.make_async_copy(a, b, sems.at[i]) for i, (a, b) in enumerate(pairs)]
    for copy in copies:
        copy.start()
    return copies


def load_planes(inputs, start, out, kinds, drains, sems):
    state, conduct, sink, labels, cotangent = inputs
    part = pl.ds(start, out.shape[1])
    pairs = [(labels.at[part], kinds), (sink.at[part], drains), (state.at[part], out.at[S])]
    return load_all(pairs + [(conduct.at[part], out.at[C]), (cotangent.at[part], out.at[T])], sems)


def fill_planes(out, kinds, drains):
    for i in range(out.shape[1]):
        out[F, i] = half_fluid(kinds[i])
        out[K, i] = jnp.where(touching(kinds[i]), drains[i], 0.0)


def pack_inputs(state, conduct, sink, labels, cotangent, up, down, trade, kinds, drains, ends, sems, plane_sems):
    count = state.shape[0]
    pairs = []
    for which, (out, plane) in enumerate(((up, count - 1), (down, 0))):
        pairs += [(state.at[plane], out.at[S]), (conduct.at[plane], out.at[C]), (cotangent.at[plane], out.at[T])]
        pairs += [(labels.at[plane], ends.at[which])]
    copies = load_all(pairs, plane_sems)
    start = (1 - lax.axis_index("gz")) * (count - trade.shape[1])
    copies += load_planes((state, conduct, sink, labels, cotangent), start, trade, kinds, drains, sems)
    for copy in copies:
        copy.wait()
    up[F] = half_fluid(ends[0])
    down[F] = half_fluid(ends[1])
    fill_planes(trade, kinds, drains)


def own_planes(state, conduct, sink, labels, cotangent, mine, kinds, drains, sems):
    start = lax.axis_index("gz") * (state.shape[0] - mine.shape[1])
    for copy in load_planes((state, conduct, sink, labels, cotangent), start, mine, kinds, drains, sems):
        copy.wait()
    fill_planes(mine, kinds, drains)


def pack_rims(two, planes, outs):
    for k in range(0, len(planes), 2):
        even, odd = planes[k], planes[min(k + 1, len(planes) - 1)]
        ny = even.shape[0]
        low_even, high_even = even[0:TILE], even[ny - TILE : ny]
        low_odd, high_odd = odd[0:TILE], odd[ny - TILE : ny]
        upper = rows_of(low_even) < HALO
        low = jnp.where(upper, low_even, pltpu.roll(low_odd, HALO, 0))
        high = jnp.where(upper, pltpu.roll(high_even, HALO, 0), high_odd)
        if two:
            outs[0][k // 2] = jnp.where(lax.axis_index("gy") == 0, high, low)
        else:
            outs[0][k // 2] = low
            outs[1][k // 2] = high


def unpack_rims(two, count_y, rims, planes):
    place = lax.axis_index("gy")
    for k in range(0, len(planes), 2):
        above = jnp.where(place < count_y - 1, rims[0][k // 2], 0.0)
        below = jnp.where(place > 0, rims[0 if two else 1][k // 2], 0.0)
        upper = rows_of(above) < HALO
        planes[k][...] = jnp.where(upper, above, pltpu.roll(below, HALO, 0))
        if k + 1 < len(planes):
            planes[k + 1][...] = jnp.where(upper, pltpu.roll(above, HALO, 0), below)


def gather_planes(mine, traded, block, near):
    core = lax.axis_index("gz")
    half, narrow = block.shape[1], mine.shape[3]
    own = pl.ds(pl.multiple_of(core * narrow, 128), narrow)
    other = pl.ds(pl.multiple_of((1 - core) * narrow, 128), narrow)
    start = 2 * core
    beside = (1 - core) * half + core
    beyond = (1 - core) * (half + 1)
    for j in range(5):
        for i in range(half):
            block[j, i, :, own] = mine[j, start + i]
            block[j, i, :, other] = traded[j, start + i]
        near[j, :, own] = mine[j, beside]
        near[j, :, other] = traded[j, beside]
        if j in (S, C):
            near[5 + j, :, own] = mine[j, beyond]
            near[5 + j, :, other] = traded[j, beyond]


def rim_planes(block, near):
    half = block.shape[1]
    core = lax.axis_index("gz")
    inward = lambda i: core * (half - 1) + i * (1 - 2 * core)
    early = [block.at[j, inward(0)] for j in range(5)] + [block.at[j, inward(1)] for j in (S, C)]
    late = [block.at[j, inward(1)] for j in (T, F, K)] + [block.at[j, inward(i)] for i in range(2, half) for j in range(5)]
    return early, late + [near.at[j] for j in range(7)]


def pack_along_y(two, block, near, *rims):
    early, late = rim_planes(block, near)
    ways = 1 if two else 2
    pack_rims(two, early, rims[:ways])
    pack_rims(two, late, rims[ways:])


class Lazy:
    def __init__(self, count, make):
        self.count, self.make, self.known = count, make, {}

    def __getitem__(self, t):
        t = t % self.count
        if t not in self.known:
            self.known[t] = self.make(t)
        return self.known[t]

    def __len__(self):
        return self.count


def prepare(todo, count_y, block, near, ghost, near_ghost, kx, ky_out, kz_out, diag, part, back, one):
    place = lax.axis_index("gy")
    core = lax.axis_index("gz")
    half, ny = block.shape[1], block.shape[2]
    count, last = ny // TILE + 1, half - 1

    def own(j, i):
        if ghost is None:
            return Tiles(*[(block.at[j, i], t) for t in range(count - 1)], (None, 0))
        return with_ghost(block.at[j, i], ghost.at[j, i])

    def next_to(j):
        if ghost is None:
            return Tiles(*[(near.at[j], t) for t in range(count - 1)], (None, 0))
        return with_ghost(near.at[j], near_ghost.at[j])

    def faces_along_y(c):
        def make(t):
            value = (c[t] + down_rows(c[t - 1], c[t])) * scale
            if t == 0:
                value = jnp.where(jnp.logical_and(rows_of(value) == 0, place == 0), 0.0, value)
            if t == count - 1:
                value = jnp.where(jnp.logical_and(rows_of(value) == 0, place == count_y - 1), 0.0, value)
            return value

        return Lazy(count, make)

    def own_weight(c, f, t):
        here = c[t] * scale
        left, right = sides_along_z(c[t], here)
        low, high = down_rows(c[t - 1], c[t]), up_rows(c[t], c[t + 1])
        return left, (2.0 * here + (low + high) * scale) + (left + right) + time_step * f[t]

    for i in range(half):
        s, c, a, f, k = (own(j, i) for j in (S, C, T, F, K))
        ky, kz = faces_along_y(c), {}
        for t in todo:
            left, weight = own_weight(c, f, t)
            kz[t] = jnp.where(lanes_of(left) == 0, 0.0, left)
            slot = at(todo.index(t))
            if i > 0:
                face = (c[t] + own(C, i - 1)[t]) * scale
                kx[i - 1, slot] = face
                weight = weight + face
            if i < last:
                weight = weight + (c[t] + own(C, i + 1)[t]) * scale
            diag[i, slot] = weight
            ky_out[i, slot] = ky[t]
            kz_out[i, slot] = kz[t]
        scaled = Lazy(count, lambda t, a=a, f=f: a[t] * (0.5 + f[t]))
        ahead = Across(ky, kz, s)
        behind = Across(ky, kz, scaled)
        for t in todo:
            slot = at(todo.index(t))
            d, b = diag[i, slot], scaled[t]
            go = ahead[t] - d * s[t] - time_step * k[t] * jnp.tanh(s[t])
            come = behind[t] - d * b
            if i > 0:
                go = go + (kx[i - 1, slot] + time_step * f[t]) * own(S, i - 1)[t]
                come = come + kx[i - 1, slot] * (own(T, i - 1)[t] * (0.5 + own(F, i - 1)[t]))
            if i < last:
                face, high_f = (c[t] + own(C, i + 1)[t]) * scale, own(F, i + 1)[t]
                go = go + face * own(S, i + 1)[t]
                come = come + (face + time_step * high_f) * (own(T, i + 1)[t] * (0.5 + high_f))
            part[i, slot] = s[t] + (0.5 + f[t]) * go
            back[i, slot] = a[t] + come
    s, c, f, k = (next_to(j) for j in (S, C, F, K))
    kz = {}
    for t in todo:
        left, _ = own_weight(c, f, t)
        kz[t] = jnp.where(lanes_of(left) == 0, 0.0, left)
    ahead = Across(faces_along_y(c), kz, s)
    is_low = core == 0
    for t in todo:
        _, weight = own_weight(c, f, t)
        c_own = jnp.where(is_low, own(C, last)[t], own(C, 0)[t])
        s_own = jnp.where(is_low, own(S, last)[t], own(S, 0)[t])
        face_own, face_far = (c[t] + c_own) * scale, (c[t] + next_to(5 + C)[t]) * scale
        wind = time_step * f[t]
        go = ahead[t] - (weight + face_own + face_far) * s[t] - time_step * k[t] * jnp.tanh(s[t])
        go = go + (face_own + jnp.where(is_low, wind, 0.0)) * s_own
        go = go + (face_far + jnp.where(is_low, 0.0, wind)) * next_to(5 + S)[t]
        one[at(todo.index(t))] = s[t] + (0.5 + f[t]) * go


def prepare_mid(count_y, block, near, *outs):
    prepare(list(range(1, block.shape[2] // TILE - 1)), count_y, block, near, None, None, *outs)


def prepare_rim(two, count_y, block, near, *refs):
    ways = 1 if two else 2
    rims, (ghost, near_ghost, *outs) = refs[: 2 * ways], refs[2 * ways :]
    count = block.shape[2] // TILE
    early, late = rim_planes(ghost, near_ghost)
    unpack_rims(two, count_y, rims[:ways], early)
    unpack_rims(two, count_y, rims[ways:], late)
    prepare([0, count - 1, count], count_y, block, near, ghost, near_ghost, *outs)


def pack_pair(place, a, b):
    upper = rows_of(a) < HALO
    turned_a, turned_b = pltpu.roll(a, HALO, 0), pltpu.roll(b, HALO, 0)
    return jnp.where(upper, jnp.where(place == 0, a, turned_a), jnp.where(place == 0, turned_b, b))


def unpack_pair(place, both):
    upper = rows_of(both) < HALO
    turned = pltpu.roll(both, HALO, 0)
    valid = upper == (place == 0)
    a = jnp.where(place == 0, both, turned)
    b = jnp.where(place == 0, turned, both)
    return jnp.where(valid, a, 0.0), jnp.where(valid, b, 0.0)


def pack_off(two, count_y, block, part_mid, *refs):
    ways = 1 if two else 2
    rims, (off, ghost) = refs[:ways], refs[ways:]
    place = lax.axis_index("gy")
    core = lax.axis_index("gz")
    last = block.shape[1] - 1
    outer = core * last
    inside = outer + 1 - 2 * core
    unpack_rims(two, count_y, rims, [ghost.at[j] for j in range(7)])
    s, c, f, k = (with_ghost(block.at[j, outer], ghost.at[j]) for j in (S, C, F, K))
    s_in, c_in = (with_ghost(block.at[j, inside], ghost.at[5 + j]) for j in (S, C))
    count = len(s)

    def face_along_y(t):
        value = (c[t] + down_rows(c[t - 1], c[t])) * scale
        if t == 0:
            value = jnp.where(jnp.logical_and(rows_of(value) == 0, place == 0), 0.0, value)
        if t == count - 1:
            value = jnp.where(jnp.logical_and(rows_of(value) == 0, place == count_y - 1), 0.0, value)
        return value

    todo, kz, weight = (0, count - 2, count - 1), {}, {}
    for t in todo:
        here = c[t] * scale
        left, right = sides_along_z(c[t], here)
        kz[t] = jnp.where(lanes_of(left) == 0, 0.0, left)
        low, high = down_rows(c[t - 1], c[t]), up_rows(c[t], c[t + 1])
        weight[t] = (2.0 * here + (low + high) * scale) + (left + right) + time_step * f[t]
    flow = Across(Lazy(count, face_along_y), kz, s)
    for t in range(count):
        if t in todo:
            face = (c[t] + c_in[t]) * scale
            go = flow[t] - (weight[t] + face) * s[t] - time_step * k[t] * jnp.tanh(s[t])
            go = go + (face + jnp.where(core == 0, 0.0, time_step) * f[t]) * s_in[t]
            off[at(t)] = s[t] + (0.5 + f[t]) * go
        else:
            off[at(t)] = part_mid[outer, at(t - 1)]
    for j in range(0, 4, 2):
        if two:
            off[at(count + j // 2)] = pack_pair(place, ghost[j], ghost[j + 1])
        else:
            off[at(count + j)] = ghost[j]
            off[at(count + j + 1)] = ghost[j + 1]


def choose_half(up, down, *refs):
    for j in range(4):
        refs[j - 4][...] = jnp.where(lax.axis_index("gz") == 0, down[j], up[j])


def coefficients(refs):
    mids, rims = refs[:6], refs[7:13]
    return [lambda i, m=m, r=r: mid_and_rim(m.at[i], r.at[i]) for m, r in zip(mids, rims)]


def middle(two, block, ghost, near, near_ghost, up, down, *refs):
    passed, off, refs = refs[:4], refs[4], refs[5:]
    kx, ky, kz, diag, part, back = coefficients(refs[:14])
    side, edge, add, first, known, linear, adjoint, sa, b2, hot2, inward = refs[14:]
    core = lax.axis_index("gz")
    place = lax.axis_index("gy")
    half, ny, narrow = block.shape[1], block.shape[2], up.shape[2]
    count, last = ny // TILE, half - 1
    own = lambda j, i: with_ghost(block.at[j, i], ghost.at[j, i])
    outside, inside = core, 1 - core
    for j in range(4):
        side[j, outside, 0:ny, 0:narrow] = jnp.where(core == 0, up[j], passed[j][...])
        side[j, outside, 0:ny, narrow : 2 * narrow] = jnp.where(core == 0, passed[j][...], down[j])
        side[j, inside, 0:ny] = near[j]
        side[j, inside, ny : ny + TILE] = near_ghost[j]
    for j in range(0, 4, 2):
        if two:
            a, b = unpack_pair(place, off[at(count + 1 + j // 2)])
        else:
            a, b = off[at(count + 1 + j)], off[at(count + 2 + j)]
        side[j, outside, ny : ny + TILE] = a
        side[j + 1, outside, ny : ny + TILE] = b
    for which, i in ((0, 0), (1, last)):
        s, f, c = own(S, i), own(F, i), own(C, i)
        s_out, c_out, f_out = (whole(side.at[j, which]) for j in (S, C, F))
        for t in range(count + 1):
            face = (c[t] + c_out[t]) * scale
            edge[which, at(t)] = face
            v, beyond = s[t], s_out[t]
            if which == 0:
                inner_add = (face + time_step * f[t]) * beyond - face * v
                outer_add = face * (v - beyond)
            else:
                inner_add = face * (beyond - v)
                outer_add = (face + time_step * f_out[t]) * v - face * beyond
            first[i, at(t)] = part(i)[t] + (0.5 + f[t]) * inner_add
            add[which, at(t)] = (0.5 + f_out[t]) * outer_add
    for i in range(1, last):
        for t in range(count + 1):
            first[i, at(t)] = part(i)[t]
    for i in range(half):
        v, f, k, s, a = whole(first.at[i]), own(F, i), own(K, i), own(S, i), own(T, i)
        flow = Across(ky(i), kz(i), v)
        for t in range(count + 1):
            rc = 0.5 + f[t]
            sink = time_step * k[t]
            hot1 = jnp.tanh(v[t])
            full = diag(i)[t]
            if i == 0:
                full = full + edge[0, at(t)]
            if i == last:
                full = full + edge[1, at(t)]
            adjoint[i, at(t)] = full + sink * (1.0 - hot1 * hot1)
            rate = flow[t] - full * v[t] - sink * hot1
            if i > 0:
                rate = rate + (kx(i - 1)[t] + time_step * f[t]) * first[i - 1, at(t)]
            if i < last:
                rate = rate + kx(i)[t] * first[i + 1, at(t)]
            value = 0.75 * s[t] + 0.25 * (v[t] + rc * rate)
            b = a[t] * rc
            total = back(i)[t]
            if i == 0:
                total = total + edge[0, at(t)] * (side[T, 0, at(t)] * (0.5 + side[F, 0, at(t)]) - b)
            if i == last:
                high, high_f = edge[1, at(t)], side[F, 1, at(t)]
                total = total + ((high + time_step * high_f) * (side[T, 1, at(t)] * (0.5 + high_f)) - high * b)
            if i == 0 or i == last:
                which = 0 if i == 0 else 1
                known[which, at(t)] = value
                linear[which, at(t)] = total
            else:
                hot = jnp.tanh(value)
                hot2[i, at(t)] = hot
                total = (2.0 / 3.0) * (total - sink * (1.0 - hot * hot) * b)
                sa[i, at(t)] = total
                b2[i, at(t)] = total * rc
    for t in range(count + 1):
        inward[0, at(t)] = (kx(0)[t] + time_step * own(F, 1)[t]) * b2[1, at(t)]
        inward[1, at(t)] = kx(last - 1)[t] * b2[last - 1, at(t)]


def outward(block, ghost, one_mid, one_rim, edge, add, known, linear, off, hot2, sa, b2, off_b, on_b):
    core = lax.axis_index("gz")
    half, ny = block.shape[1], block.shape[2]
    count, last = ny // TILE, half - 1
    own = lambda j, i: with_ghost(block.at[j, i], ghost.at[j, i])
    for which, i in ((0, 0), (1, last)):
        f, k, a = own(F, i), own(K, i), own(T, i)
        mine = core == which
        for t in range(count + 1):
            one = jnp.where(mine, off[at(t)] + add[which, at(t)], mid_and_rim(one_mid, one_rim)[t])
            face = edge[which, at(t)]
            if which == 0:
                face = face + time_step * f[t]
            rc = 0.5 + f[t]
            hot = jnp.tanh(known[which, at(t)] + 0.25 * rc * face * one)
            total = (2.0 / 3.0) * (linear[which, at(t)] - time_step * k[t] * (1.0 - hot * hot) * (a[t] * rc))
            hot2[which, at(t)] = hot
            sa[which, at(t)] = total
            b2[which, at(t)] = total * rc
    off_b[...] = b2[core]
    on_b[...] = b2[1 - core]


def outward_first(ky_mid, kz_mid, ky_rim, kz_rim, adjoint, inward, sa, b2, fa, on_p, cross, along):
    core = lax.axis_index("gz")
    half, (ny, nz) = adjoint.shape[0], cross.shape
    for which, i in ((0, 0), (1, half - 1)):
        b = whole(b2.at[which])
        flow = Across(mid_and_rim(ky_mid.at[i], ky_rim.at[i]), mid_and_rim(kz_mid.at[i], kz_rim.at[i]), b)
        for t in range(len(b)):
            total = sa[which, at(t)] + flow[t] - adjoint[i, at(t)] * b[t] + inward[which, at(t)]
            fa[which, at(t)] = 0.25 * total
    on_p[...] = fa[1 - core, 0:ny]
    for t in range(ny // TILE):
        along[at(t)], cross[at(t)] = halves(core, fa[core, at(t)])


def inner(block, ghost, edge, side, first, adjoint, sa_in, b2_in, hot2_in, sa_out, b2_out, hot2_out, fa_out, *refs):
    kx, ky, kz, diag, _, _ = coefficients(refs[:14])
    value, term, adjoint0, hot0, fa, b3 = refs[14:]
    half, ny = block.shape[1], block.shape[2]
    count, last = ny // TILE, half - 1
    own = lambda j, i: with_ghost(block.at[j, i], ghost.at[j, i])
    pick = lambda i, inside, outside: inside.at[i] if 0 < i < last else outside.at[0 if i == 0 else 1]
    sa = lambda i: whole(pick(i, sa_in, sa_out))
    b2 = lambda i: whole(pick(i, b2_in, b2_out))
    hot2 = lambda i: whole(pick(i, hot2_in, hot2_out))
    for i in range(half):
        f = own(F, i)
        flow = Across(ky(i), kz(i), b2(i))
        for t in range(count + 1):
            if 0 < i < last:
                total = sa(i)[t] + flow[t] - adjoint[i, at(t)] * b2(i)[t]
                total = total + kx(i - 1)[t] * b2(i - 1)[t] + (kx(i)[t] + time_step * own(F, i + 1)[t]) * b2(i + 1)[t]
                total = 0.25 * total
            else:
                total = fa_out[0 if i == 0 else 1, at(t)]
            fa[i, at(t)] = total
            b3[i, at(t)] = total * (0.5 + f[t])
    for i in range(half):
        s, f, k, a = own(S, i), own(F, i), own(K, i), own(T, i)
        b = whole(b3.at[i])
        flow = Across(ky(i), kz(i), b)
        for t in range(count):
            hot = jnp.tanh(s[t])
            full = diag(i)[t]
            if i == 0:
                full = full + edge[0, at(t)]
            if i == last:
                full = full + edge[1, at(t)]
            full = full + time_step * k[t] * (1.0 - hot * hot)
            total = flow[t] - full * b[t] + fa[i, at(t)] + 0.75 * sa(i)[t] + a[t] * (1.0 / 3.0)
            if i > 0:
                total = total + kx(i - 1)[t] * b3[i - 1, at(t)]
            if i < last:
                total = total + (kx(i)[t] + time_step * own(F, i + 1)[t]) * b3[i + 1, at(t)]
            value[i, at(t)] = total
            first_hot = jnp.tanh(first[i, at(t)])
            total = (2.0 / 3.0) * hot2(i)[t] * a[t] + 0.25 * first_hot * sa(i)[t] + hot * fa[i, at(t)]
            term[i, at(t)] = -time_step * (0.5 + f[t]) * total
            if i == 0 or i == last:
                which = 0 if i == 0 else 1
                adjoint0[which, at(t)] = full
                hot0[which, at(t)] = -time_step * (0.5 + f[t]) * hot


class Pieces:
    def __init__(self, refs):
        self.refs, self.size = refs, refs[0].shape[0]

    def __getitem__(self, place):
        return self.refs[place // self.size][place % self.size]

    def __setitem__(self, place, value):
        self.refs[place[0] // self.size][place[0] % self.size, place[1]] = value


def halves(core, value):
    narrow = value.shape[1] // 2
    left, right = value[:, :narrow], value[:, narrow:]
    return jnp.where(core == 0, left, right), jnp.where(core == 0, right, left)


def finish(block, ghost, edge, side, b2_out, value, term, adjoint0, hot0, off_b, on_b, on_p, *refs):
    kx_mid, ky_mid, kz_mid, kx_rim, ky_rim, kz_rim, keep, *pieces, late = refs
    give = Pieces(pieces)
    core = lax.axis_index("gz")
    half, ny = block.shape[1], block.shape[2]
    count, last = ny // TILE, half - 1
    own = lambda j, i: with_ghost(block.at[j, i], ghost.at[j, i])
    both = lambda mid, rim: lambda i: mid_and_rim(mid.at[i], rim.at[i])
    kx, ky, kz = both(kx_mid, kx_rim), both(ky_mid, ky_rim), both(kz_mid, kz_rim)

    def write(place, t, value):
        keep[place, at(t)], give[place, at(t)] = halves(core, value)

    gains, factors = {}, {}
    for which, i in ((0, 0), (1, last)):
        mine = core == which
        f = own(F, i)
        for t in range(count + 1):
            face = edge[which, at(t)]
            if which == 1:
                face = face + time_step * side[F, 1, at(t)]
            gain = 0.25 * face * jnp.where(mine, off_b[at(t)], on_b[at(t)])
            late[which, at(t)] = gain * (0.5 + f[t])
            gains[which, t] = gain
    for which, i in ((0, 0), (1, last)):
        mine = core == which
        flow = Across(ky(i), kz(i), whole(late.at[which]))
        for t in range(count):
            face, f_out = edge[which, at(t)], side[F, which, at(t)]
            into, out_of = face, face
            if which == 0:
                out_of = out_of + time_step * own(F, 0)[t]
            else:
                into = into + time_step * f_out
            total = value[i, at(t)] + gains[which, t] + flow[t] - adjoint0[which, at(t)] * late[which, at(t)]
            into = into * (0.5 + f_out)
            known = 0.25 * out_of * b2_out[which, at(t)]
            write(half + i, t, total + into * jnp.where(mine, known, known + on_p[at(t)]))
            write(i, t, term[i, at(t)] + hot0[which, at(t)] * gains[which, t])
            factors[which, t] = into
    for t in range(count):
        write(2 * half, t, jnp.where(core == 0, factors[0, t], factors[1, t]))
    for i in range(1, last):
        for t in range(count):
            total = value[i, at(t)]
            if i == 1:
                total = total + kx(0)[t] * late[0, at(t)]
            if i == last - 1:
                total = total + (kx(last - 1)[t] + time_step * own(F, last)[t]) * late[1, at(t)]
            write(half + i, t, total)
            write(i, t, term[i, at(t)])


def take(cross, along, cross_out, along_out):
    cross_out[...] = cross[...]
    along_out[...] = along[...]


def assemble(labels, keep, cross, along, *refs):
    *pieces, grad_state, grad_sink = refs
    core = lax.axis_index("gz")
    count = grad_state.shape[0]
    half = count // 2
    for start, source in ((core * half, keep), ((1 - core) * half, Pieces(pieces))):
        for i in range(half):
            grad_state[start + i] = source[half + i]
            grad_sink[start + i] = jnp.where(touching(labels[start + i]), source[i], 0.0)
    for plane, source, adjoint in ((core * (count - 1), keep, cross), ((1 - core) * (count - 1), Pieces(pieces), along)):
        grad_state[plane] = grad_state[plane] + source[2 * half] * adjoint[...]


def on_device(state, conduct, sink, labels, cotangent):
    count, ny, nz = state.shape
    half, wide, rows = count // 2, 2 * nz, ny + TILE
    count_x, count_y = lax.axis_size("gx"), lax.axis_size("gy")
    assert lax.axis_size("gz") == 2 and half >= 3 and ny % TILE == 0 and ny >= 3 * TILE
    two = count_y == 2
    ahead = [(i, (i + 1) % count_x) for i in range(count_x)]
    behind = [(b, a) for a, b in ahead]
    chips = [(2 * i + 1, (2 * i + 2) % (2 * count_x)) for i in range(count_x)]
    chips = chips + [(b, a) for a, b in chips]

    def swap_cores(x):
        return lax.ppermute(x, "gz", [(0, 1), (1, 0)])

    def swap_chips(x):
        return lax.ppermute(x, ("gx", "gz"), chips)

    def to_slabs(x):
        route = [(2 * i + c, 2 * ((i + 2 * c - 1) % count_x) + c) for i in range(count_x) for c in range(2)]
        return lax.ppermute(x, ("gx", "gz"), route)

    def along_y(rims):
        forward = [(i, (i + 1) % count_y) for i in range(count_y)]
        backward = [(b, a) for a, b in forward]
        routes = [forward] if two else [backward, forward]
        return [lax.ppermute(rim, "gy", routes[i % len(routes)]) for i, rim in enumerate(rims)]

    ways = 1 if two else 2
    inputs = (state, conduct, sink, labels, cotangent)
    plane, span = (4, ny, nz), (5, half + 2, ny, nz)
    kinds = pltpu.VMEM((half + 2, ny, nz), jnp.int32)
    drains = pltpu.VMEM((half + 2, ny, nz), jnp.float32)
    sems = lambda many: pltpu.SemaphoreType.DMA((many,))
    up, down, trade = call(
        pack_inputs, [plane, plane, span], *inputs, given=HBM,
        scratch=[kinds, drains, pltpu.VMEM((2, ny, nz), jnp.int32), sems(5), sems(8)],
    )
    up = lax.ppermute(up, "gx", ahead)
    down = lax.ppermute(down, "gx", behind)
    traded = swap_cores(trade)
    (mine,) = call(own_planes, [span], *inputs, given=HBM, scratch=[kinds, drains, sems(5)])
    block, near = call(gather_planes, [(5, half, ny, wide), (7, ny, wide)], mine, traded)
    sizes = [4, (5 * half + 1) // 2]
    rims = call(functools.partial(pack_along_y, two), [(n, TILE, wide) for n in sizes for _ in range(ways)], block, near)
    rims = along_y(rims)
    split = lambda r: [(half - 1, r, wide)] + [(half, r, wide)] * 5 + [(r, wide)]
    mids = call(functools.partial(prepare_mid, count_y), split(ny - 2 * TILE), block, near)
    ghost, near_ghost, *edges = call(
        functools.partial(prepare_rim, two, count_y),
        [(5, half, TILE, wide), (7, TILE, wide)] + split(3 * TILE), block, near, *rims,
    )
    off, _ = call(
        functools.partial(pack_off, two, count_y), [(rows + (2 if two else 4) * TILE, wide), (7, TILE, wide)],
        block, mids[4], *rims[:ways],
    )
    passed = call(choose_half, [(ny, nz)] * 4, up, down, *rims)
    passed = [swap_cores(x) for x in passed]
    off = swap_chips(off)
    own, outer = (half, rows, wide), (2, rows, wide)
    side, edge, add, first, known, linear, adjoint, sa, b2, hot2, inward = call(
        functools.partial(middle, two),
        [(4, 2, rows, wide), outer, outer, own, outer, outer, own, own, own, own, outer],
        block, ghost, near, near_ghost, up, down, *passed, off, *mids, *edges,
    )
    ends, mains = (rows, wide), (ny, wide)
    hot2_out, sa_out, b2_out, off_b, on_b = call(
        outward, [outer] * 3 + [ends] * 2, block, ghost, mids[6], edges[6], edge, add, known, linear, off
    )
    off_b, on_b = swap_chips(off_b), swap_cores(on_b)
    fa_out, on_p, cross, along = call(
        outward_first, [outer, mains, (ny, nz), (ny, nz)],
        mids[1], mids[2], edges[1], edges[2], adjoint, inward, sa_out, b2_out,
    )
    on_p, cross, along = swap_cores(on_p), swap_chips(cross), to_slabs(along)
    main = lambda planes: (planes, ny, wide)
    value, term, adjoint0, hot0, _, _ = call(
        inner, [main(half), main(half), main(2), main(2), own, own],
        block, ghost, edge, side, first, adjoint, sa, b2, hot2, sa_out, b2_out, hot2_out, fa_out, *mids, *edges,
    )
    most = (2 * half + 1, ny, nz)
    pieces = RETURNS if most[0] % RETURNS == 0 else 1
    keep, *give, _ = call(
        finish, [most] + [(most[0] // pieces, ny, nz)] * pieces + [outer],
        block, ghost, edge, side, b2_out, value, term, adjoint0, hot0, off_b, on_b, on_p, *mids[:3], *edges[:3],
    )
    got = [swap_cores(x) for x in give]
    cross, along = call(take, [(ny, nz)] * 2, cross, along, flops=FLOPS)
    grad_state, grad_sink = call(
        assemble, [state.shape, state.shape], labels, keep, cross, along, *got, keep=False
    )
    return (grad_state, grad_sink)


def solution(mesh):
    block = P(("groups", "gx"), "gy", "gz")
    in_specs = (block, P("gx", "gy", "gz"), block, block, block)
    return jax.shard_map(on_device, mesh=mesh, in_specs=in_specs, out_specs=(block, block), check_vma=False)
```

```python
import functools

import jax
import jax.numpy as jnp
from jax import lax
from jax.experimental import pallas as pl
from jax.experimental.pallas import tpu as pltpu
from jax.sharding import PartitionSpec as P

VMEM = pltpu.VMEM
HBM = pltpu.HBM
time_step = 0.06
scale = 0.5 * time_step
HALO = 4
TILE = 8
SWEPT = 11
PACK_FLOPS = 700000000
FLOPS = 100000000000
S, C, T, F, K = range(5)
ONE = 4


def call(kernel, outs, *ins, keep=True, given=VMEM, scratch=(), flops=1024, aliases=None):
    space = VMEM if keep else jax.ShapeDtypeStruct
    block = pl.BlockSpec(memory_space=VMEM if given is VMEM else pl.ANY)
    return pl.pallas_call(
        kernel,
        out_shape=[space(shape, jnp.float32) for shape in outs],
        in_specs=[block] * len(ins),
        out_specs=[pl.BlockSpec(memory_space=VMEM if keep else pl.ANY)] * len(outs),
        scratch_shapes=list(scratch),
        input_output_aliases=aliases or {},
        compiler_params=pltpu.CompilerParams(vmem_limit_bytes=8 * 1024 * 1024),
        cost_estimate=pl.CostEstimate(flops=flops, bytes_accessed=1024, transcendentals=0),
    )(*[pltpu.with_memory_space_constraint(x, given) for x in ins])


def half_fluid(labels):
    return jnp.where(labels <= 1, 0.5, 0.0)


def touching(labels):
    return jnp.logical_or(labels == 1, labels == 2)


def rows_of(value):
    return lax.broadcasted_iota(jnp.int32, value.shape, 0)


def lanes_of(value):
    return lax.broadcasted_iota(jnp.int32, value.shape, 1)


def down_rows(before, here):
    return pltpu.roll(jnp.where(rows_of(here) == TILE - 1, before, here), 1, 0)


def up_rows(here, after):
    return pltpu.roll(jnp.where(rows_of(here) == 0, after, here), TILE - 1, 0)


def down_lanes(here):
    return pltpu.roll(here, 1, 1)


def up_lanes(here):
    return pltpu.roll(here, here.shape[1] - 1, 1)


def at(t):
    return slice(t * TILE, (t + 1) * TILE)


class Tiles:
    def __init__(self, *places):
        self.places = places

    def __getitem__(self, t):
        ref, slot = self.places[t % len(self.places)]
        return ref[at(slot)]

    def __setitem__(self, t, value):
        ref, slot = self.places[t]
        ref[at(slot)] = value

    def __len__(self):
        return len(self.places)


def whole(ref):
    return Tiles(*[(ref, t) for t in range(ref.shape[0] // TILE)])


def with_ghost(main, ghost):
    return Tiles(*[(main, t) for t in range(main.shape[0] // TILE)], (ghost, 0))


def mid_and_rim(mid, rim):
    return Tiles((rim, 0), *[(mid, t) for t in range(mid.shape[0] // TILE)], (rim, 1), (rim, 2))


class Across:
    def __init__(self, ky, kz, v):
        self.ky, self.kz, self.v = ky, kz, v
        self.known = {}

    def product(self, t):
        t = t % len(self.v)
        if t not in self.known:
            self.known[t] = self.ky[t] * self.v[t]
        return self.known[t]

    def __getitem__(self, t):
        here, kz = self.v[t], self.kz[t]
        along_y = self.ky[t] * down_rows(self.v[t - 1], here) + up_rows(self.product(t), self.product(t + 1))
        return along_y + (kz * down_lanes(here) + up_lanes(kz * here))


class Made:
    def __init__(self, values):
        self.values = values

    def __getitem__(self, t):
        return self.values[t % len(self.values)]

    def __len__(self):
        return len(self.values)


def sides_along_z(c, here):
    lanes = lanes_of(c)
    left = here + jnp.where(lanes == 0, 0.0, down_lanes(c)) * scale
    right = here + jnp.where(lanes == lanes.shape[1] - 1, 0.0, up_lanes(c)) * scale
    return left, right


def load_all(pairs, sems):
    copies = [pltpu.make_async_copy(a, b, sems.at[i]) for i, (a, b) in enumerate(pairs)]
    for copy in copies:
        copy.start()
    return copies


def load_planes(inputs, start, out, kinds, drains, sems):
    state, conduct, sink, labels, cotangent = inputs
    part = pl.ds(start, out.shape[1])
    pairs = [(labels.at[part], kinds), (sink.at[part], drains), (state.at[part], out.at[S])]
    return load_all(pairs + [(conduct.at[part], out.at[C]), (cotangent.at[part], out.at[T])], sems)


def fill_planes(out, kinds, drains):
    for i in range(out.shape[1]):
        out[F, i] = half_fluid(kinds[i])
        out[K, i] = jnp.where(touching(kinds[i]), drains[i], 0.0)


def pack_inputs(state, conduct, sink, labels, cotangent, up, down, trade, kinds, drains, ends, sems, plane_sems):
    count = state.shape[0]
    pairs = []
    for which, (out, plane) in enumerate(((up, count - 1), (down, 0))):
        pairs += [(state.at[plane], out.at[S]), (conduct.at[plane], out.at[C]), (cotangent.at[plane], out.at[T])]
        pairs += [(labels.at[plane], ends.at[which])]
    copies = load_all(pairs, plane_sems)
    start = (1 - lax.axis_index("gz")) * (count - trade.shape[1])
    copies += load_planes((state, conduct, sink, labels, cotangent), start, trade, kinds, drains, sems)
    for copy in copies:
        copy.wait()
    up[F] = half_fluid(ends[0])
    down[F] = half_fluid(ends[1])
    fill_planes(trade, kinds, drains)


def own_planes(state, conduct, sink, labels, cotangent, mine, kinds, drains, sems):
    start = lax.axis_index("gz") * (state.shape[0] - mine.shape[1])
    for copy in load_planes((state, conduct, sink, labels, cotangent), start, mine, kinds, drains, sems):
        copy.wait()
    fill_planes(mine, kinds, drains)


def pack_rims(two, planes, outs):
    for k in range(0, len(planes), 2):
        even, odd = planes[k], planes[min(k + 1, len(planes) - 1)]
        ny = even.shape[0]
        low_even, high_even = even[0:TILE], even[ny - TILE : ny]
        low_odd, high_odd = odd[0:TILE], odd[ny - TILE : ny]
        upper = rows_of(low_even) < HALO
        low = jnp.where(upper, low_even, pltpu.roll(low_odd, HALO, 0))
        high = jnp.where(upper, pltpu.roll(high_even, HALO, 0), high_odd)
        if two:
            outs[0][k // 2] = jnp.where(lax.axis_index("gy") == 0, high, low)
        else:
            outs[0][k // 2] = low
            outs[1][k // 2] = high


def unpack_rims(two, count_y, rims, planes):
    place = lax.axis_index("gy")
    for k in range(0, len(planes), 2):
        above = jnp.where(place < count_y - 1, rims[0][k // 2], 0.0)
        below = jnp.where(place > 0, rims[0 if two else 1][k // 2], 0.0)
        upper = rows_of(above) < HALO
        planes[k][...] = jnp.where(upper, above, pltpu.roll(below, HALO, 0))
        if k + 1 < len(planes):
            planes[k + 1][...] = jnp.where(upper, pltpu.roll(above, HALO, 0), below)


def gather_planes(mine, traded, block, near):
    core = lax.axis_index("gz")
    half, narrow = block.shape[1], mine.shape[3]
    own = pl.ds(pl.multiple_of(core * narrow, 128), narrow)
    other = pl.ds(pl.multiple_of((1 - core) * narrow, 128), narrow)
    start = 2 * core
    beside = (1 - core) * half + core
    beyond = (1 - core) * (half + 1)
    for j in range(5):
        for i in range(half):
            block[j, i, :, own] = mine[j, start + i]
            block[j, i, :, other] = traded[j, start + i]
        near[j, :, own] = mine[j, beside]
        near[j, :, other] = traded[j, beside]
        if j in (S, C):
            near[5 + j, :, own] = mine[j, beyond]
            near[5 + j, :, other] = traded[j, beyond]


def rim_planes(block, near):
    half = block.shape[1]
    core = lax.axis_index("gz")
    inward = lambda i: core * (half - 1) + i * (1 - 2 * core)
    early = [block.at[j, inward(0)] for j in range(5)] + [block.at[j, inward(1)] for j in (S, C)]
    late = [block.at[j, inward(1)] for j in (T, F, K)] + [block.at[j, inward(i)] for i in range(2, half) for j in range(5)]
    return early, late + [near.at[j] for j in range(7)]


def pack_along_y(two, block, near, *rims):
    early, late = rim_planes(block, near)
    ways = 1 if two else 2
    pack_rims(two, early, rims[:ways])
    pack_rims(two, late, rims[ways:])


class Lazy:
    def __init__(self, count, make):
        self.count, self.make, self.known = count, make, {}

    def __getitem__(self, t):
        t = t % self.count
        if t not in self.known:
            self.known[t] = self.make(t)
        return self.known[t]

    def __len__(self):
        return self.count


def prepare(todo, count_y, block, near, ghost, near_ghost, kx, ky_out, kz_out, diag, part, back, one):
    place = lax.axis_index("gy")
    core = lax.axis_index("gz")
    half, ny = block.shape[1], block.shape[2]
    count, last = ny // TILE + 1, half - 1

    def own(j, i):
        if ghost is None:
            return Tiles(*[(block.at[j, i], t) for t in range(count - 1)], (None, 0))
        return with_ghost(block.at[j, i], ghost.at[j, i])

    def next_to(j):
        if ghost is None:
            return Tiles(*[(near.at[j], t) for t in range(count - 1)], (None, 0))
        return with_ghost(near.at[j], near_ghost.at[j])

    def faces_along_y(c):
        def make(t):
            value = (c[t] + down_rows(c[t - 1], c[t])) * scale
            if t == 0:
                value = jnp.where(jnp.logical_and(rows_of(value) == 0, place == 0), 0.0, value)
            if t == count - 1:
                value = jnp.where(jnp.logical_and(rows_of(value) == 0, place == count_y - 1), 0.0, value)
            return value

        return Lazy(count, make)

    def own_weight(c, f, t):
        here = c[t] * scale
        left, right = sides_along_z(c[t], here)
        low, high = down_rows(c[t - 1], c[t]), up_rows(c[t], c[t + 1])
        return left, (2.0 * here + (low + high) * scale) + (left + right) + time_step * f[t]

    for i in range(half):
        s, c, a, f, k = (own(j, i) for j in (S, C, T, F, K))
        ky, kz = faces_along_y(c), {}
        for t in todo:
            left, weight = own_weight(c, f, t)
            kz[t] = jnp.where(lanes_of(left) == 0, 0.0, left)
            slot = at(todo.index(t))
            if i > 0:
                face = (c[t] + own(C, i - 1)[t]) * scale
                kx[i - 1, slot] = face
                weight = weight + face
            if i < last:
                weight = weight + (c[t] + own(C, i + 1)[t]) * scale
            diag[i, slot] = weight
            ky_out[i, slot] = ky[t]
            kz_out[i, slot] = kz[t]
        scaled = Lazy(count, lambda t, a=a, f=f: a[t] * (0.5 + f[t]))
        ahead = Across(ky, kz, s)
        behind = Across(ky, kz, scaled)
        for t in todo:
            slot = at(todo.index(t))
            d, b = diag[i, slot], scaled[t]
            go = ahead[t] - d * s[t] - time_step * k[t] * jnp.tanh(s[t])
            come = behind[t] - d * b
            if i > 0:
                go = go + (kx[i - 1, slot] + time_step * f[t]) * own(S, i - 1)[t]
                come = come + kx[i - 1, slot] * (own(T, i - 1)[t] * (0.5 + own(F, i - 1)[t]))
            if i < last:
                face, high_f = (c[t] + own(C, i + 1)[t]) * scale, own(F, i + 1)[t]
                go = go + face * own(S, i + 1)[t]
                come = come + (face + time_step * high_f) * (own(T, i + 1)[t] * (0.5 + high_f))
            part[i, slot] = s[t] + (0.5 + f[t]) * go
            back[i, slot] = a[t] + come
    s, c, f, k = (next_to(j) for j in (S, C, F, K))
    kz = {}
    for t in todo:
        left, _ = own_weight(c, f, t)
        kz[t] = jnp.where(lanes_of(left) == 0, 0.0, left)
    ahead = Across(faces_along_y(c), kz, s)
    is_low = core == 0
    for t in todo:
        _, weight = own_weight(c, f, t)
        c_own = jnp.where(is_low, own(C, last)[t], own(C, 0)[t])
        s_own = jnp.where(is_low, own(S, last)[t], own(S, 0)[t])
        face_own, face_far = (c[t] + c_own) * scale, (c[t] + next_to(5 + C)[t]) * scale
        wind = time_step * f[t]
        go = ahead[t] - (weight + face_own + face_far) * s[t] - time_step * k[t] * jnp.tanh(s[t])
        go = go + (face_own + jnp.where(is_low, wind, 0.0)) * s_own
        go = go + (face_far + jnp.where(is_low, 0.0, wind)) * next_to(5 + S)[t]
        one[at(todo.index(t))] = s[t] + (0.5 + f[t]) * go


def prepare_mid(count_y, block, near, *outs):
    prepare(list(range(1, block.shape[2] // TILE - 1)), count_y, block, near, None, None, *outs)


def prepare_rim(two, count_y, block, near, *refs):
    ways = 1 if two else 2
    rims, (ghost, near_ghost, *outs) = refs[: 2 * ways], refs[2 * ways :]
    count = block.shape[2] // TILE
    early, late = rim_planes(ghost, near_ghost)
    unpack_rims(two, count_y, rims[:ways], early)
    unpack_rims(two, count_y, rims[ways:], late)
    prepare([0, count - 1, count], count_y, block, near, ghost, near_ghost, *outs)


PACKED = (((S, 3), (C, 3), (ONE, 2)), ((T, 2), (F, 2)))


def pack_ghosts(place, parts, ghosts):
    rows = rows_of(ghosts[S])
    low = high = jnp.zeros_like(ghosts[S])
    taken = 0
    for j, depth in parts:
        span = jnp.logical_and(rows >= taken, rows < taken + depth)
        low = jnp.where(span, pltpu.roll(ghosts[j], taken, 0) if taken else ghosts[j], low)
        span = jnp.logical_and(rows >= TILE - taken - depth, rows < TILE - taken)
        high = jnp.where(span, pltpu.roll(ghosts[j], TILE - taken, 0) if taken else ghosts[j], high)
        taken += depth
    return jnp.where(place == 0, low, high)


def unpack_ghosts(place, parts, packed):
    rows = rows_of(packed)
    ghosts, taken = {}, 0
    for j, depth in parts:
        low = pltpu.roll(packed, TILE - taken, 0) if taken else packed
        high = pltpu.roll(packed, taken, 0) if taken else packed
        low = jnp.where(rows < depth, low, 0.0)
        high = jnp.where(rows >= TILE - depth, high, 0.0)
        ghosts[j] = jnp.where(place == 0, low, high)
        taken += depth
    return ghosts


def pack_off(two, count_y, block, part_mid, *refs):
    ways = 1 if two else 2
    rims, (off, ghost) = refs[:ways], refs[ways:]
    place = lax.axis_index("gy")
    core = lax.axis_index("gz")
    last = block.shape[1] - 1
    outer = core * last
    inside = outer + 1 - 2 * core
    unpack_rims(two, count_y, rims, [ghost.at[j] for j in range(7)])
    s, c, f, k = (with_ghost(block.at[j, outer], ghost.at[j]) for j in (S, C, F, K))
    s_in, c_in = (with_ghost(block.at[j, inside], ghost.at[5 + j]) for j in (S, C))
    count = len(s)

    def face_along_y(t):
        value = (c[t] + down_rows(c[t - 1], c[t])) * scale
        if t == 0:
            value = jnp.where(jnp.logical_and(rows_of(value) == 0, place == 0), 0.0, value)
        if t == count - 1:
            value = jnp.where(jnp.logical_and(rows_of(value) == 0, place == count_y - 1), 0.0, value)
        return value

    todo, kz, weight = (0, count - 2, count - 1), {}, {}
    for t in todo:
        here = c[t] * scale
        left, right = sides_along_z(c[t], here)
        kz[t] = jnp.where(lanes_of(left) == 0, 0.0, left)
        low, high = down_rows(c[t - 1], c[t]), up_rows(c[t], c[t + 1])
        weight[t] = (2.0 * here + (low + high) * scale) + (left + right) + time_step * f[t]
    flow = Across(Lazy(count, face_along_y), kz, s)
    one = {}
    for t in range(count):
        if t in todo:
            face = (c[t] + c_in[t]) * scale
            go = flow[t] - (weight[t] + face) * s[t] - time_step * k[t] * jnp.tanh(s[t])
            go = go + (face + jnp.where(core == 0, 0.0, time_step) * f[t]) * s_in[t]
            one[t] = s[t] + (0.5 + f[t]) * go
        else:
            one[t] = part_mid[outer, at(t - 1)]
        if t < count - 1:
            off[at(t)] = one[t]
    ghosts = {j: ghost[j] for j in range(4)}
    ghosts[ONE] = one[count - 1]
    if two:
        for slot, parts in enumerate(PACKED):
            off[at(count - 1 + slot)] = pack_ghosts(place, parts, ghosts)
    else:
        for j in range(5):
            off[at(count - 1 + j)] = ghosts[j]


def choose_half(up, down, *refs):
    for j in range(4):
        refs[j - 4][...] = jnp.where(lax.axis_index("gz") == 0, down[j], up[j])


def coefficients(refs):
    mids, rims = refs[:6], refs[7:13]
    return [lambda i, m=m, r=r: mid_and_rim(m.at[i], r.at[i]) for m, r in zip(mids, rims)]


def fill_sides(near, near_ghost, up, down, passed, side):
    core = lax.axis_index("gz")
    ny, narrow = up.shape[1], up.shape[2]
    outside, inside = core, 1 - core
    for j in range(4):
        side[j, outside, 0:ny, 0:narrow] = jnp.where(core == 0, up[j], passed[j][...])
        side[j, outside, 0:ny, narrow : 2 * narrow] = jnp.where(core == 0, passed[j][...], down[j])
        side[j, inside, 0:ny] = near[j]
        side[j, inside, ny : ny + TILE] = near_ghost[j]


def fill_side_ghosts(two, ny, off, side):
    place, outside = lax.axis_index("gy"), lax.axis_index("gz")
    first = ny // TILE
    if two:
        ghosts = {}
        for slot, parts in enumerate(PACKED):
            ghosts.update(unpack_ghosts(place, parts, off[at(first + slot)]))
    else:
        ghosts = {j: off[at(first + j)] for j in range(5)}
    for j in range(4):
        side[j, outside, ny : ny + TILE] = ghosts[j]
    return ghosts[ONE]


def sweep(late, block, ghost, weights, side, edge, add, first, known, linear, adjoint, sa, b2, hot2, inward):
    kx, ky, kz, diag, part, back = weights
    half, ny = block.shape[1], block.shape[2]
    count, last = ny // TILE, half - 1
    own = lambda j, i: with_ghost(block.at[j, i], ghost.at[j, i])
    for which, i in ((0, 0), (1, last)):
        s, f, c = own(S, i), own(F, i), own(C, i)
        s_out, c_out, f_out = (whole(side.at[j, which]) for j in (S, C, F))
        for t in [count] if late else range(count):
            face = (c[t] + c_out[t]) * scale
            edge[which, at(t)] = face
            v, beyond = s[t], s_out[t]
            if which == 0:
                inner_add = (face + time_step * f[t]) * beyond - face * v
                outer_add = face * (v - beyond)
            else:
                inner_add = face * (beyond - v)
                outer_add = (face + time_step * f_out[t]) * v - face * beyond
            first[i, at(t)] = part(i)[t] + (0.5 + f[t]) * inner_add
            add[which, at(t)] = (0.5 + f_out[t]) * outer_add
    for i in range(1, last):
        for t in [] if late else range(count + 1):
            first[i, at(t)] = part(i)[t]
    for i in range(half):
        outer = i in (0, last)
        v, f, k, s, a = whole(first.at[i]), own(F, i), own(K, i), own(S, i), own(T, i)
        flow = Across(ky(i), kz(i), v)
        if outer:
            todo = [0, count - 1, count] if late else range(1, count - 1)
        else:
            todo = [count] if late else range(count)
        for t in todo:
            rc = 0.5 + f[t]
            sink = time_step * k[t]
            hot1 = jnp.tanh(v[t])
            full = diag(i)[t]
            if i == 0:
                full = full + edge[0, at(t)]
            if i == last:
                full = full + edge[1, at(t)]
            adjoint[i, at(t)] = full + sink * (1.0 - hot1 * hot1)
            rate = flow[t] - full * v[t] - sink * hot1
            if i > 0:
                rate = rate + (kx(i - 1)[t] + time_step * f[t]) * first[i - 1, at(t)]
            if i < last:
                rate = rate + kx(i)[t] * first[i + 1, at(t)]
            value = 0.75 * s[t] + 0.25 * (v[t] + rc * rate)
            b = a[t] * rc
            total = back(i)[t]
            if i == 0:
                total = total + edge[0, at(t)] * (side[T, 0, at(t)] * (0.5 + side[F, 0, at(t)]) - b)
            if i == last:
                high, high_f = edge[1, at(t)], side[F, 1, at(t)]
                total = total + ((high + time_step * high_f) * (side[T, 1, at(t)] * (0.5 + high_f)) - high * b)
            if outer:
                which = 0 if i == 0 else 1
                known[which, at(t)] = value
                linear[which, at(t)] = total
            else:
                hot = jnp.tanh(value)
                hot2[i, at(t)] = hot
                total = (2.0 / 3.0) * (total - sink * (1.0 - hot * hot) * b)
                sa[i, at(t)] = total
                b2[i, at(t)] = total * rc
    for t in [count] if late else range(count):
        inward[0, at(t)] = (kx(0)[t] + time_step * own(F, 1)[t]) * b2[1, at(t)]
        inward[1, at(t)] = kx(last - 1)[t] * b2[last - 1, at(t)]


def middle(block, ghost, near, near_ghost, up, down, *refs):
    passed, weights, outs = refs[:4], coefficients(refs[4:18]), refs[18:]
    fill_sides(near, near_ghost, up, down, passed, outs[0])
    sweep(False, block, ghost, weights, *outs)


def outward(two, block, ghost, off, *refs):
    weights, one_mid, one_rim = coefficients(refs[:14]), refs[6], refs[13]
    outs = refs[14 + SWEPT : 14 + 2 * SWEPT]
    hot2, sa, b2, off_b, on_b = refs[14 + 2 * SWEPT :]
    side, edge, add, _, known, linear, *_ = outs
    core = lax.axis_index("gz")
    half, ny = block.shape[1], block.shape[2]
    count, last = ny // TILE, half - 1
    own = lambda j, i: with_ghost(block.at[j, i], ghost.at[j, i])
    one_ghost = fill_side_ghosts(two, ny, off, side)
    sweep(True, block, ghost, weights, *outs)
    for which, i in ((0, 0), (1, last)):
        f, k, a = own(F, i), own(K, i), own(T, i)
        mine = core == which
        for t in range(count + 1):
            one = off[at(t)] if t < count else one_ghost
            one = jnp.where(mine, one + add[which, at(t)], mid_and_rim(one_mid, one_rim)[t])
            face = edge[which, at(t)]
            if which == 0:
                face = face + time_step * f[t]
            rc = 0.5 + f[t]
            hot = jnp.tanh(known[which, at(t)] + 0.25 * rc * face * one)
            total = (2.0 / 3.0) * (linear[which, at(t)] - time_step * k[t] * (1.0 - hot * hot) * (a[t] * rc))
            hot2[which, at(t)] = hot
            sa[which, at(t)] = total
            b2[which, at(t)] = total * rc
    off_b[...] = b2[core]
    on_b[...] = b2[1 - core]


def outward_first(ky_mid, kz_mid, ky_rim, kz_rim, adjoint, inward, sa, b2, fa, on_p, cross, along):
    core = lax.axis_index("gz")
    half, (ny, nz) = adjoint.shape[0], cross.shape
    for which, i in ((0, 0), (1, half - 1)):
        b = whole(b2.at[which])
        flow = Across(mid_and_rim(ky_mid.at[i], ky_rim.at[i]), mid_and_rim(kz_mid.at[i], kz_rim.at[i]), b)
        for t in range(len(b)):
            total = sa[which, at(t)] + flow[t] - adjoint[i, at(t)] * b[t] + inward[which, at(t)]
            fa[which, at(t)] = 0.25 * total
    on_p[...] = fa[1 - core, 0:ny]
    for t in range(ny // TILE):
        along[at(t)], cross[at(t)] = halves(core, fa[core, at(t)])


def inner(block, ghost, edge, side, first, adjoint, sa_in, b2_in, hot2_in, sa_out, b2_out, hot2_out, fa_out, *refs):
    kx, ky, kz, diag, _, _ = coefficients(refs[:14])
    value, term, adjoint0, hot0, keep, give, fa, b3 = refs[14:]
    core = lax.axis_index("gz")
    half, ny = block.shape[1], block.shape[2]
    count, last = ny // TILE, half - 1
    own = lambda j, i: with_ghost(block.at[j, i], ghost.at[j, i])
    pick = lambda i, inside, outside: inside.at[i] if 0 < i < last else outside.at[0 if i == 0 else 1]
    sa = lambda i: whole(pick(i, sa_in, sa_out))
    b2 = lambda i: whole(pick(i, b2_in, b2_out))
    hot2 = lambda i: whole(pick(i, hot2_in, hot2_out))
    for i in range(half):
        f = own(F, i)
        flow = Across(ky(i), kz(i), b2(i))
        for t in range(count + 1):
            if 0 < i < last:
                total = sa(i)[t] + flow[t] - adjoint[i, at(t)] * b2(i)[t]
                total = total + kx(i - 1)[t] * b2(i - 1)[t] + (kx(i)[t] + time_step * own(F, i + 1)[t]) * b2(i + 1)[t]
                total = 0.25 * total
            else:
                total = fa_out[0 if i == 0 else 1, at(t)]
            fa[i, at(t)] = total
            b3[i, at(t)] = total * (0.5 + f[t])
    for i in range(half):
        s, f, k, a = own(S, i), own(F, i), own(K, i), own(T, i)
        b = whole(b3.at[i])
        flow = Across(ky(i), kz(i), b)
        for t in range(count):
            hot = jnp.tanh(s[t])
            full = diag(i)[t]
            if i == 0:
                full = full + edge[0, at(t)]
            if i == last:
                full = full + edge[1, at(t)]
            full = full + time_step * k[t] * (1.0 - hot * hot)
            total = flow[t] - full * b[t] + fa[i, at(t)] + 0.75 * sa(i)[t] + a[t] * (1.0 / 3.0)
            if i > 0:
                total = total + kx(i - 1)[t] * b3[i - 1, at(t)]
            if i < last:
                total = total + (kx(i)[t] + time_step * own(F, i + 1)[t]) * b3[i + 1, at(t)]
            value[i, at(t)] = total
            first_hot = jnp.tanh(first[i, at(t)])
            total = (2.0 / 3.0) * hot2(i)[t] * a[t] + 0.25 * first_hot * sa(i)[t] + hot * fa[i, at(t)]
            total = -time_step * (0.5 + f[t]) * total
            if 0 < i < last:
                keep[i - 1, at(t)], give[i - 1, at(t)] = halves(core, total)
            else:
                which = 0 if i == 0 else 1
                term[which, at(t)] = total
                adjoint0[which, at(t)] = full
                hot0[which, at(t)] = -time_step * (0.5 + f[t]) * hot


def halves(core, value):
    narrow = value.shape[1] // 2
    left, right = value[:, :narrow], value[:, narrow:]
    return jnp.where(core == 0, left, right), jnp.where(core == 0, right, left)


def finish(block, ghost, edge, side, b2_out, value, term, adjoint0, hot0, off_b, on_b, on_p, *refs):
    kx_mid, ky_mid, kz_mid, kx_rim, ky_rim, kz_rim, keep, give, late = refs
    core = lax.axis_index("gz")
    half, ny = block.shape[1], block.shape[2]
    count, last = ny // TILE, half - 1
    own = lambda j, i: with_ghost(block.at[j, i], ghost.at[j, i])
    both = lambda mid, rim: lambda i: mid_and_rim(mid.at[i], rim.at[i])
    kx, ky, kz = both(kx_mid, kx_rim), both(ky_mid, ky_rim), both(kz_mid, kz_rim)

    def write(place, t, value):
        keep[place, at(t)], give[place, at(t)] = halves(core, value)

    gains, factors = {}, {}
    for which, i in ((0, 0), (1, last)):
        mine = core == which
        f = own(F, i)
        for t in range(count + 1):
            face = edge[which, at(t)]
            if which == 1:
                face = face + time_step * side[F, 1, at(t)]
            gain = 0.25 * face * jnp.where(mine, off_b[at(t)], on_b[at(t)])
            late[which, at(t)] = gain * (0.5 + f[t])
            gains[which, t] = gain
    for which, i in ((0, 0), (1, last)):
        mine = core == which
        flow = Across(ky(i), kz(i), whole(late.at[which]))
        for t in range(count):
            face, f_out = edge[which, at(t)], side[F, which, at(t)]
            into, out_of = face, face
            if which == 0:
                out_of = out_of + time_step * own(F, 0)[t]
            else:
                into = into + time_step * f_out
            total = value[i, at(t)] + gains[which, t] + flow[t] - adjoint0[which, at(t)] * late[which, at(t)]
            into = into * (0.5 + f_out)
            known = 0.25 * out_of * b2_out[which, at(t)]
            write(2 + i, t, total + into * jnp.where(mine, known, known + on_p[at(t)]))
            write(which, t, term[which, at(t)] + hot0[which, at(t)] * gains[which, t])
            factors[which, t] = into
    for t in range(count):
        write(2 + half, t, jnp.where(core == 0, factors[0, t], factors[1, t]))
    for i in range(1, last):
        for t in range(count):
            total = value[i, at(t)]
            if i == 1:
                total = total + kx(0)[t] * late[0, at(t)]
            if i == last - 1:
                total = total + (kx(last - 1)[t] + time_step * own(F, last)[t]) * late[1, at(t)]
            write(2 + i, t, total)


def take(cross, along, cross_out, along_out):
    cross_out[...] = cross[...]
    along_out[...] = along[...]


def assemble(labels, keep, got, keep_inner, got_inner, cross, along, grad_state, grad_sink, masked, outer, sems):
    core = lax.axis_index("gz")
    count = grad_state.shape[0]
    half = count // 2
    sides = ((core, keep, keep_inner, cross), (1 - core, got, got_inner, along))
    copies = []

    def send(source, target):
        copies.append(pltpu.make_async_copy(source, target, sems.at[len(copies)]))
        copies[-1].start()

    for who, source, _, _ in sides:
        skip = 1 - who
        send(source.at[pl.ds(2 + skip, half - 1)], grad_state.at[pl.ds(who * half + skip, half - 1)])
    for slot, (who, source, inside, adjoint) in enumerate(sides):
        plane = who * (count - 1)
        outer[slot] = source[2 + who * (half - 1)] + source[2 + half] * adjoint[...]
        send(outer.at[slot], grad_state.at[plane])
        for i in range(half):
            term = source[0] if i == 0 else source[1] if i == half - 1 else inside[i - 1]
            masked[slot, i] = jnp.where(touching(labels[who * half + i]), term, 0.0)
        send(masked.at[slot], grad_sink.at[pl.ds(who * half, half)])
    for copy in copies:
        copy.wait()


def on_device(state, conduct, sink, labels, cotangent):
    count, ny, nz = state.shape
    half, wide, rows = count // 2, 2 * nz, ny + TILE
    count_x, count_y = lax.axis_size("gx"), lax.axis_size("gy")
    assert lax.axis_size("gz") == 2 and half >= 3 and ny % TILE == 0 and ny >= 3 * TILE
    two = count_y == 2
    ahead = [(i, (i + 1) % count_x) for i in range(count_x)]
    behind = [(b, a) for a, b in ahead]
    chips = [(2 * i + 1, (2 * i + 2) % (2 * count_x)) for i in range(count_x)]
    chips = chips + [(b, a) for a, b in chips]

    def swap_cores(x):
        return lax.ppermute(x, "gz", [(0, 1), (1, 0)])

    def swap_chips(x):
        return lax.ppermute(x, ("gx", "gz"), chips)

    def to_slabs(x):
        route = [(2 * i + c, 2 * ((i + 2 * c - 1) % count_x) + c) for i in range(count_x) for c in range(2)]
        return lax.ppermute(x, ("gx", "gz"), route)

    def along_y(rims):
        forward = [(i, (i + 1) % count_y) for i in range(count_y)]
        backward = [(b, a) for a, b in forward]
        routes = [forward] if two else [backward, forward]
        return [lax.ppermute(rim, "gy", routes[i % len(routes)]) for i, rim in enumerate(rims)]

    ways = 1 if two else 2
    inputs = (state, conduct, sink, labels, cotangent)
    plane, span = (4, ny, nz), (5, half + 2, ny, nz)
    kinds = pltpu.VMEM((half + 2, ny, nz), jnp.int32)
    drains = pltpu.VMEM((half + 2, ny, nz), jnp.float32)
    sems = lambda many: pltpu.SemaphoreType.DMA((many,))
    up, down, trade = call(
        pack_inputs, [plane, plane, span], *inputs, given=HBM,
        scratch=[kinds, drains, pltpu.VMEM((2, ny, nz), jnp.int32), sems(5), sems(8)],
    )
    up = lax.ppermute(up, "gx", ahead)
    down = lax.ppermute(down, "gx", behind)
    traded = swap_cores(trade)
    (mine,) = call(own_planes, [span], *inputs, given=HBM, scratch=[kinds, drains, sems(5)])
    block, near = call(gather_planes, [(5, half, ny, wide), (7, ny, wide)], mine, traded)
    sizes = [4, (5 * half + 1) // 2]
    rims = call(functools.partial(pack_along_y, two), [(n, TILE, wide) for n in sizes for _ in range(ways)], block, near)
    rims = along_y(rims)
    split = lambda r: [(half - 1, r, wide)] + [(half, r, wide)] * 5 + [(r, wide)]
    mids = call(functools.partial(prepare_mid, count_y), split(ny - 2 * TILE), block, near)
    ghost, near_ghost, *edges = call(
        functools.partial(prepare_rim, two, count_y),
        [(5, half, TILE, wide), (7, TILE, wide)] + split(3 * TILE), block, near, *rims,
    )
    off, _ = call(
        functools.partial(pack_off, two, count_y), [(ny + (len(PACKED) if two else 5) * TILE, wide), (7, TILE, wide)],
        block, mids[4], *rims[:ways], flops=PACK_FLOPS,
    )
    passed = call(choose_half, [(ny, nz)] * 4, up, down, *rims)
    passed = [swap_cores(x) for x in passed]
    off = swap_chips(off)
    own, outer = (half, rows, wide), (2, rows, wide)
    swept_shapes = [(4, 2, rows, wide), outer, outer, own, outer, outer, own, own, own, own, outer]
    assert len(swept_shapes) == SWEPT
    swept = call(middle, swept_shapes, block, ghost, near, near_ghost, up, down, *passed, *mids, *edges)
    ends, mains = (rows, wide), (ny, wide)
    *swept, hot2_out, sa_out, b2_out, off_b, on_b = call(
        functools.partial(outward, two), swept_shapes + [outer] * 3 + [ends] * 2, block, ghost, off, *mids, *edges, *swept,
        aliases={17 + i: i for i in range(SWEPT)},
    )
    side, edge, add, first, known, linear, adjoint, sa, b2, hot2, inward = swept
    off_b, on_b = swap_chips(off_b), swap_cores(on_b)
    fa_out, on_p, cross, along = call(
        outward_first, [outer, mains, (ny, nz), (ny, nz)],
        mids[1], mids[2], edges[1], edges[2], adjoint, inward, sa_out, b2_out,
    )
    on_p, cross, along = swap_cores(on_p), swap_chips(cross), to_slabs(along)
    main = lambda planes: (planes, ny, wide)
    planes = lambda many: (many, ny, nz)
    value, term, adjoint0, hot0, keep_inner, give_inner, _, _ = call(
        inner, [main(half), main(2), main(2), main(2), planes(half - 2), planes(half - 2), own, own],
        block, ghost, edge, side, first, adjoint, sa, b2, hot2, sa_out, b2_out, hot2_out, fa_out, *mids, *edges,
    )
    got_inner = swap_cores(give_inner)
    keep, give, _ = call(
        finish, [planes(half + 3), planes(half + 3), outer],
        block, ghost, edge, side, b2_out, value, term, adjoint0, hot0, off_b, on_b, on_p, *mids[:3], *edges[:3],
    )
    got = swap_cores(give)
    cross, along = call(take, [(ny, nz)] * 2, cross, along, flops=FLOPS)
    grad_state, grad_sink = call(
        assemble, [state.shape, state.shape], labels, keep, got, keep_inner, got_inner, cross, along, keep=False,
        scratch=[pltpu.VMEM((2, half, ny, nz), jnp.float32), pltpu.VMEM((2, ny, nz), jnp.float32), pltpu.SemaphoreType.DMA((6,))],
    )
    return (grad_state, grad_sink)


def solution(mesh):
    block = P(("groups", "gx"), "gy", "gz")
    in_specs = (block, P("gx", "gy", "gz"), block, block, block)
    return jax.shard_map(on_device, mesh=mesh, in_specs=in_specs, out_specs=(block, block), check_vma=False)
```

```python
import functools

import jax
import jax.numpy as jnp
from jax import lax
from jax.experimental import pallas as pl
from jax.experimental.pallas import tpu as pltpu
from jax.sharding import PartitionSpec as P

VMEM = pltpu.VMEM
HBM = pltpu.HBM
time_step = 0.06
scale = 0.5 * time_step
HALO = 4
TILE = 8
SWEPT = 11
LAST_FLOPS = 10000000000
PACK_FLOPS = 1100000000
FLOPS = 2200000000
S, C, T, F, K = range(5)
ONE = 4


def call(kernel, outs, *ins, keep=True, given=VMEM, scratch=(), flops=1024, aliases=None):
    space = VMEM if keep else jax.ShapeDtypeStruct
    block = pl.BlockSpec(memory_space=VMEM if given is VMEM else pl.ANY)
    return pl.pallas_call(
        kernel,
        out_shape=[space(shape, jnp.float32) for shape in outs],
        in_specs=[block] * len(ins),
        out_specs=[pl.BlockSpec(memory_space=VMEM if keep else pl.ANY)] * len(outs),
        scratch_shapes=list(scratch),
        input_output_aliases=aliases or {},
        compiler_params=pltpu.CompilerParams(vmem_limit_bytes=8 * 1024 * 1024),
        cost_estimate=pl.CostEstimate(flops=flops, bytes_accessed=1024, transcendentals=0),
    )(*[pltpu.with_memory_space_constraint(x, given) for x in ins])


def half_fluid(labels):
    return jnp.where(labels <= 1, 0.5, 0.0)


def touching(labels):
    return jnp.logical_or(labels == 1, labels == 2)


def rows_of(value):
    return lax.broadcasted_iota(jnp.int32, value.shape, 0)


def lanes_of(value):
    return lax.broadcasted_iota(jnp.int32, value.shape, 1)


def down_rows(before, here):
    return pltpu.roll(jnp.where(rows_of(here) == TILE - 1, before, here), 1, 0)


def up_rows(here, after):
    return pltpu.roll(jnp.where(rows_of(here) == 0, after, here), TILE - 1, 0)


def down_lanes(here):
    return pltpu.roll(here, 1, 1)


def up_lanes(here):
    return pltpu.roll(here, here.shape[1] - 1, 1)


def at(t):
    return slice(t * TILE, (t + 1) * TILE)


class Tiles:
    def __init__(self, *places):
        self.places = places

    def __getitem__(self, t):
        ref, slot = self.places[t % len(self.places)]
        return ref[at(slot)]

    def __setitem__(self, t, value):
        ref, slot = self.places[t]
        ref[at(slot)] = value

    def __len__(self):
        return len(self.places)


class Draft:
    def __init__(self, ref, values=None, prefix=()):
        self.ref, self.prefix = ref, prefix
        self.values = {} if values is None else values
        self.shape = ref.shape[len(prefix) :]

    @property
    def at(self):
        return _At(self)

    def _key(self, key):
        return self.prefix + (key if isinstance(key, tuple) else (key,))

    def __getitem__(self, key):
        key = self._key(key)
        name = key[:-1] + (key[-1].start,)
        return self.values[name][1] if name in self.values else self.ref[key]

    def __setitem__(self, key, value):
        key = self._key(key)
        self.values[key[:-1] + (key[-1].start,)] = (key, value)

    def flush(self):
        for key, value in self.values.values():
            self.ref[key] = value


class _At:
    def __init__(self, draft):
        self.draft = draft

    def __getitem__(self, key):
        return Draft(self.draft.ref, self.draft.values, self.draft._key(key))


def whole(ref):
    return Tiles(*[(ref, t) for t in range(ref.shape[0] // TILE)])


def with_ghost(main, ghost):
    return Tiles(*[(main, t) for t in range(main.shape[0] // TILE)], (ghost, 0))


def mid_and_rim(mid, rim):
    return Tiles((rim, 0), *[(mid, t) for t in range(mid.shape[0] // TILE)], (rim, 1), (rim, 2))


def put(ref, values):
    for t, value in enumerate(values):
        ref[at(t)] = value


class Across:
    def __init__(self, ky, kz, v):
        self.ky, self.kz, self.v = ky, kz, v
        self.known = {}

    def product(self, t):
        t = t % len(self.v)
        if t not in self.known:
            self.known[t] = self.ky[t] * self.v[t]
        return self.known[t]

    def __getitem__(self, t):
        here, kz = self.v[t], self.kz[t]
        along_y = self.ky[t] * down_rows(self.v[t - 1], here) + up_rows(self.product(t), self.product(t + 1))
        return along_y + (kz * down_lanes(here) + up_lanes(kz * here))


class Made:
    def __init__(self, values):
        self.values = values

    def __getitem__(self, t):
        return self.values[t % len(self.values)]

    def __len__(self):
        return len(self.values)


def sides_along_z(c, here):
    lanes = lanes_of(c)
    left = here + jnp.where(lanes == 0, 0.0, down_lanes(c)) * scale
    right = here + jnp.where(lanes == lanes.shape[1] - 1, 0.0, up_lanes(c)) * scale
    return left, right


def load_all(pairs, sems):
    copies = [pltpu.make_async_copy(a, b, sems.at[i]) for i, (a, b) in enumerate(pairs)]
    for copy in copies:
        copy.start()
    return copies


def load_planes(inputs, start, out, kinds, drains, sems):
    state, conduct, sink, labels, cotangent = inputs
    part = pl.ds(start, out.shape[1])
    pairs = [(labels.at[part], kinds), (sink.at[part], drains), (state.at[part], out.at[S])]
    return load_all(pairs + [(conduct.at[part], out.at[C]), (cotangent.at[part], out.at[T])], sems)


def fill_planes(out, kinds, drains):
    for i in range(out.shape[1]):
        out[F, i] = half_fluid(kinds[i])
        out[K, i] = jnp.where(touching(kinds[i]), drains[i], 0.0)


def pack_inputs(state, conduct, sink, labels, cotangent, up, down, trade, kinds, drains, ends, sems, plane_sems):
    count = state.shape[0]
    pairs = []
    for which, (out, plane) in enumerate(((up, count - 1), (down, 0))):
        pairs += [(state.at[plane], out.at[S]), (conduct.at[plane], out.at[C]), (cotangent.at[plane], out.at[T])]
        pairs += [(labels.at[plane], ends.at[which])]
    copies = load_all(pairs, plane_sems)
    start = (1 - lax.axis_index("gz")) * (count - trade.shape[1])
    copies += load_planes((state, conduct, sink, labels, cotangent), start, trade, kinds, drains, sems)
    for copy in copies:
        copy.wait()
    up[F] = half_fluid(ends[0])
    down[F] = half_fluid(ends[1])
    fill_planes(trade, kinds, drains)


def own_planes(state, conduct, sink, labels, cotangent, mine, kinds, drains, sems):
    start = lax.axis_index("gz") * (state.shape[0] - mine.shape[1])
    for copy in load_planes((state, conduct, sink, labels, cotangent), start, mine, kinds, drains, sems):
        copy.wait()
    fill_planes(mine, kinds, drains)


def pack_rims(two, planes, outs):
    for k in range(0, len(planes), 2):
        even, odd = planes[k], planes[min(k + 1, len(planes) - 1)]
        ny = even.shape[0]
        low_even, high_even = even[0:TILE], even[ny - TILE : ny]
        low_odd, high_odd = odd[0:TILE], odd[ny - TILE : ny]
        upper = rows_of(low_even) < HALO
        low = jnp.where(upper, low_even, pltpu.roll(low_odd, HALO, 0))
        high = jnp.where(upper, pltpu.roll(high_even, HALO, 0), high_odd)
        if two:
            outs[0][k // 2] = jnp.where(lax.axis_index("gy") == 0, high, low)
        else:
            outs[0][k // 2] = low
            outs[1][k // 2] = high


def unpack_rims(two, count_y, rims, planes):
    place = lax.axis_index("gy")
    for k in range(0, len(planes), 2):
        above = jnp.where(place < count_y - 1, rims[0][k // 2], 0.0)
        below = jnp.where(place > 0, rims[0 if two else 1][k // 2], 0.0)
        upper = rows_of(above) < HALO
        planes[k][...] = jnp.where(upper, above, pltpu.roll(below, HALO, 0))
        if k + 1 < len(planes):
            planes[k + 1][...] = jnp.where(upper, pltpu.roll(above, HALO, 0), below)


def gather_planes(mine, traded, block, near):
    core = lax.axis_index("gz")
    half, narrow = block.shape[1], mine.shape[3]
    own = pl.ds(pl.multiple_of(core * narrow, 128), narrow)
    other = pl.ds(pl.multiple_of((1 - core) * narrow, 128), narrow)
    start = 2 * core
    beside = (1 - core) * half + core
    beyond = (1 - core) * (half + 1)
    for j in range(5):
        for i in range(half):
            block[j, i, :, own] = mine[j, start + i]
            block[j, i, :, other] = traded[j, start + i]
        near[j, :, own] = mine[j, beside]
        near[j, :, other] = traded[j, beside]
        if j in (S, C):
            near[5 + j, :, own] = mine[j, beyond]
            near[5 + j, :, other] = traded[j, beyond]


def rim_planes(block, near):
    half = block.shape[1]
    core = lax.axis_index("gz")
    inward = lambda i: core * (half - 1) + i * (1 - 2 * core)
    early = [block.at[j, inward(0)] for j in range(5)] + [block.at[j, inward(1)] for j in (S, C)]
    late = [block.at[j, inward(1)] for j in (T, F, K)] + [block.at[j, inward(i)] for i in range(2, half) for j in range(5)]
    return early, late + [near.at[j] for j in range(7)]


def pack_along_y(two, block, near, *rims):
    early, late = rim_planes(block, near)
    ways = 1 if two else 2
    pack_rims(two, early, rims[:ways])
    pack_rims(two, late, rims[ways:])


class Lazy:
    def __init__(self, count, make):
        self.count, self.make, self.known = count, make, {}

    def __getitem__(self, t):
        t = t % self.count
        if t not in self.known:
            self.known[t] = self.make(t)
        return self.known[t]

    def __len__(self):
        return self.count


def prepare(todo, count_y, block, near, ghost, near_ghost, kx, ky_out, kz_out, diag, part, back, one):
    place = lax.axis_index("gy")
    core = lax.axis_index("gz")
    half, ny = block.shape[1], block.shape[2]
    count, last = ny // TILE + 1, half - 1

    def own(j, i):
        if ghost is None:
            return Tiles(*[(block.at[j, i], t) for t in range(count - 1)], (None, 0))
        return with_ghost(block.at[j, i], ghost.at[j, i])

    def next_to(j):
        if ghost is None:
            return Tiles(*[(near.at[j], t) for t in range(count - 1)], (None, 0))
        return with_ghost(near.at[j], near_ghost.at[j])

    def faces_along_y(c):
        def make(t):
            value = (c[t] + down_rows(c[t - 1], c[t])) * scale
            if t == 0:
                value = jnp.where(jnp.logical_and(rows_of(value) == 0, place == 0), 0.0, value)
            if t == count - 1:
                value = jnp.where(jnp.logical_and(rows_of(value) == 0, place == count_y - 1), 0.0, value)
            return value

        return Lazy(count, make)

    def own_weight(c, f, t):
        here = c[t] * scale
        left, right = sides_along_z(c[t], here)
        low, high = down_rows(c[t - 1], c[t]), up_rows(c[t], c[t + 1])
        return left, (2.0 * here + (low + high) * scale) + (left + right) + time_step * f[t]

    for i in range(half):
        s, c, a, f, k = (own(j, i) for j in (S, C, T, F, K))
        ky, kz = faces_along_y(c), {}
        for t in todo:
            left, weight = own_weight(c, f, t)
            kz[t] = jnp.where(lanes_of(left) == 0, 0.0, left)
            slot = at(todo.index(t))
            if i > 0:
                face = (c[t] + own(C, i - 1)[t]) * scale
                kx[i - 1, slot] = face
                weight = weight + face
            if i < last:
                weight = weight + (c[t] + own(C, i + 1)[t]) * scale
            diag[i, slot] = weight
            ky_out[i, slot] = ky[t]
            kz_out[i, slot] = kz[t]
        scaled = Lazy(count, lambda t, a=a, f=f: a[t] * (0.5 + f[t]))
        ahead = Across(ky, kz, s)
        behind = Across(ky, kz, scaled)
        for t in todo:
            slot = at(todo.index(t))
            d, b = diag[i, slot], scaled[t]
            go = ahead[t] - d * s[t] - time_step * k[t] * jnp.tanh(s[t])
            come = behind[t] - d * b
            if i > 0:
                go = go + (kx[i - 1, slot] + time_step * f[t]) * own(S, i - 1)[t]
                come = come + kx[i - 1, slot] * (own(T, i - 1)[t] * (0.5 + own(F, i - 1)[t]))
            if i < last:
                face, high_f = (c[t] + own(C, i + 1)[t]) * scale, own(F, i + 1)[t]
                go = go + face * own(S, i + 1)[t]
                come = come + (face + time_step * high_f) * (own(T, i + 1)[t] * (0.5 + high_f))
            part[i, slot] = s[t] + (0.5 + f[t]) * go
            back[i, slot] = a[t] + come
    s, c, f, k = (next_to(j) for j in (S, C, F, K))
    kz = {}
    for t in todo:
        left, _ = own_weight(c, f, t)
        kz[t] = jnp.where(lanes_of(left) == 0, 0.0, left)
    ahead = Across(faces_along_y(c), kz, s)
    is_low = core == 0
    for t in todo:
        _, weight = own_weight(c, f, t)
        c_own = jnp.where(is_low, own(C, last)[t], own(C, 0)[t])
        s_own = jnp.where(is_low, own(S, last)[t], own(S, 0)[t])
        face_own, face_far = (c[t] + c_own) * scale, (c[t] + next_to(5 + C)[t]) * scale
        wind = time_step * f[t]
        go = ahead[t] - (weight + face_own + face_far) * s[t] - time_step * k[t] * jnp.tanh(s[t])
        go = go + (face_own + jnp.where(is_low, wind, 0.0)) * s_own
        go = go + (face_far + jnp.where(is_low, 0.0, wind)) * next_to(5 + S)[t]
        one[at(todo.index(t))] = s[t] + (0.5 + f[t]) * go


def prepare_mid(count_y, block, near, *outs):
    prepare(list(range(1, block.shape[2] // TILE - 1)), count_y, block, near, None, None, *outs)


def prepare_rim(two, count_y, block, near, *refs):
    ways = 1 if two else 2
    rims, (ghost, near_ghost, *outs) = refs[: 2 * ways], refs[2 * ways :]
    count = block.shape[2] // TILE
    early, late = rim_planes(ghost, near_ghost)
    unpack_rims(two, count_y, rims[:ways], early)
    unpack_rims(two, count_y, rims[ways:], late)
    prepare([0, count - 1, count], count_y, block, near, ghost, near_ghost, *outs)


PACKED = (((S, 3), (C, 3), (ONE, 2)), ((T, 2), (F, 2)))


def pack_ghosts(place, parts, ghosts):
    rows = rows_of(ghosts[S])
    low = high = jnp.zeros_like(ghosts[S])
    taken = 0
    for j, depth in parts:
        span = jnp.logical_and(rows >= taken, rows < taken + depth)
        low = jnp.where(span, pltpu.roll(ghosts[j], taken, 0) if taken else ghosts[j], low)
        span = jnp.logical_and(rows >= TILE - taken - depth, rows < TILE - taken)
        high = jnp.where(span, pltpu.roll(ghosts[j], TILE - taken, 0) if taken else ghosts[j], high)
        taken += depth
    return jnp.where(place == 0, low, high)


def unpack_ghosts(place, parts, packed):
    rows = rows_of(packed)
    ghosts, taken = {}, 0
    for j, depth in parts:
        low = pltpu.roll(packed, TILE - taken, 0) if taken else packed
        high = pltpu.roll(packed, taken, 0) if taken else packed
        low = jnp.where(rows < depth, low, 0.0)
        high = jnp.where(rows >= TILE - depth, high, 0.0)
        ghosts[j] = jnp.where(place == 0, low, high)
        taken += depth
    return ghosts


def pack_off(two, count_y, block, part_mid, *refs):
    ways = 1 if two else 2
    rims, (off, ghost) = refs[:ways], refs[ways:]
    place = lax.axis_index("gy")
    core = lax.axis_index("gz")
    last = block.shape[1] - 1
    outer = core * last
    inside = outer + 1 - 2 * core
    unpack_rims(two, count_y, rims, [ghost.at[j] for j in range(7)])
    s, c, f, k = (with_ghost(block.at[j, outer], ghost.at[j]) for j in (S, C, F, K))
    s_in, c_in = (with_ghost(block.at[j, inside], ghost.at[5 + j]) for j in (S, C))
    count = len(s)

    def face_along_y(t):
        value = (c[t] + down_rows(c[t - 1], c[t])) * scale
        if t == 0:
            value = jnp.where(jnp.logical_and(rows_of(value) == 0, place == 0), 0.0, value)
        if t == count - 1:
            value = jnp.where(jnp.logical_and(rows_of(value) == 0, place == count_y - 1), 0.0, value)
        return value

    todo, kz, weight = (0, count - 2, count - 1), {}, {}
    for t in todo:
        here = c[t] * scale
        left, right = sides_along_z(c[t], here)
        kz[t] = jnp.where(lanes_of(left) == 0, 0.0, left)
        low, high = down_rows(c[t - 1], c[t]), up_rows(c[t], c[t + 1])
        weight[t] = (2.0 * here + (low + high) * scale) + (left + right) + time_step * f[t]
    flow = Across(Lazy(count, face_along_y), kz, s)
    one = {}
    for t in range(count):
        if t in todo:
            face = (c[t] + c_in[t]) * scale
            go = flow[t] - (weight[t] + face) * s[t] - time_step * k[t] * jnp.tanh(s[t])
            go = go + (face + jnp.where(core == 0, 0.0, time_step) * f[t]) * s_in[t]
            one[t] = s[t] + (0.5 + f[t]) * go
        else:
            one[t] = part_mid[outer, at(t - 1)]
        if t < count - 1:
            off[at(t)] = one[t]
    ghosts = {j: ghost[j] for j in range(4)}
    ghosts[ONE] = one[count - 1]
    if two:
        for slot, parts in enumerate(PACKED):
            off[at(count - 1 + slot)] = pack_ghosts(place, parts, ghosts)
    else:
        for j in range(5):
            off[at(count - 1 + j)] = ghosts[j]


def choose_half(up, down, *refs):
    for j in range(4):
        refs[j // 2 - 2][j % 2] = jnp.where(lax.axis_index("gz") == 0, down[j], up[j])


def coefficients(refs):
    mids, rims = refs[:6], refs[7:13]
    return [lambda i, m=m, r=r: mid_and_rim(m.at[i], r.at[i]) for m, r in zip(mids, rims)]


def fill_sides(near, near_ghost, up, down, passed, side):
    core = lax.axis_index("gz")
    ny, narrow = up.shape[1], up.shape[2]
    outside, inside = core, 1 - core
    for j in range(4):
        side[j, outside, 0:ny, 0:narrow] = jnp.where(core == 0, up[j], passed[j // 2][j % 2])
        side[j, outside, 0:ny, narrow : 2 * narrow] = jnp.where(core == 0, passed[j // 2][j % 2], down[j])
        side[j, inside, 0:ny] = near[j]
        side[j, inside, ny : ny + TILE] = near_ghost[j]


def fill_side_ghosts(two, ny, off, side):
    place, outside = lax.axis_index("gy"), lax.axis_index("gz")
    first = ny // TILE
    if two:
        ghosts = {}
        for slot, parts in enumerate(PACKED):
            ghosts.update(unpack_ghosts(place, parts, off[at(first + slot)]))
    else:
        ghosts = {j: off[at(first + j)] for j in range(5)}
    for j in range(4):
        for which in range(2):
            place = (j, which, slice(ny, ny + TILE))
            side[place] = jnp.where(outside == which, ghosts[j], side[place])
    return ghosts[ONE]


def sweep(late, block, ghost, weights, side, edge, add, first, known, linear, adjoint, sa, b2, hot2, inward):
    kx, ky, kz, diag, part, back = weights
    half, ny = block.shape[1], block.shape[2]
    count, last = ny // TILE, half - 1
    own = lambda j, i: with_ghost(block.at[j, i], ghost.at[j, i])
    for which, i in ((0, 0), (1, last)):
        s, f, c = own(S, i), own(F, i), own(C, i)
        s_out, c_out, f_out = (whole(side.at[j, which]) for j in (S, C, F))
        for t in [count] if late else range(count):
            face = (c[t] + c_out[t]) * scale
            edge[which, at(t)] = face
            v, beyond = s[t], s_out[t]
            if which == 0:
                inner_add = (face + time_step * f[t]) * beyond - face * v
                outer_add = face * (v - beyond)
            else:
                inner_add = face * (beyond - v)
                outer_add = (face + time_step * f_out[t]) * v - face * beyond
            first[i, at(t)] = part(i)[t] + (0.5 + f[t]) * inner_add
            add[which, at(t)] = (0.5 + f_out[t]) * outer_add
    for i in range(1, last):
        for t in [] if late else range(count + 1):
            first[i, at(t)] = part(i)[t]
    for i in range(half):
        outer = i in (0, last)
        v, f, k, s, a = whole(first.at[i]), own(F, i), own(K, i), own(S, i), own(T, i)
        flow = Across(ky(i), kz(i), v)
        if outer:
            todo = [0, count - 1, count] if late else range(1, count - 1)
        else:
            todo = [count] if late else range(count)
        for t in todo:
            rc = 0.5 + f[t]
            sink = time_step * k[t]
            hot1 = jnp.tanh(v[t])
            full = diag(i)[t]
            if i == 0:
                full = full + edge[0, at(t)]
            if i == last:
                full = full + edge[1, at(t)]
            adjoint[i, at(t)] = full + sink * (1.0 - hot1 * hot1)
            rate = flow[t] - full * v[t] - sink * hot1
            if i > 0:
                rate = rate + (kx(i - 1)[t] + time_step * f[t]) * first[i - 1, at(t)]
            if i < last:
                rate = rate + kx(i)[t] * first[i + 1, at(t)]
            value = 0.75 * s[t] + 0.25 * (v[t] + rc * rate)
            b = a[t] * rc
            total = back(i)[t]
            if i == 0:
                total = total + edge[0, at(t)] * (side[T, 0, at(t)] * (0.5 + side[F, 0, at(t)]) - b)
            if i == last:
                high, high_f = edge[1, at(t)], side[F, 1, at(t)]
                total = total + ((high + time_step * high_f) * (side[T, 1, at(t)] * (0.5 + high_f)) - high * b)
            if outer:
                which = 0 if i == 0 else 1
                known[which, at(t)] = value
                linear[which, at(t)] = total
            else:
                hot = jnp.tanh(value)
                hot2[i, at(t)] = hot
                total = (2.0 / 3.0) * (total - sink * (1.0 - hot * hot) * b)
                sa[i, at(t)] = total
                b2[i, at(t)] = total * rc
    for t in [count] if late else range(count):
        inward[0, at(t)] = (kx(0)[t] + time_step * own(F, 1)[t]) * b2[1, at(t)]
        inward[1, at(t)] = kx(last - 1)[t] * b2[last - 1, at(t)]


def middle(block, ghost, near, near_ghost, up, down, *refs):
    passed, weights, outs = refs[:2], coefficients(refs[2:16]), refs[16:]
    fill_sides(near, near_ghost, up, down, passed, outs[0])
    sweep(False, block, ghost, weights, *outs)


def outward(two, block, ghost, off, *refs):
    weights, one_mid, one_rim = coefficients(refs[:14]), refs[6], refs[13]
    outs = [Draft(ref) for ref in refs[14 + SWEPT : 14 + 2 * SWEPT]]
    *ends, off_b = refs[14 + 2 * SWEPT :]
    hot2, sa, b2 = (Draft(ref) for ref in ends)
    side, edge, add, _, known, linear, *_ = outs
    core = lax.axis_index("gz")
    half, ny = block.shape[1], block.shape[2]
    count, last = ny // TILE, half - 1
    own = lambda j, i: with_ghost(block.at[j, i], ghost.at[j, i])
    one_ghost = fill_side_ghosts(two, ny, off, side)
    sweep(True, block, ghost, weights, *outs)
    for which, i in ((0, 0), (1, last)):
        f, k, a = own(F, i), own(K, i), own(T, i)
        mine = core == which
        for t in range(count + 1):
            one = off[at(t)] if t < count else one_ghost
            one = jnp.where(mine, one + add[which, at(t)], mid_and_rim(one_mid, one_rim)[t])
            face = edge[which, at(t)]
            if which == 0:
                face = face + time_step * f[t]
            rc = 0.5 + f[t]
            hot = jnp.tanh(known[which, at(t)] + 0.25 * rc * face * one)
            total = (2.0 / 3.0) * (linear[which, at(t)] - time_step * k[t] * (1.0 - hot * hot) * (a[t] * rc))
            hot2[which, at(t)] = hot
            sa[which, at(t)] = total
            b2[which, at(t)] = total * rc
    for t in range(count + 1):
        off_b[at(t)] = jnp.where(core == 0, b2[0, at(t)], b2[1, at(t)])
    for draft in (b2, sa, hot2, *outs):
        draft.flush()


def inside_adjoint(block, ghost, near, near_ghost, *refs):
    (kx, ky, kz, diag, part, back), on_b = coefficients(refs[:14]), refs[14]
    core = lax.axis_index("gz")
    half, ny = block.shape[1], block.shape[2]
    last = half - 1
    i = (1 - core) * last
    beside = i - 1 + 2 * core
    own = lambda j, plane: with_ghost(block.at[j, plane], ghost.at[j, plane])
    c_h, s_h, t_h, f_h = (with_ghost(near.at[j], near_ghost.at[j]) for j in (C, S, T, F))
    one = mid_and_rim(refs[6], refs[13])
    s, c, a, f, k = (own(j, i) for j in (S, C, T, F, K))
    above, below = jnp.where(core == 0, time_step, 0.0), jnp.where(core == 0, 0.0, time_step)
    step, next_first = kx((1 - core) * (last - 1)), part(beside)
    faces, first = [], []
    for t in range(ny // TILE + 1):
        faces.append((c[t] + c_h[t]) * scale)
        first.append(part(i)[t] + (0.5 + f[t]) * ((faces[t] + below * f[t]) * s_h[t] - faces[t] * s[t]))
    flow = Across(ky(i), kz(i), Made(first))
    out = []
    for t in range(ny // TILE + 1):
        rc, sink, face = 0.5 + f[t], time_step * k[t], faces[t]
        rate = flow[t] - (diag(i)[t] + face) * first[t] - sink * jnp.tanh(first[t])
        rate = rate + (step[t] + above * f[t]) * next_first[t] + (face + below * f[t]) * one[t]
        hot = jnp.tanh(0.75 * s[t] + 0.25 * (first[t] + rc * rate))
        b = a[t] * rc
        total = back(i)[t] + (face + above * f_h[t]) * (t_h[t] * (0.5 + f_h[t])) - face * b
        out.append((2.0 / 3.0) * (total - sink * (1.0 - hot * hot) * b) * rc)
    put(on_b, out)


def outward_first(ky_mid, kz_mid, ky_rim, kz_rim, adjoint, inward, sa, b2, fa, along, cross):
    core = lax.axis_index("gz")
    half, ny = adjoint.shape[0], along.shape[0]
    values = []
    for which, i in ((0, 0), (1, half - 1)):
        b = whole(b2.at[which])
        flow = Across(mid_and_rim(ky_mid.at[i], ky_rim.at[i]), mid_and_rim(kz_mid.at[i], kz_rim.at[i]), b)
        total = lambda t: sa[which, at(t)] + flow[t] - adjoint[i, at(t)] * b[t] + inward[which, at(t)]
        values.append([0.25 * total(t) for t in range(len(b))])
    low, high = values
    for t in range(ny // TILE):
        along[at(t)], cross[at(t)] = halves(core, jnp.where(core == 0, low[t], high[t]))
    for which in range(2):
        put(fa.at[which], values[which])


def inner(block, ghost, edge, side, first, adjoint, sa_in, b2_in, hot2_in, sa_out, b2_out, hot2_out, fa_out, *refs):
    kx, ky, kz, diag, _, _ = coefficients(refs[:14])
    value, term, adjoint0, hot0, fa, b3 = refs[14:]
    half, ny = block.shape[1], block.shape[2]
    count, last = ny // TILE, half - 1
    own = lambda j, i: with_ghost(block.at[j, i], ghost.at[j, i])
    pick = lambda i, inside, outside: inside.at[i] if 0 < i < last else outside.at[0 if i == 0 else 1]
    sa = lambda i: whole(pick(i, sa_in, sa_out))
    b2 = lambda i: whole(pick(i, b2_in, b2_out))
    hot2 = lambda i: whole(pick(i, hot2_in, hot2_out))
    for i in range(half):
        f = own(F, i)
        flow = Across(ky(i), kz(i), b2(i))
        for t in range(count + 1):
            if 0 < i < last:
                total = sa(i)[t] + flow[t] - adjoint[i, at(t)] * b2(i)[t]
                total = total + kx(i - 1)[t] * b2(i - 1)[t] + (kx(i)[t] + time_step * own(F, i + 1)[t]) * b2(i + 1)[t]
                total = 0.25 * total
            else:
                total = fa_out[0 if i == 0 else 1, at(t)]
            fa[i, at(t)] = total
            b3[i, at(t)] = total * (0.5 + f[t])
    for i in range(half):
        s, f, k, a = own(S, i), own(F, i), own(K, i), own(T, i)
        b = whole(b3.at[i])
        flow = Across(ky(i), kz(i), b)
        for t in range(count):
            hot = jnp.tanh(s[t])
            full = diag(i)[t]
            if i == 0:
                full = full + edge[0, at(t)]
            if i == last:
                full = full + edge[1, at(t)]
            full = full + time_step * k[t] * (1.0 - hot * hot)
            total = flow[t] - full * b[t] + fa[i, at(t)] + 0.75 * sa(i)[t] + a[t] * (1.0 / 3.0)
            if i > 0:
                total = total + kx(i - 1)[t] * b3[i - 1, at(t)]
            if i < last:
                total = total + (kx(i)[t] + time_step * own(F, i + 1)[t]) * b3[i + 1, at(t)]
            value[i, at(t)] = total
            first_hot = jnp.tanh(first[i, at(t)])
            total = (2.0 / 3.0) * hot2(i)[t] * a[t] + 0.25 * first_hot * sa(i)[t] + hot * fa[i, at(t)]
            term[i, at(t)] = -time_step * (0.5 + f[t]) * total
            if i == 0 or i == last:
                which = 0 if i == 0 else 1
                adjoint0[which, at(t)] = full
                hot0[which, at(t)] = -time_step * (0.5 + f[t]) * hot


def halves(core, value):
    narrow = value.shape[1] // 2
    left, right = value[:, :narrow], value[:, narrow:]
    return jnp.where(core == 0, left, right), jnp.where(core == 0, right, left)


def from_beyond(which, message, block, ghost, edge, side, b2_out, value, term, adjoint0, hot0, weights):
    kx, ky, kz = weights
    half, ny = block.shape[1], block.shape[2]
    count, last = ny // TILE, half - 1
    i = which * last
    beside = i + 1 - 2 * which
    wind = jnp.where(which == 1, time_step, 0.0)
    against = time_step - wind
    f = with_ghost(block.at[F, i], ghost.at[F, i])
    into, gains, late = [], [], []
    for t in range(count + 1):
        into.append(edge[which, at(t)] + wind * side[F, which, at(t)])
        gains.append(0.25 * into[t] * message[at(t)])
        late.append(gains[t] * (0.5 + f[t]))
    flow = Across(ky(i), kz(i), Made(late))
    step = kx(which * (last - 1))
    out = []
    for t in range(count):
        factor = into[t] * (0.5 + side[F, which, at(t)])
        known = 0.25 * (edge[which, at(t)] + against * f[t]) * b2_out[which, at(t)]
        total = value[i, at(t)] + gains[t] + flow[t] - adjoint0[which, at(t)] * late[t] + factor * known
        next_total = value[beside, at(t)] + (step[t] + wind * f[t]) * late[t]
        out.append((t, total, next_total, term[i, at(t)] + hot0[which, at(t)] * gains[t], factor))
    return out


def three(refs):
    return [lambda i, m=m, r=r: mid_and_rim(m.at[i], r.at[i]) for m, r in zip(refs[:3], refs[3:])]


def finish_inside(block, ghost, edge, side, b2_out, value, term, adjoint0, hot0, on_b, *refs):
    *six, keep, give = refs
    core = lax.axis_index("gz")
    half, ny = block.shape[1], block.shape[2]
    plane = lambda r: core * (half - 1) + r * (1 - 2 * core)

    def write(place, t, value):
        keep[place, at(t)], give[place, at(t)] = halves(core, value)

    parts = from_beyond(1 - core, on_b, block, ghost, edge, side, b2_out, value, term, adjoint0, hot0, three(six))
    for t, total, next_total, sink, factor in parts:
        write(half - 3, t, total)
        write(half - 4, t, next_total)
        write(2 * half - 4, t, sink)
        write(2 * half - 2, t, factor)
        for r in range(2, half - 2):
            write(r - 2, t, value[plane(r), at(t)])
        for r in range(1, half - 1):
            write(half - 3 + r, t, term[plane(r), at(t)])
        wind = jnp.where(core == 1, time_step, 0.0)
        f_out = side[F, core, at(t)]
        write(2 * half - 3, t, (edge[core, at(t)] + wind * f_out) * (0.5 + f_out))


def finish_outside(block, ghost, edge, side, b2_out, value, term, adjoint0, hot0, off_b, *refs):
    *six, fa_out, _, keep, give = refs
    core = lax.axis_index("gz")
    parts = from_beyond(core, off_b, block, ghost, edge, side, b2_out, value, term, adjoint0, hot0, three(six))
    for t, total, next_total, sink, _ in parts:
        for place, value_here in enumerate((total, next_total, sink, fa_out[1 - core, at(t)])):
            keep[place, at(t)], give[place, at(t)] = halves(core, value_here)


def take(cross, along, cross_out, along_out):
    cross_out[...] = cross[...]
    along_out[...] = along[...]


def assemble(labels, keep, got, keep_last, got_last, along, cross, grad_state, grad_sink, *refs):
    masked, ends, sems = refs
    core = lax.axis_index("gz")
    count = grad_state.shape[0]
    half = count // 2
    copies = []

    def send(source, target):
        copies.append(pltpu.make_async_copy(source, target, sems.at[len(copies)]))
        copies[-1].start()

    sides = ((core, keep, keep_last, got_last.at[3], cross), (1 - core, got, got_last, keep_last.at[3], along))
    plane = lambda who, r: who * (count - 1) + r * (1 - 2 * who)
    for who, most, outermost, _, _ in sides:
        send(outermost.at[1], grad_state.at[plane(who, 1)])
        for r in range(2, half - 1):
            send(most.at[r - 2], grad_state.at[plane(who, r)])
    for slot, (who, most, outermost, inside, outside) in enumerate(sides):
        ends[slot, 0] = outermost[0] + most[2 * half - 3] * outside[...]
        send(ends.at[slot, 0], grad_state.at[plane(who, 0)])
        ends[slot, 1] = most[half - 3] + most[2 * half - 2] * inside[...]
        send(ends.at[slot, 1], grad_state.at[plane(who, half - 1)])
        for r in range(half):
            term = outermost[2] if r == 0 else most[half - 3 + r]
            place = plane(who, r)
            masked[slot, place - who * half] = jnp.where(touching(labels[place]), term, 0.0)
        send(masked.at[slot], grad_sink.at[pl.ds(who * half, half)])
    for copy in copies:
        copy.wait()


def on_device(state, conduct, sink, labels, cotangent):
    count, ny, nz = state.shape
    half, wide, rows = count // 2, 2 * nz, ny + TILE
    count_x, count_y = lax.axis_size("gx"), lax.axis_size("gy")
    assert lax.axis_size("gz") == 2 and half >= 4 and ny % TILE == 0 and ny >= 3 * TILE
    two = count_y == 2
    ahead = [(i, (i + 1) % count_x) for i in range(count_x)]
    behind = [(b, a) for a, b in ahead]
    chips = [(2 * i + 1, (2 * i + 2) % (2 * count_x)) for i in range(count_x)]
    chips = chips + [(b, a) for a, b in chips]

    def swap_cores(x):
        return lax.ppermute(x, "gz", [(0, 1), (1, 0)])

    def swap_chips(x):
        return lax.ppermute(x, ("gx", "gz"), chips)

    def to_slabs(x):
        route = [(2 * i + c, 2 * ((i + 2 * c - 1) % count_x) + c) for i in range(count_x) for c in range(2)]
        return lax.ppermute(x, ("gx", "gz"), route)

    def along_y(rims):
        forward = [(i, (i + 1) % count_y) for i in range(count_y)]
        backward = [(b, a) for a, b in forward]
        routes = [forward] if two else [backward, forward]
        return [lax.ppermute(rim, "gy", routes[i % len(routes)]) for i, rim in enumerate(rims)]

    ways = 1 if two else 2
    inputs = (state, conduct, sink, labels, cotangent)
    plane, span = (4, ny, nz), (5, half + 2, ny, nz)
    kinds = pltpu.VMEM((half + 2, ny, nz), jnp.int32)
    drains = pltpu.VMEM((half + 2, ny, nz), jnp.float32)
    sems = lambda many: pltpu.SemaphoreType.DMA((many,))
    up, down, trade = call(
        pack_inputs, [plane, plane, span], *inputs, given=HBM,
        scratch=[kinds, drains, pltpu.VMEM((2, ny, nz), jnp.int32), sems(5), sems(8)],
    )
    up = lax.ppermute(up, "gx", ahead)
    down = lax.ppermute(down, "gx", behind)
    traded = swap_cores(trade)
    (mine,) = call(own_planes, [span], *inputs, given=HBM, scratch=[kinds, drains, sems(5)])
    block, near = call(gather_planes, [(5, half, ny, wide), (7, ny, wide)], mine, traded)
    sizes = [4, (5 * half + 1) // 2]
    rims = call(functools.partial(pack_along_y, two), [(n, TILE, wide) for n in sizes for _ in range(ways)], block, near)
    rims = along_y(rims)
    split = lambda r: [(half - 1, r, wide)] + [(half, r, wide)] * 5 + [(r, wide)]
    mids = call(functools.partial(prepare_mid, count_y), split(ny - 2 * TILE), block, near)
    ghost, near_ghost, *edges = call(
        functools.partial(prepare_rim, two, count_y),
        [(5, half, TILE, wide), (7, TILE, wide)] + split(3 * TILE), block, near, *rims,
    )
    off, _ = call(
        functools.partial(pack_off, two, count_y), [(ny + (len(PACKED) if two else 5) * TILE, wide), (7, TILE, wide)],
        block, mids[4], *rims[:ways], flops=PACK_FLOPS,
    )
    off = swap_chips(off)
    own, outer = (half, rows, wide), (2, rows, wide)
    (on_b,) = call(inside_adjoint, [(rows, wide)], block, ghost, near, near_ghost, *mids, *edges)
    passed = [swap_cores(x) for x in call(choose_half, [(2, ny, nz)] * 2, up, down, on_b)]
    on_b = swap_cores(on_b)
    swept_shapes = [(4, 2, rows, wide), outer, outer, own, outer, outer, own, own, own, own, outer]
    assert len(swept_shapes) == SWEPT
    swept = call(middle, swept_shapes, block, ghost, near, near_ghost, up, down, *passed, *mids, *edges)
    ends, mains = (rows, wide), (ny, wide)
    *swept, hot2_out, sa_out, b2_out, off_b = call(
        functools.partial(outward, two), swept_shapes + [outer] * 3 + [ends], block, ghost, off, *mids, *edges, *swept,
        aliases={17 + i: i for i in range(SWEPT)},
    )
    side, edge, add, first, known, linear, adjoint, sa, b2, hot2, inward = swept
    off_b = swap_chips(off_b)
    half_plane = (ny, nz)
    fa_out, along, cross = call(
        outward_first, [outer] + [half_plane] * 2,
        mids[1], mids[2], edges[1], edges[2], adjoint, inward, sa_out, b2_out,
    )
    cross, along = swap_chips(cross), to_slabs(along)
    main = lambda planes: (planes, ny, wide)
    planes = lambda many: (many, ny, nz)
    value, term, adjoint0, hot0, _, _ = call(
        inner, [main(half), main(half), main(2), main(2), own, own],
        block, ghost, edge, side, first, adjoint, sa, b2, hot2, sa_out, b2_out, hot2_out, fa_out, *mids, *edges,
    )
    ready = (block, ghost, edge, side, b2_out, value, term, adjoint0, hot0)
    keep, give = call(finish_inside, [planes(2 * half - 1)] * 2, *ready, on_b, *mids[:3], *edges[:3])
    got = swap_cores(give)
    keep_last, give_last = call(finish_outside, [planes(4)] * 2, *ready, off_b, *mids[:3], *edges[:3], fa_out, keep, flops=LAST_FLOPS)
    got_last = swap_cores(give_last)
    cross, along = call(take, [half_plane] * 2, cross, along, flops=FLOPS)
    grad_state, grad_sink = call(
        assemble, [state.shape, state.shape],
        labels, keep, got, keep_last, got_last, along, cross, keep=False,
        scratch=[pltpu.VMEM((2, half, ny, nz), jnp.float32), pltpu.VMEM((2, 2, ny, nz), jnp.float32), pltpu.SemaphoreType.DMA((2 * half + 4,))],
    )
    return (grad_state, grad_sink)


def solution(mesh):
    block = P(("groups", "gx"), "gy", "gz")
    in_specs = (block, P("gx", "gy", "gz"), block, block, block)
    return jax.shard_map(on_device, mesh=mesh, in_specs=in_specs, out_specs=(block, block), check_vma=False)
```

```python
import functools

import jax
import jax.numpy as jnp
from jax import lax
from jax.experimental import pallas as pl
from jax.experimental.pallas import tpu as pltpu
from jax.sharding import PartitionSpec as P

VMEM = pltpu.VMEM
HBM = pltpu.HBM
time_step = 0.06
scale = 0.5 * time_step
HALO = 4
TILE = 8
SWEPT = 11
LAST_FLOPS = 10000000000
PACK_FLOPS = 1100000000
OWN_FLOPS = 1024
FLOPS = 2200000000
S, C, T, F, K = range(5)
ONE = 4


def call(kernel, outs, *ins, keep=True, given=VMEM, scratch=(), flops=1024, aliases=None):
    space = VMEM if keep else jax.ShapeDtypeStruct
    block = pl.BlockSpec(memory_space=VMEM if given is VMEM else pl.ANY)
    return pl.pallas_call(
        kernel,
        out_shape=[space(shape, jnp.float32) for shape in outs],
        in_specs=[block] * len(ins),
        out_specs=[pl.BlockSpec(memory_space=VMEM if keep else pl.ANY)] * len(outs),
        scratch_shapes=list(scratch),
        input_output_aliases=aliases or {},
        compiler_params=pltpu.CompilerParams(vmem_limit_bytes=8 * 1024 * 1024),
        cost_estimate=pl.CostEstimate(flops=flops, bytes_accessed=1024, transcendentals=0),
    )(*[pltpu.with_memory_space_constraint(x, given) for x in ins])


def half_fluid(labels):
    return jnp.where(labels <= 1, 0.5, 0.0)


def touching(labels):
    return jnp.logical_or(labels == 1, labels == 2)


def rows_of(value):
    return lax.broadcasted_iota(jnp.int32, value.shape, 0)


def lanes_of(value):
    return lax.broadcasted_iota(jnp.int32, value.shape, 1)


def down_rows(before, here):
    return pltpu.roll(jnp.where(rows_of(here) == TILE - 1, before, here), 1, 0)


def up_rows(here, after):
    return pltpu.roll(jnp.where(rows_of(here) == 0, after, here), TILE - 1, 0)


def down_lanes(here):
    return pltpu.roll(here, 1, 1)


def up_lanes(here):
    return pltpu.roll(here, here.shape[1] - 1, 1)


def at(t):
    return slice(t * TILE, (t + 1) * TILE)


class Tiles:
    def __init__(self, *places):
        self.places = places

    def __getitem__(self, t):
        ref, slot = self.places[t % len(self.places)]
        return ref[at(slot)]

    def __setitem__(self, t, value):
        ref, slot = self.places[t]
        ref[at(slot)] = value

    def __len__(self):
        return len(self.places)


class Draft:
    def __init__(self, ref, values=None, prefix=()):
        self.ref, self.prefix = ref, prefix
        self.values = {} if values is None else values
        self.shape = ref.shape[len(prefix) :]

    @property
    def at(self):
        return _At(self)

    def _key(self, key):
        return self.prefix + (key if isinstance(key, tuple) else (key,))

    def __getitem__(self, key):
        key = self._key(key)
        name = key[:-1] + (key[-1].start,)
        return self.values[name][1] if name in self.values else self.ref[key]

    def __setitem__(self, key, value):
        key = self._key(key)
        self.values[key[:-1] + (key[-1].start,)] = (key, value)

    def flush(self):
        for key, value in self.values.values():
            self.ref[key] = value


class Held:
    def __setitem__(self, key, value):
        self.value = value

    def __getitem__(self, key):
        return self.value


class _At:
    def __init__(self, draft):
        self.draft = draft

    def __getitem__(self, key):
        return Draft(self.draft.ref, self.draft.values, self.draft._key(key))


def whole(ref):
    return Tiles(*[(ref, t) for t in range(ref.shape[0] // TILE)])


def with_ghost(main, ghost):
    return Tiles(*[(main, t) for t in range(main.shape[0] // TILE)], (ghost, 0))


def mid_and_rim(mid, rim):
    return Tiles((rim, 0), *[(mid, t) for t in range(mid.shape[0] // TILE)], (rim, 1), (rim, 2))


def put(ref, values):
    for t, value in enumerate(values):
        ref[at(t)] = value


class Across:
    def __init__(self, ky, kz, v):
        self.ky, self.kz, self.v = ky, kz, v
        self.known = {}

    def product(self, t):
        t = t % len(self.v)
        if t not in self.known:
            self.known[t] = self.ky[t] * self.v[t]
        return self.known[t]

    def __getitem__(self, t):
        here, kz = self.v[t], self.kz[t]
        along_y = self.ky[t] * down_rows(self.v[t - 1], here) + up_rows(self.product(t), self.product(t + 1))
        return along_y + (kz * down_lanes(here) + up_lanes(kz * here))


class Made:
    def __init__(self, values):
        self.values = values

    def __getitem__(self, t):
        return self.values[t % len(self.values)]

    def __len__(self):
        return len(self.values)


def sides_along_z(c, here):
    lanes = lanes_of(c)
    left = here + jnp.where(lanes == 0, 0.0, down_lanes(c)) * scale
    right = here + jnp.where(lanes == lanes.shape[1] - 1, 0.0, up_lanes(c)) * scale
    return left, right


def load_all(pairs, sems):
    copies = [pltpu.make_async_copy(a, b, sems.at[i]) for i, (a, b) in enumerate(pairs)]
    for copy in copies:
        copy.start()
    return copies


def load_planes(inputs, start, out, kinds, drains, sems):
    state, conduct, sink, labels, cotangent = inputs
    part = pl.ds(start, out.shape[1])
    pairs = [(labels.at[part], kinds), (sink.at[part], drains), (state.at[part], out.at[S])]
    return load_all(pairs + [(conduct.at[part], out.at[C]), (cotangent.at[part], out.at[T])], sems)


def fill_planes(out, kinds, drains):
    for i in range(out.shape[1]):
        out[F, i] = half_fluid(kinds[i])
        out[K, i] = jnp.where(touching(kinds[i]), drains[i], 0.0)


def pack_inputs(state, conduct, sink, labels, cotangent, up, down, trade, kinds, drains, ends, sems, plane_sems):
    count = state.shape[0]
    pairs = []
    for which, (out, plane) in enumerate(((up, count - 1), (down, 0))):
        pairs += [(state.at[plane], out.at[S]), (conduct.at[plane], out.at[C]), (cotangent.at[plane], out.at[T])]
        pairs += [(labels.at[plane], ends.at[which])]
    copies = load_all(pairs, plane_sems)
    start = (1 - lax.axis_index("gz")) * (count - trade.shape[1])
    copies += load_planes((state, conduct, sink, labels, cotangent), start, trade, kinds, drains, sems)
    for copy in copies:
        copy.wait()
    up[F] = half_fluid(ends[0])
    down[F] = half_fluid(ends[1])
    fill_planes(trade, kinds, drains)


def own_planes(state, conduct, sink, labels, cotangent, mine, kinds, drains, sems):
    start = lax.axis_index("gz") * (state.shape[0] - mine.shape[1])
    for copy in load_planes((state, conduct, sink, labels, cotangent), start, mine, kinds, drains, sems):
        copy.wait()
    fill_planes(mine, kinds, drains)


def pack_rims(two, planes, outs):
    for k in range(0, len(planes), 2):
        even, odd = planes[k], planes[min(k + 1, len(planes) - 1)]
        ny = even.shape[0]
        low_even, high_even = even[0:TILE], even[ny - TILE : ny]
        low_odd, high_odd = odd[0:TILE], odd[ny - TILE : ny]
        upper = rows_of(low_even) < HALO
        low = jnp.where(upper, low_even, pltpu.roll(low_odd, HALO, 0))
        high = jnp.where(upper, pltpu.roll(high_even, HALO, 0), high_odd)
        if two:
            outs[0][k // 2] = jnp.where(lax.axis_index("gy") == 0, high, low)
        else:
            outs[0][k // 2] = low
            outs[1][k // 2] = high


def unpack_rims(two, count_y, rims, planes):
    place = lax.axis_index("gy")
    for k in range(0, len(planes), 2):
        above = jnp.where(place < count_y - 1, rims[0][k // 2], 0.0)
        below = jnp.where(place > 0, rims[0 if two else 1][k // 2], 0.0)
        upper = rows_of(above) < HALO
        planes[k][...] = jnp.where(upper, above, pltpu.roll(below, HALO, 0))
        if k + 1 < len(planes):
            planes[k + 1][...] = jnp.where(upper, pltpu.roll(above, HALO, 0), below)


def gather_planes(mine, traded, block, near):
    core = lax.axis_index("gz")
    half, narrow = block.shape[1], mine.shape[3]
    own = pl.ds(pl.multiple_of(core * narrow, 128), narrow)
    other = pl.ds(pl.multiple_of((1 - core) * narrow, 128), narrow)
    start = 2 * core
    beside = (1 - core) * half + core
    beyond = (1 - core) * (half + 1)
    for j in range(5):
        for i in range(half):
            block[j, i, :, own] = mine[j, start + i]
            block[j, i, :, other] = traded[j, start + i]
        near[j, :, own] = mine[j, beside]
        near[j, :, other] = traded[j, beside]
        if j in (S, C):
            near[5 + j, :, own] = mine[j, beyond]
            near[5 + j, :, other] = traded[j, beyond]


def rim_planes(block, near):
    half = block.shape[1]
    core = lax.axis_index("gz")
    inward = lambda i: core * (half - 1) + i * (1 - 2 * core)
    early = [block.at[j, inward(0)] for j in range(5)] + [block.at[j, inward(1)] for j in (S, C)]
    late = [block.at[j, inward(1)] for j in (T, F, K)] + [block.at[j, inward(i)] for i in range(2, half) for j in range(5)]
    return early, late + [near.at[j] for j in range(7)]


def pack_along_y(two, block, near, *rims):
    early, late = rim_planes(block, near)
    ways = 1 if two else 2
    pack_rims(two, early, rims[:ways])
    pack_rims(two, late, rims[ways:])


class Lazy:
    def __init__(self, count, make):
        self.count, self.make, self.known = count, make, {}

    def __getitem__(self, t):
        t = t % self.count
        if t not in self.known:
            self.known[t] = self.make(t)
        return self.known[t]

    def __len__(self):
        return self.count


def prepare(todo, count_y, block, near, ghost, near_ghost, kx, ky_out, kz_out, diag, part, back, one):
    drafts = [Draft(ref) for ref in (kx, ky_out, kz_out, diag, part, back, one)]
    kx, ky_out, kz_out, diag, part, back, one = drafts
    place = lax.axis_index("gy")
    core = lax.axis_index("gz")
    half, ny = block.shape[1], block.shape[2]
    count, last = ny // TILE + 1, half - 1

    def own(j, i):
        if ghost is None:
            return Tiles(*[(block.at[j, i], t) for t in range(count - 1)], (None, 0))
        return with_ghost(block.at[j, i], ghost.at[j, i])

    def next_to(j):
        if ghost is None:
            return Tiles(*[(near.at[j], t) for t in range(count - 1)], (None, 0))
        return with_ghost(near.at[j], near_ghost.at[j])

    def faces_along_y(c):
        def make(t):
            value = (c[t] + down_rows(c[t - 1], c[t])) * scale
            if t == 0:
                value = jnp.where(jnp.logical_and(rows_of(value) == 0, place == 0), 0.0, value)
            if t == count - 1:
                value = jnp.where(jnp.logical_and(rows_of(value) == 0, place == count_y - 1), 0.0, value)
            return value

        return Lazy(count, make)

    def own_weight(c, f, t):
        here = c[t] * scale
        left, right = sides_along_z(c[t], here)
        low, high = down_rows(c[t - 1], c[t]), up_rows(c[t], c[t + 1])
        return left, (2.0 * here + (low + high) * scale) + (left + right) + time_step * f[t]

    for i in range(half):
        s, c, a, f, k = (own(j, i) for j in (S, C, T, F, K))
        ky, kz = faces_along_y(c), {}
        for t in todo:
            left, weight = own_weight(c, f, t)
            kz[t] = jnp.where(lanes_of(left) == 0, 0.0, left)
            slot = at(todo.index(t))
            if i > 0:
                face = (c[t] + own(C, i - 1)[t]) * scale
                kx[i - 1, slot] = face
                weight = weight + face
            if i < last:
                weight = weight + (c[t] + own(C, i + 1)[t]) * scale
            diag[i, slot] = weight
            ky_out[i, slot] = ky[t]
            kz_out[i, slot] = kz[t]
        scaled = Lazy(count, lambda t, a=a, f=f: a[t] * (0.5 + f[t]))
        ahead = Across(ky, kz, s)
        behind = Across(ky, kz, scaled)
        for t in todo:
            slot = at(todo.index(t))
            d, b = diag[i, slot], scaled[t]
            go = ahead[t] - d * s[t] - time_step * k[t] * jnp.tanh(s[t])
            come = behind[t] - d * b
            if i > 0:
                go = go + (kx[i - 1, slot] + time_step * f[t]) * own(S, i - 1)[t]
                come = come + kx[i - 1, slot] * (own(T, i - 1)[t] * (0.5 + own(F, i - 1)[t]))
            if i < last:
                face, high_f = (c[t] + own(C, i + 1)[t]) * scale, own(F, i + 1)[t]
                go = go + face * own(S, i + 1)[t]
                come = come + (face + time_step * high_f) * (own(T, i + 1)[t] * (0.5 + high_f))
            part[i, slot] = s[t] + (0.5 + f[t]) * go
            back[i, slot] = a[t] + come
    s, c, f, k = (next_to(j) for j in (S, C, F, K))
    kz = {}
    for t in todo:
        left, _ = own_weight(c, f, t)
        kz[t] = jnp.where(lanes_of(left) == 0, 0.0, left)
    ahead = Across(faces_along_y(c), kz, s)
    is_low = core == 0
    for t in todo:
        _, weight = own_weight(c, f, t)
        c_own = jnp.where(is_low, own(C, last)[t], own(C, 0)[t])
        s_own = jnp.where(is_low, own(S, last)[t], own(S, 0)[t])
        face_own, face_far = (c[t] + c_own) * scale, (c[t] + next_to(5 + C)[t]) * scale
        wind = time_step * f[t]
        go = ahead[t] - (weight + face_own + face_far) * s[t] - time_step * k[t] * jnp.tanh(s[t])
        go = go + (face_own + jnp.where(is_low, wind, 0.0)) * s_own
        go = go + (face_far + jnp.where(is_low, 0.0, wind)) * next_to(5 + S)[t]
        one[at(todo.index(t))] = s[t] + (0.5 + f[t]) * go
    for draft in drafts:
        draft.flush()


def prepare_mid(count_y, block, near, *outs):
    prepare(list(range(1, block.shape[2] // TILE - 1)), count_y, block, near, None, None, *outs)


def prepare_rim(two, count_y, block, near, *refs):
    ways = 1 if two else 2
    rims, (ghost, near_ghost, *outs) = refs[: 2 * ways], refs[2 * ways :]
    count = block.shape[2] // TILE
    early, late = rim_planes(ghost, near_ghost)
    unpack_rims(two, count_y, rims[:ways], early)
    unpack_rims(two, count_y, rims[ways:], late)
    prepare([0, count - 1, count], count_y, block, near, ghost, near_ghost, *outs)


PACKED = (((S, 3), (C, 3), (ONE, 2)), ((T, 2), (F, 2)))


def pack_ghosts(place, parts, ghosts):
    rows = rows_of(ghosts[S])
    low = high = jnp.zeros_like(ghosts[S])
    taken = 0
    for j, depth in parts:
        span = jnp.logical_and(rows >= taken, rows < taken + depth)
        low = jnp.where(span, pltpu.roll(ghosts[j], taken, 0) if taken else ghosts[j], low)
        span = jnp.logical_and(rows >= TILE - taken - depth, rows < TILE - taken)
        high = jnp.where(span, pltpu.roll(ghosts[j], TILE - taken, 0) if taken else ghosts[j], high)
        taken += depth
    return jnp.where(place == 0, low, high)


def unpack_ghosts(place, parts, packed):
    rows = rows_of(packed)
    ghosts, taken = {}, 0
    for j, depth in parts:
        low = pltpu.roll(packed, TILE - taken, 0) if taken else packed
        high = pltpu.roll(packed, taken, 0) if taken else packed
        low = jnp.where(rows < depth, low, 0.0)
        high = jnp.where(rows >= TILE - depth, high, 0.0)
        ghosts[j] = jnp.where(place == 0, low, high)
        taken += depth
    return ghosts


def pack_off(two, count_y, block, part_mid, *refs):
    ways = 1 if two else 2
    rims, (off,) = refs[:ways], refs[ways:]
    place = lax.axis_index("gy")
    core = lax.axis_index("gz")
    last = block.shape[1] - 1
    outer = core * last
    inside = outer + 1 - 2 * core
    ghost = [Held() for _ in range(7)]
    unpack_rims(two, count_y, rims, ghost)
    s, c, f, k = (with_ghost(block.at[j, outer], ghost[j]) for j in (S, C, F, K))
    s_in, c_in = (with_ghost(block.at[j, inside], ghost[5 + j]) for j in (S, C))
    count = len(s)

    def face_along_y(t):
        value = (c[t] + down_rows(c[t - 1], c[t])) * scale
        if t == 0:
            value = jnp.where(jnp.logical_and(rows_of(value) == 0, place == 0), 0.0, value)
        if t == count - 1:
            value = jnp.where(jnp.logical_and(rows_of(value) == 0, place == count_y - 1), 0.0, value)
        return value

    todo, kz, weight = (0, count - 2, count - 1), {}, {}
    for t in todo:
        here = c[t] * scale
        left, right = sides_along_z(c[t], here)
        kz[t] = jnp.where(lanes_of(left) == 0, 0.0, left)
        low, high = down_rows(c[t - 1], c[t]), up_rows(c[t], c[t + 1])
        weight[t] = (2.0 * here + (low + high) * scale) + (left + right) + time_step * f[t]
    flow = Across(Lazy(count, face_along_y), kz, s)
    one = {}
    for t in range(count):
        if t in todo:
            face = (c[t] + c_in[t]) * scale
            go = flow[t] - (weight[t] + face) * s[t] - time_step * k[t] * jnp.tanh(s[t])
            go = go + (face + jnp.where(core == 0, 0.0, time_step) * f[t]) * s_in[t]
            one[t] = s[t] + (0.5 + f[t]) * go
    for t in range(count - 1):
        off[at(t)] = one[t] if t in todo else part_mid[outer, at(t - 1)]
    ghosts = {j: ghost[j][...] for j in range(4)}
    ghosts[ONE] = one[count - 1]
    if two:
        for slot, parts in enumerate(PACKED):
            off[at(count - 1 + slot)] = pack_ghosts(place, parts, ghosts)
    else:
        for j in range(5):
            off[at(count - 1 + j)] = ghosts[j]


def choose_half(up, down, *refs):
    for j in range(4):
        refs[j // 2 - 2][j % 2] = jnp.where(lax.axis_index("gz") == 0, down[j], up[j])


def coefficients(refs):
    mids, rims = refs[:6], refs[7:13]
    return [lambda i, m=m, r=r: mid_and_rim(m.at[i], r.at[i]) for m, r in zip(mids, rims)]


def fill_sides(near, near_ghost, up, down, passed, side):
    core = lax.axis_index("gz")
    ny, narrow = up.shape[1], up.shape[2]
    outside, inside = core, 1 - core
    for j in range(4):
        side[j, outside, 0:ny, 0:narrow] = jnp.where(core == 0, up[j], passed[j // 2][j % 2])
        side[j, outside, 0:ny, narrow : 2 * narrow] = jnp.where(core == 0, passed[j // 2][j % 2], down[j])
        side[j, inside, 0:ny] = near[j]
        side[j, inside, ny : ny + TILE] = near_ghost[j]


def fill_side_ghosts(two, ny, off, side):
    place, outside = lax.axis_index("gy"), lax.axis_index("gz")
    first = ny // TILE
    if two:
        ghosts = {}
        for slot, parts in enumerate(PACKED):
            ghosts.update(unpack_ghosts(place, parts, off[at(first + slot)]))
    else:
        ghosts = {j: off[at(first + j)] for j in range(5)}
    for j in range(4):
        for which in range(2):
            place = (j, which, slice(ny, ny + TILE))
            side[place] = jnp.where(outside == which, ghosts[j], side[place])
    return ghosts[ONE]


def sweep(late, block, ghost, weights, side, edge, add, first, known, linear, adjoint, sa, b2, hot2, inward):
    kx, ky, kz, diag, part, back = weights
    half, ny = block.shape[1], block.shape[2]
    count, last = ny // TILE, half - 1
    own = lambda j, i: with_ghost(block.at[j, i], ghost.at[j, i])
    for which, i in ((0, 0), (1, last)):
        s, f, c = own(S, i), own(F, i), own(C, i)
        s_out, c_out, f_out = (whole(side.at[j, which]) for j in (S, C, F))
        for t in [count] if late else range(count):
            face = (c[t] + c_out[t]) * scale
            edge[which, at(t)] = face
            v, beyond = s[t], s_out[t]
            if which == 0:
                inner_add = (face + time_step * f[t]) * beyond - face * v
                outer_add = face * (v - beyond)
            else:
                inner_add = face * (beyond - v)
                outer_add = (face + time_step * f_out[t]) * v - face * beyond
            first[i, at(t)] = part(i)[t] + (0.5 + f[t]) * inner_add
            add[which, at(t)] = (0.5 + f_out[t]) * outer_add
    for i in range(1, last):
        for t in [] if late else range(count + 1):
            first[i, at(t)] = part(i)[t]
    for i in range(half):
        outer = i in (0, last)
        v, f, k, s, a = whole(first.at[i]), own(F, i), own(K, i), own(S, i), own(T, i)
        flow = Across(ky(i), kz(i), v)
        if outer:
            todo = [0, count - 1, count] if late else range(1, count - 1)
        else:
            todo = [count] if late else range(count)
        for t in todo:
            rc = 0.5 + f[t]
            sink = time_step * k[t]
            hot1 = jnp.tanh(v[t])
            full = diag(i)[t]
            if i == 0:
                full = full + edge[0, at(t)]
            if i == last:
                full = full + edge[1, at(t)]
            adjoint[i, at(t)] = full + sink * (1.0 - hot1 * hot1)
            rate = flow[t] - full * v[t] - sink * hot1
            if i > 0:
                rate = rate + (kx(i - 1)[t] + time_step * f[t]) * first[i - 1, at(t)]
            if i < last:
                rate = rate + kx(i)[t] * first[i + 1, at(t)]
            value = 0.75 * s[t] + 0.25 * (v[t] + rc * rate)
            b = a[t] * rc
            total = back(i)[t]
            if i == 0:
                total = total + edge[0, at(t)] * (side[T, 0, at(t)] * (0.5 + side[F, 0, at(t)]) - b)
            if i == last:
                high, high_f = edge[1, at(t)], side[F, 1, at(t)]
                total = total + ((high + time_step * high_f) * (side[T, 1, at(t)] * (0.5 + high_f)) - high * b)
            if outer:
                which = 0 if i == 0 else 1
                known[which, at(t)] = value
                linear[which, at(t)] = total
            else:
                hot = jnp.tanh(value)
                hot2[i, at(t)] = hot
                total = (2.0 / 3.0) * (total - sink * (1.0 - hot * hot) * b)
                sa[i, at(t)] = total
                b2[i, at(t)] = total * rc
    for t in [count] if late else range(count):
        inward[0, at(t)] = (kx(0)[t] + time_step * own(F, 1)[t]) * b2[1, at(t)]
        inward[1, at(t)] = kx(last - 1)[t] * b2[last - 1, at(t)]


def middle(block, ghost, near, near_ghost, up, down, *refs):
    passed, weights, outs = refs[:2], coefficients(refs[2:16]), refs[16:]
    fill_sides(near, near_ghost, up, down, passed, outs[0])
    drafts = [Draft(ref) for ref in outs[1:]]
    sweep(False, block, ghost, weights, outs[0], *drafts)
    for draft in drafts:
        draft.flush()


def outward(two, block, ghost, off, *refs):
    weights, one_mid, one_rim = coefficients(refs[:14]), refs[6], refs[13]
    outs = [Draft(ref) for ref in refs[14 + SWEPT : 14 + 2 * SWEPT]]
    *ends, off_b = refs[14 + 2 * SWEPT :]
    hot2, sa, b2 = (Draft(ref) for ref in ends)
    side, edge, add, _, known, linear, *_ = outs
    core = lax.axis_index("gz")
    half, ny = block.shape[1], block.shape[2]
    count, last = ny // TILE, half - 1
    own = lambda j, i: with_ghost(block.at[j, i], ghost.at[j, i])
    one_ghost = fill_side_ghosts(two, ny, off, side)
    sweep(True, block, ghost, weights, *outs)
    for which, i in ((0, 0), (1, last)):
        f, k, a = own(F, i), own(K, i), own(T, i)
        mine = core == which
        for t in range(count + 1):
            one = off[at(t)] if t < count else one_ghost
            one = jnp.where(mine, one + add[which, at(t)], mid_and_rim(one_mid, one_rim)[t])
            face = edge[which, at(t)]
            if which == 0:
                face = face + time_step * f[t]
            rc = 0.5 + f[t]
            hot = jnp.tanh(known[which, at(t)] + 0.25 * rc * face * one)
            total = (2.0 / 3.0) * (linear[which, at(t)] - time_step * k[t] * (1.0 - hot * hot) * (a[t] * rc))
            hot2[which, at(t)] = hot
            sa[which, at(t)] = total
            b2[which, at(t)] = total * rc
    for t in range(count + 1):
        off_b[at(t)] = jnp.where(core == 0, b2[0, at(t)], b2[1, at(t)])
    for draft in (b2, sa, hot2, *outs):
        draft.flush()


def inside_adjoint(block, ghost, near, near_ghost, *refs):
    (kx, ky, kz, diag, part, back), on_b = coefficients(refs[:14]), refs[14]
    core = lax.axis_index("gz")
    half, ny = block.shape[1], block.shape[2]
    last = half - 1
    i = (1 - core) * last
    beside = i - 1 + 2 * core
    own = lambda j, plane: with_ghost(block.at[j, plane], ghost.at[j, plane])
    c_h, s_h, t_h, f_h = (with_ghost(near.at[j], near_ghost.at[j]) for j in (C, S, T, F))
    one = mid_and_rim(refs[6], refs[13])
    s, c, a, f, k = (own(j, i) for j in (S, C, T, F, K))
    above, below = jnp.where(core == 0, time_step, 0.0), jnp.where(core == 0, 0.0, time_step)
    step, next_first = kx((1 - core) * (last - 1)), part(beside)
    faces, first = [], []
    for t in range(ny // TILE + 1):
        faces.append((c[t] + c_h[t]) * scale)
        first.append(part(i)[t] + (0.5 + f[t]) * ((faces[t] + below * f[t]) * s_h[t] - faces[t] * s[t]))
    flow = Across(ky(i), kz(i), Made(first))
    out = []
    for t in range(ny // TILE + 1):
        rc, sink, face = 0.5 + f[t], time_step * k[t], faces[t]
        rate = flow[t] - (diag(i)[t] + face) * first[t] - sink * jnp.tanh(first[t])
        rate = rate + (step[t] + above * f[t]) * next_first[t] + (face + below * f[t]) * one[t]
        hot = jnp.tanh(0.75 * s[t] + 0.25 * (first[t] + rc * rate))
        b = a[t] * rc
        total = back(i)[t] + (face + above * f_h[t]) * (t_h[t] * (0.5 + f_h[t])) - face * b
        out.append((2.0 / 3.0) * (total - sink * (1.0 - hot * hot) * b) * rc)
    put(on_b, out)


def outward_first(ky_mid, kz_mid, ky_rim, kz_rim, adjoint, inward, sa, b2, fa, along, cross):
    core = lax.axis_index("gz")
    half, ny = adjoint.shape[0], along.shape[0]
    values = []
    for which, i in ((0, 0), (1, half - 1)):
        b = whole(b2.at[which])
        flow = Across(mid_and_rim(ky_mid.at[i], ky_rim.at[i]), mid_and_rim(kz_mid.at[i], kz_rim.at[i]), b)
        total = lambda t: sa[which, at(t)] + flow[t] - adjoint[i, at(t)] * b[t] + inward[which, at(t)]
        values.append([0.25 * total(t) for t in range(len(b))])
    low, high = values
    for t in range(ny // TILE):
        along[at(t)], cross[at(t)] = halves(core, jnp.where(core == 0, low[t], high[t]))
    for which in range(2):
        put(fa.at[which], values[which])


def inner(block, ghost, edge, side, first, adjoint, sa_in, b2_in, hot2_in, sa_out, b2_out, hot2_out, fa_out, *refs):
    kx, ky, kz, diag, _, _ = coefficients(refs[:14])
    value, term, adjoint0, hot0, fa, b3 = refs[14:]
    half, ny = block.shape[1], block.shape[2]
    count, last = ny // TILE, half - 1
    own = lambda j, i: with_ghost(block.at[j, i], ghost.at[j, i])
    pick = lambda i, inside, outside: inside.at[i] if 0 < i < last else outside.at[0 if i == 0 else 1]
    sa = lambda i: whole(pick(i, sa_in, sa_out))
    b2 = lambda i: whole(pick(i, b2_in, b2_out))
    hot2 = lambda i: whole(pick(i, hot2_in, hot2_out))
    for i in range(half):
        f = own(F, i)
        flow = Across(ky(i), kz(i), b2(i))
        for t in range(count + 1):
            if 0 < i < last:
                total = sa(i)[t] + flow[t] - adjoint[i, at(t)] * b2(i)[t]
                total = total + kx(i - 1)[t] * b2(i - 1)[t] + (kx(i)[t] + time_step * own(F, i + 1)[t]) * b2(i + 1)[t]
                total = 0.25 * total
            else:
                total = fa_out[0 if i == 0 else 1, at(t)]
            fa[i, at(t)] = total
            b3[i, at(t)] = total * (0.5 + f[t])
    for i in range(half):
        s, f, k, a = own(S, i), own(F, i), own(K, i), own(T, i)
        b = whole(b3.at[i])
        flow = Across(ky(i), kz(i), b)
        for t in range(count):
            hot = jnp.tanh(s[t])
            full = diag(i)[t]
            if i == 0:
                full = full + edge[0, at(t)]
            if i == last:
                full = full + edge[1, at(t)]
            full = full + time_step * k[t] * (1.0 - hot * hot)
            total = flow[t] - full * b[t] + fa[i, at(t)] + 0.75 * sa(i)[t] + a[t] * (1.0 / 3.0)
            if i > 0:
                total = total + kx(i - 1)[t] * b3[i - 1, at(t)]
            if i < last:
                total = total + (kx(i)[t] + time_step * own(F, i + 1)[t]) * b3[i + 1, at(t)]
            value[i, at(t)] = total
            first_hot = jnp.tanh(first[i, at(t)])
            total = (2.0 / 3.0) * hot2(i)[t] * a[t] + 0.25 * first_hot * sa(i)[t] + hot * fa[i, at(t)]
            term[i, at(t)] = -time_step * (0.5 + f[t]) * total
            if i == 0 or i == last:
                which = 0 if i == 0 else 1
                adjoint0[which, at(t)] = full
                hot0[which, at(t)] = -time_step * (0.5 + f[t]) * hot


def halves(core, value):
    narrow = value.shape[1] // 2
    left, right = value[:, :narrow], value[:, narrow:]
    return jnp.where(core == 0, left, right), jnp.where(core == 0, right, left)


def from_beyond(which, message, block, ghost, edge, side, b2_out, value, term, adjoint0, hot0, weights):
    kx, ky, kz = weights
    half, ny = block.shape[1], block.shape[2]
    count, last = ny // TILE, half - 1
    i = which * last
    beside = i + 1 - 2 * which
    wind = jnp.where(which == 1, time_step, 0.0)
    against = time_step - wind
    f = with_ghost(block.at[F, i], ghost.at[F, i])
    into, gains, late = [], [], []
    for t in range(count + 1):
        into.append(edge[which, at(t)] + wind * side[F, which, at(t)])
        gains.append(0.25 * into[t] * message[at(t)])
        late.append(gains[t] * (0.5 + f[t]))
    flow = Across(ky(i), kz(i), Made(late))
    step = kx(which * (last - 1))
    out = []
    for t in range(count):
        factor = into[t] * (0.5 + side[F, which, at(t)])
        known = 0.25 * (edge[which, at(t)] + against * f[t]) * b2_out[which, at(t)]
        total = value[i, at(t)] + gains[t] + flow[t] - adjoint0[which, at(t)] * late[t] + factor * known
        next_total = value[beside, at(t)] + (step[t] + wind * f[t]) * late[t]
        out.append((t, total, next_total, term[i, at(t)] + hot0[which, at(t)] * gains[t], factor))
    return out


def three(refs):
    return [lambda i, m=m, r=r: mid_and_rim(m.at[i], r.at[i]) for m, r in zip(refs[:3], refs[3:])]


def finish_inside(block, ghost, edge, side, b2_out, value, term, adjoint0, hot0, on_b, *refs):
    *six, keep, give = refs
    core = lax.axis_index("gz")
    half, ny = block.shape[1], block.shape[2]
    plane = lambda r: core * (half - 1) + r * (1 - 2 * core)

    def write(place, t, value):
        keep[place, at(t)], give[place, at(t)] = halves(core, value)

    parts = from_beyond(1 - core, on_b, block, ghost, edge, side, b2_out, value, term, adjoint0, hot0, three(six))
    for t, total, next_total, sink, factor in parts:
        write(half - 3, t, total)
        write(half - 4, t, next_total)
        write(2 * half - 4, t, sink)
        write(2 * half - 2, t, factor)
        for r in range(2, half - 2):
            write(r - 2, t, value[plane(r), at(t)])
        for r in range(1, half - 1):
            write(half - 3 + r, t, term[plane(r), at(t)])
        wind = jnp.where(core == 1, time_step, 0.0)
        f_out = side[F, core, at(t)]
        write(2 * half - 3, t, (edge[core, at(t)] + wind * f_out) * (0.5 + f_out))


def finish_outside(block, ghost, edge, side, b2_out, value, term, adjoint0, hot0, off_b, *refs):
    *six, fa_out, _, keep, give = refs
    core = lax.axis_index("gz")
    parts = from_beyond(core, off_b, block, ghost, edge, side, b2_out, value, term, adjoint0, hot0, three(six))
    for t, total, next_total, sink, _ in parts:
        for place, value_here in enumerate((total, next_total, sink, fa_out[1 - core, at(t)])):
            keep[place, at(t)], give[place, at(t)] = halves(core, value_here)


def take(cross, along, cross_out, along_out):
    cross_out[...] = cross[...]
    along_out[...] = along[...]


def assemble(labels, keep, got, keep_last, got_last, along, cross, grad_state, grad_sink, *refs):
    masked, ends, sems = refs
    core = lax.axis_index("gz")
    count = grad_state.shape[0]
    half = count // 2
    copies = []

    def send(source, target):
        copies.append(pltpu.make_async_copy(source, target, sems.at[len(copies)]))
        copies[-1].start()

    sides = ((core, keep, keep_last, got_last.at[3], cross), (1 - core, got, got_last, keep_last.at[3], along))
    plane = lambda who, r: who * (count - 1) + r * (1 - 2 * who)
    for who, most, outermost, _, _ in sides:
        send(outermost.at[1], grad_state.at[plane(who, 1)])
        for r in range(2, half - 1):
            send(most.at[r - 2], grad_state.at[plane(who, r)])
    for slot, (who, most, outermost, inside, outside) in enumerate(sides):
        ends[slot, 0] = outermost[0] + most[2 * half - 3] * outside[...]
        send(ends.at[slot, 0], grad_state.at[plane(who, 0)])
        ends[slot, 1] = most[half - 3] + most[2 * half - 2] * inside[...]
        send(ends.at[slot, 1], grad_state.at[plane(who, half - 1)])
        for r in range(half):
            term = outermost[2] if r == 0 else most[half - 3 + r]
            place = plane(who, r)
            masked[slot, place - who * half] = jnp.where(touching(labels[place]), term, 0.0)
        send(masked.at[slot], grad_sink.at[pl.ds(who * half, half)])
    for copy in copies:
        copy.wait()


def on_device(state, conduct, sink, labels, cotangent):
    count, ny, nz = state.shape
    half, wide, rows = count // 2, 2 * nz, ny + TILE
    count_x, count_y = lax.axis_size("gx"), lax.axis_size("gy")
    assert lax.axis_size("gz") == 2 and half >= 4 and ny % TILE == 0 and ny >= 3 * TILE
    two = count_y == 2
    ahead = [(i, (i + 1) % count_x) for i in range(count_x)]
    behind = [(b, a) for a, b in ahead]
    chips = [(2 * i + 1, (2 * i + 2) % (2 * count_x)) for i in range(count_x)]
    chips = chips + [(b, a) for a, b in chips]

    def swap_cores(x):
        return lax.ppermute(x, "gz", [(0, 1), (1, 0)])

    def swap_chips(x):
        return lax.ppermute(x, ("gx", "gz"), chips)

    def to_slabs(x):
        route = [(2 * i + c, 2 * ((i + 2 * c - 1) % count_x) + c) for i in range(count_x) for c in range(2)]
        return lax.ppermute(x, ("gx", "gz"), route)

    def along_y(rims):
        forward = [(i, (i + 1) % count_y) for i in range(count_y)]
        backward = [(b, a) for a, b in forward]
        routes = [forward] if two else [backward, forward]
        return [lax.ppermute(rim, "gy", routes[i % len(routes)]) for i, rim in enumerate(rims)]

    ways = 1 if two else 2
    inputs = (state, conduct, sink, labels, cotangent)
    plane, span = (4, ny, nz), (5, half + 2, ny, nz)
    kinds = pltpu.VMEM((half + 2, ny, nz), jnp.int32)
    drains = pltpu.VMEM((half + 2, ny, nz), jnp.float32)
    sems = lambda many: pltpu.SemaphoreType.DMA((many,))
    up, down, trade = call(
        pack_inputs, [plane, plane, span], *inputs, given=HBM,
        scratch=[kinds, drains, pltpu.VMEM((2, ny, nz), jnp.int32), sems(5), sems(8)],
    )
    up = lax.ppermute(up, "gx", ahead)
    down = lax.ppermute(down, "gx", behind)
    traded = swap_cores(trade)
    (mine,) = call(own_planes, [span], *inputs, given=HBM, scratch=[kinds, drains, sems(5)], flops=OWN_FLOPS)
    block, near = call(gather_planes, [(5, half, ny, wide), (7, ny, wide)], mine, traded)
    sizes = [4, (5 * half + 1) // 2]
    rims = call(functools.partial(pack_along_y, two), [(n, TILE, wide) for n in sizes for _ in range(ways)], block, near)
    rims = along_y(rims)
    split = lambda r: [(half - 1, r, wide)] + [(half, r, wide)] * 5 + [(r, wide)]
    mids = call(functools.partial(prepare_mid, count_y), split(ny - 2 * TILE), block, near)
    ghost, near_ghost, *edges = call(
        functools.partial(prepare_rim, two, count_y),
        [(5, half, TILE, wide), (7, TILE, wide)] + split(3 * TILE), block, near, *rims,
    )
    (off,) = call(
        functools.partial(pack_off, two, count_y), [(ny + (len(PACKED) if two else 5) * TILE, wide)],
        block, mids[4], *rims[:ways], flops=PACK_FLOPS,
    )
    off = swap_chips(off)
    own, outer = (half, rows, wide), (2, rows, wide)
    (on_b,) = call(inside_adjoint, [(rows, wide)], block, ghost, near, near_ghost, *mids, *edges)
    passed = [swap_cores(x) for x in call(choose_half, [(2, ny, nz)] * 2, up, down, on_b)]
    on_b = swap_cores(on_b)
    swept_shapes = [(4, 2, rows, wide), outer, outer, own, outer, outer, own, own, own, own, outer]
    assert len(swept_shapes) == SWEPT
    swept = call(middle, swept_shapes, block, ghost, near, near_ghost, up, down, *passed, *mids, *edges)
    ends, mains = (rows, wide), (ny, wide)
    *swept, hot2_out, sa_out, b2_out, off_b = call(
        functools.partial(outward, two), swept_shapes + [outer] * 3 + [ends], block, ghost, off, *mids, *edges, *swept,
        aliases={17 + i: i for i in range(SWEPT)},
    )
    side, edge, add, first, known, linear, adjoint, sa, b2, hot2, inward = swept
    off_b = swap_chips(off_b)
    half_plane = (ny, nz)
    fa_out, along, cross = call(
        outward_first, [outer] + [half_plane] * 2,
        mids[1], mids[2], edges[1], edges[2], adjoint, inward, sa_out, b2_out,
    )
    cross, along = swap_chips(cross), to_slabs(along)
    main = lambda planes: (planes, ny, wide)
    planes = lambda many: (many, ny, nz)
    value, term, adjoint0, hot0, _, _ = call(
        inner, [main(half), main(half), main(2), main(2), own, own],
        block, ghost, edge, side, first, adjoint, sa, b2, hot2, sa_out, b2_out, hot2_out, fa_out, *mids, *edges,
    )
    ready = (block, ghost, edge, side, b2_out, value, term, adjoint0, hot0)
    keep, give = call(finish_inside, [planes(2 * half - 1)] * 2, *ready, on_b, *mids[:3], *edges[:3])
    got = swap_cores(give)
    keep_last, give_last = call(finish_outside, [planes(4)] * 2, *ready, off_b, *mids[:3], *edges[:3], fa_out, keep, flops=LAST_FLOPS)
    got_last = swap_cores(give_last)
    cross, along = call(take, [half_plane] * 2, cross, along, flops=FLOPS)
    grad_state, grad_sink = call(
        assemble, [state.shape, state.shape],
        labels, keep, got, keep_last, got_last, along, cross, keep=False,
        scratch=[pltpu.VMEM((2, half, ny, nz), jnp.float32), pltpu.VMEM((2, 2, ny, nz), jnp.float32), pltpu.SemaphoreType.DMA((2 * half + 4,))],
    )
    return (grad_state, grad_sink)


def solution(mesh):
    block = P(("groups", "gx"), "gy", "gz")
    in_specs = (block, P("gx", "gy", "gz"), block, block, block)
    return jax.shard_map(on_device, mesh=mesh, in_specs=in_specs, out_specs=(block, block), check_vma=False)
```

```python
import functools

import jax
import jax.numpy as jnp
from jax import lax
from jax.experimental import pallas as pl
from jax.experimental.pallas import tpu as pltpu
from jax.sharding import PartitionSpec as P

VMEM = pltpu.VMEM
HBM = pltpu.HBM
time_step = 0.06
scale = 0.5 * time_step
HALO = 4
TILE = 8
SWEPT = 11
LAST_FLOPS = 10000000000
PACK_FLOPS = 700000000
FLOPS = 2200000000
S, C, T, F, K = range(5)
ONE = 4


def call(kernel, outs, *ins, keep=True, given=VMEM, scratch=(), flops=1024, aliases=None):
    space = VMEM if keep else jax.ShapeDtypeStruct
    block = pl.BlockSpec(memory_space=VMEM if given is VMEM else pl.ANY)
    return pl.pallas_call(
        kernel,
        out_shape=[space(shape, jnp.float32) for shape in outs],
        in_specs=[block] * len(ins),
        out_specs=[pl.BlockSpec(memory_space=VMEM if keep else pl.ANY)] * len(outs),
        scratch_shapes=list(scratch),
        input_output_aliases=aliases or {},
        compiler_params=pltpu.CompilerParams(vmem_limit_bytes=8 * 1024 * 1024),
        cost_estimate=pl.CostEstimate(flops=flops, bytes_accessed=1024, transcendentals=0),
    )(*[pltpu.with_memory_space_constraint(x, given) for x in ins])


def half_fluid(labels):
    return jnp.where(labels <= 1, 0.5, 0.0)


def touching(labels):
    return jnp.logical_or(labels == 1, labels == 2)


def rows_of(value):
    return lax.broadcasted_iota(jnp.int32, value.shape, 0)


def lanes_of(value):
    return lax.broadcasted_iota(jnp.int32, value.shape, 1)


def down_rows(before, here):
    return pltpu.roll(jnp.where(rows_of(here) == TILE - 1, before, here), 1, 0)


def up_rows(here, after):
    return pltpu.roll(jnp.where(rows_of(here) == 0, after, here), TILE - 1, 0)


def down_lanes(here):
    return pltpu.roll(here, 1, 1)


def up_lanes(here):
    return pltpu.roll(here, here.shape[1] - 1, 1)


def at(t):
    return slice(t * TILE, (t + 1) * TILE)


class Tiles:
    def __init__(self, *places):
        self.places = places

    def __getitem__(self, t):
        ref, slot = self.places[t % len(self.places)]
        return ref[at(slot)]

    def __setitem__(self, t, value):
        ref, slot = self.places[t]
        ref[at(slot)] = value

    def __len__(self):
        return len(self.places)


class Draft:
    def __init__(self, ref, values=None, prefix=()):
        self.ref, self.prefix = ref, prefix
        self.values = {} if values is None else values
        self.shape = ref.shape[len(prefix) :]

    @property
    def at(self):
        return _At(self)

    def _key(self, key):
        return self.prefix + (key if isinstance(key, tuple) else (key,))

    def __getitem__(self, key):
        key = self._key(key)
        name = key[:-1] + (key[-1].start,)
        return self.values[name][1] if name in self.values else self.ref[key]

    def __setitem__(self, key, value):
        key = self._key(key)
        self.values[key[:-1] + (key[-1].start,)] = (key, value)

    def flush(self):
        for key, value in self.values.values():
            self.ref[key] = value


class _At:
    def __init__(self, draft):
        self.draft = draft

    def __getitem__(self, key):
        return Draft(self.draft.ref, self.draft.values, self.draft._key(key))


def whole(ref):
    return Tiles(*[(ref, t) for t in range(ref.shape[0] // TILE)])


def with_ghost(main, ghost):
    return Tiles(*[(main, t) for t in range(main.shape[0] // TILE)], (ghost, 0))


def mid_and_rim(mid, rim):
    return Tiles((rim, 0), *[(mid, t) for t in range(mid.shape[0] // TILE)], (rim, 1), (rim, 2))


def put(ref, values):
    for t, value in enumerate(values):
        ref[at(t)] = value


class Across:
    def __init__(self, ky, kz, v):
        self.ky, self.kz, self.v = ky, kz, v
        self.known = {}

    def product(self, t):
        t = t % len(self.v)
        if t not in self.known:
            self.known[t] = self.ky[t] * self.v[t]
        return self.known[t]

    def __getitem__(self, t):
        here, kz = self.v[t], self.kz[t]
        along_y = self.ky[t] * down_rows(self.v[t - 1], here) + up_rows(self.product(t), self.product(t + 1))
        return along_y + (kz * down_lanes(here) + up_lanes(kz * here))


class Made:
    def __init__(self, values):
        self.values = values

    def __getitem__(self, t):
        return self.values[t % len(self.values)]

    def __len__(self):
        return len(self.values)


def sides_along_z(c, here):
    lanes = lanes_of(c)
    left = here + jnp.where(lanes == 0, 0.0, down_lanes(c)) * scale
    right = here + jnp.where(lanes == lanes.shape[1] - 1, 0.0, up_lanes(c)) * scale
    return left, right


def load_all(pairs, sems):
    copies = [pltpu.make_async_copy(a, b, sems.at[i]) for i, (a, b) in enumerate(pairs)]
    for copy in copies:
        copy.start()
    return copies


def load_planes(inputs, start, out, kinds, drains, sems):
    state, conduct, sink, labels, cotangent = inputs
    part = pl.ds(start, out.shape[1])
    pairs = [(labels.at[part], kinds), (sink.at[part], drains), (state.at[part], out.at[S])]
    return load_all(pairs + [(conduct.at[part], out.at[C]), (cotangent.at[part], out.at[T])], sems)


def fill_planes(out, kinds, drains):
    for i in range(out.shape[1]):
        out[F, i] = half_fluid(kinds[i])
        out[K, i] = jnp.where(touching(kinds[i]), drains[i], 0.0)


def pack_inputs(state, conduct, sink, labels, cotangent, up, down, trade, kinds, drains, ends, sems, plane_sems):
    count = state.shape[0]
    pairs = []
    for which, (out, plane) in enumerate(((up, count - 1), (down, 0))):
        pairs += [(state.at[plane], out.at[S]), (conduct.at[plane], out.at[C]), (cotangent.at[plane], out.at[T])]
        pairs += [(labels.at[plane], ends.at[which])]
    copies = load_all(pairs, plane_sems)
    start = (1 - lax.axis_index("gz")) * (count - trade.shape[1])
    copies += load_planes((state, conduct, sink, labels, cotangent), start, trade, kinds, drains, sems)
    for copy in copies:
        copy.wait()
    up[F] = half_fluid(ends[0])
    down[F] = half_fluid(ends[1])
    fill_planes(trade, kinds, drains)


def own_planes(state, conduct, sink, labels, cotangent, mine, kinds, drains, sems):
    start = lax.axis_index("gz") * (state.shape[0] - mine.shape[1])
    for copy in load_planes((state, conduct, sink, labels, cotangent), start, mine, kinds, drains, sems):
        copy.wait()
    fill_planes(mine, kinds, drains)


def pack_rims(two, planes, outs):
    for k in range(0, len(planes), 2):
        even, odd = planes[k], planes[min(k + 1, len(planes) - 1)]
        ny = even.shape[0]
        low_even, high_even = even[0:TILE], even[ny - TILE : ny]
        low_odd, high_odd = odd[0:TILE], odd[ny - TILE : ny]
        upper = rows_of(low_even) < HALO
        low = jnp.where(upper, low_even, pltpu.roll(low_odd, HALO, 0))
        high = jnp.where(upper, pltpu.roll(high_even, HALO, 0), high_odd)
        if two:
            outs[0][k // 2] = jnp.where(lax.axis_index("gy") == 0, high, low)
        else:
            outs[0][k // 2] = low
            outs[1][k // 2] = high


def unpack_rims(two, count_y, rims, planes):
    place = lax.axis_index("gy")
    for k in range(0, len(planes), 2):
        above = jnp.where(place < count_y - 1, rims[0][k // 2], 0.0)
        below = jnp.where(place > 0, rims[0 if two else 1][k // 2], 0.0)
        upper = rows_of(above) < HALO
        planes[k][...] = jnp.where(upper, above, pltpu.roll(below, HALO, 0))
        if k + 1 < len(planes):
            planes[k + 1][...] = jnp.where(upper, pltpu.roll(above, HALO, 0), below)


def gather_planes(mine, traded, block, near):
    core = lax.axis_index("gz")
    half, narrow = block.shape[1], mine.shape[3]
    own = pl.ds(pl.multiple_of(core * narrow, 128), narrow)
    other = pl.ds(pl.multiple_of((1 - core) * narrow, 128), narrow)
    start = 2 * core
    beside = (1 - core) * half + core
    beyond = (1 - core) * (half + 1)
    for j in range(5):
        for i in range(half):
            block[j, i, :, own] = mine[j, start + i]
            block[j, i, :, other] = traded[j, start + i]
        near[j, :, own] = mine[j, beside]
        near[j, :, other] = traded[j, beside]
        if j in (S, C):
            near[5 + j, :, own] = mine[j, beyond]
            near[5 + j, :, other] = traded[j, beyond]


def rim_planes(block, near):
    half = block.shape[1]
    core = lax.axis_index("gz")
    inward = lambda i: core * (half - 1) + i * (1 - 2 * core)
    early = [block.at[j, inward(0)] for j in range(5)] + [block.at[j, inward(1)] for j in (S, C)]
    late = [block.at[j, inward(1)] for j in (T, F, K)] + [block.at[j, inward(i)] for i in range(2, half) for j in range(5)]
    return early, late + [near.at[j] for j in range(7)]


def pack_along_y(two, block, near, *rims):
    early, late = rim_planes(block, near)
    ways = 1 if two else 2
    pack_rims(two, early, rims[:ways])
    pack_rims(two, late, rims[ways:])


class Lazy:
    def __init__(self, count, make):
        self.count, self.make, self.known = count, make, {}

    def __getitem__(self, t):
        t = t % self.count
        if t not in self.known:
            self.known[t] = self.make(t)
        return self.known[t]

    def __len__(self):
        return self.count


def prepare(todo, count_y, block, near, ghost, near_ghost, kx, ky_out, kz_out, diag, part, back, one):
    place = lax.axis_index("gy")
    core = lax.axis_index("gz")
    half, ny = block.shape[1], block.shape[2]
    count, last = ny // TILE + 1, half - 1

    def own(j, i):
        if ghost is None:
            return Tiles(*[(block.at[j, i], t) for t in range(count - 1)], (None, 0))
        return with_ghost(block.at[j, i], ghost.at[j, i])

    def next_to(j):
        if ghost is None:
            return Tiles(*[(near.at[j], t) for t in range(count - 1)], (None, 0))
        return with_ghost(near.at[j], near_ghost.at[j])

    def faces_along_y(c):
        def make(t):
            value = (c[t] + down_rows(c[t - 1], c[t])) * scale
            if t == 0:
                value = jnp.where(jnp.logical_and(rows_of(value) == 0, place == 0), 0.0, value)
            if t == count - 1:
                value = jnp.where(jnp.logical_and(rows_of(value) == 0, place == count_y - 1), 0.0, value)
            return value

        return Lazy(count, make)

    def own_weight(c, f, t):
        here = c[t] * scale
        left, right = sides_along_z(c[t], here)
        low, high = down_rows(c[t - 1], c[t]), up_rows(c[t], c[t + 1])
        return left, (2.0 * here + (low + high) * scale) + (left + right) + time_step * f[t]

    for i in range(half):
        s, c, a, f, k = (own(j, i) for j in (S, C, T, F, K))
        ky, kz = faces_along_y(c), {}
        for t in todo:
            left, weight = own_weight(c, f, t)
            kz[t] = jnp.where(lanes_of(left) == 0, 0.0, left)
            slot = at(todo.index(t))
            if i > 0:
                face = (c[t] + own(C, i - 1)[t]) * scale
                kx[i - 1, slot] = face
                weight = weight + face
            if i < last:
                weight = weight + (c[t] + own(C, i + 1)[t]) * scale
            diag[i, slot] = weight
            ky_out[i, slot] = ky[t]
            kz_out[i, slot] = kz[t]
        scaled = Lazy(count, lambda t, a=a, f=f: a[t] * (0.5 + f[t]))
        ahead = Across(ky, kz, s)
        behind = Across(ky, kz, scaled)
        for t in todo:
            slot = at(todo.index(t))
            d, b = diag[i, slot], scaled[t]
            go = ahead[t] - d * s[t] - time_step * k[t] * jnp.tanh(s[t])
            come = behind[t] - d * b
            if i > 0:
                go = go + (kx[i - 1, slot] + time_step * f[t]) * own(S, i - 1)[t]
                come = come + kx[i - 1, slot] * (own(T, i - 1)[t] * (0.5 + own(F, i - 1)[t]))
            if i < last:
                face, high_f = (c[t] + own(C, i + 1)[t]) * scale, own(F, i + 1)[t]
                go = go + face * own(S, i + 1)[t]
                come = come + (face + time_step * high_f) * (own(T, i + 1)[t] * (0.5 + high_f))
            part[i, slot] = s[t] + (0.5 + f[t]) * go
            back[i, slot] = a[t] + come
    s, c, f, k = (next_to(j) for j in (S, C, F, K))
    kz = {}
    for t in todo:
        left, _ = own_weight(c, f, t)
        kz[t] = jnp.where(lanes_of(left) == 0, 0.0, left)
    ahead = Across(faces_along_y(c), kz, s)
    is_low = core == 0
    for t in todo:
        _, weight = own_weight(c, f, t)
        c_own = jnp.where(is_low, own(C, last)[t], own(C, 0)[t])
        s_own = jnp.where(is_low, own(S, last)[t], own(S, 0)[t])
        face_own, face_far = (c[t] + c_own) * scale, (c[t] + next_to(5 + C)[t]) * scale
        wind = time_step * f[t]
        go = ahead[t] - (weight + face_own + face_far) * s[t] - time_step * k[t] * jnp.tanh(s[t])
        go = go + (face_own + jnp.where(is_low, wind, 0.0)) * s_own
        go = go + (face_far + jnp.where(is_low, 0.0, wind)) * next_to(5 + S)[t]
        one[at(todo.index(t))] = s[t] + (0.5 + f[t]) * go


def prepare_mid(count_y, block, near, *outs):
    prepare(list(range(1, block.shape[2] // TILE - 1)), count_y, block, near, None, None, *outs)


def prepare_rim(two, count_y, block, near, *refs):
    ways = 1 if two else 2
    rims, (ghost, near_ghost, *outs) = refs[: 2 * ways], refs[2 * ways :]
    count = block.shape[2] // TILE
    early, late = rim_planes(ghost, near_ghost)
    unpack_rims(two, count_y, rims[:ways], early)
    unpack_rims(two, count_y, rims[ways:], late)
    prepare([0, count - 1, count], count_y, block, near, ghost, near_ghost, *outs)


PACKED = (((S, 3), (C, 3), (ONE, 2)), ((T, 2), (F, 2)))


def pack_ghosts(place, parts, ghosts):
    rows = rows_of(ghosts[S])
    low = high = jnp.zeros_like(ghosts[S])
    taken = 0
    for j, depth in parts:
        span = jnp.logical_and(rows >= taken, rows < taken + depth)
        low = jnp.where(span, pltpu.roll(ghosts[j], taken, 0) if taken else ghosts[j], low)
        span = jnp.logical_and(rows >= TILE - taken - depth, rows < TILE - taken)
        high = jnp.where(span, pltpu.roll(ghosts[j], TILE - taken, 0) if taken else ghosts[j], high)
        taken += depth
    return jnp.where(place == 0, low, high)


def unpack_ghosts(place, parts, packed):
    rows = rows_of(packed)
    ghosts, taken = {}, 0
    for j, depth in parts:
        low = pltpu.roll(packed, TILE - taken, 0) if taken else packed
        high = pltpu.roll(packed, taken, 0) if taken else packed
        low = jnp.where(rows < depth, low, 0.0)
        high = jnp.where(rows >= TILE - depth, high, 0.0)
        ghosts[j] = jnp.where(place == 0, low, high)
        taken += depth
    return ghosts


def pack_off(two, count_y, block, part_mid, *refs):
    ways = 1 if two else 2
    rims, (off, ghost) = refs[:ways], refs[ways:]
    place = lax.axis_index("gy")
    core = lax.axis_index("gz")
    last = block.shape[1] - 1
    outer = core * last
    inside = outer + 1 - 2 * core
    unpack_rims(two, count_y, rims, [ghost.at[j] for j in range(7)])
    s, c, f, k = (with_ghost(block.at[j, outer], ghost.at[j]) for j in (S, C, F, K))
    s_in, c_in = (with_ghost(block.at[j, inside], ghost.at[5 + j]) for j in (S, C))
    count = len(s)

    def face_along_y(t):
        value = (c[t] + down_rows(c[t - 1], c[t])) * scale
        if t == 0:
            value = jnp.where(jnp.logical_and(rows_of(value) == 0, place == 0), 0.0, value)
        if t == count - 1:
            value = jnp.where(jnp.logical_and(rows_of(value) == 0, place == count_y - 1), 0.0, value)
        return value

    todo, kz, weight = (0, count - 2, count - 1), {}, {}
    for t in todo:
        here = c[t] * scale
        left, right = sides_along_z(c[t], here)
        kz[t] = jnp.where(lanes_of(left) == 0, 0.0, left)
        low, high = down_rows(c[t - 1], c[t]), up_rows(c[t], c[t + 1])
        weight[t] = (2.0 * here + (low + high) * scale) + (left + right) + time_step * f[t]
    flow = Across(Lazy(count, face_along_y), kz, s)
    one = {}
    for t in range(count):
        if t in todo:
            face = (c[t] + c_in[t]) * scale
            go = flow[t] - (weight[t] + face) * s[t] - time_step * k[t] * jnp.tanh(s[t])
            go = go + (face + jnp.where(core == 0, 0.0, time_step) * f[t]) * s_in[t]
            one[t] = s[t] + (0.5 + f[t]) * go
        else:
            one[t] = part_mid[outer, at(t - 1)]
        if t < count - 1:
            off[at(t)] = one[t]
    ghosts = {j: ghost[j] for j in range(4)}
    ghosts[ONE] = one[count - 1]
    if two:
        for slot, parts in enumerate(PACKED):
            off[at(count - 1 + slot)] = pack_ghosts(place, parts, ghosts)
    else:
        for j in range(5):
            off[at(count - 1 + j)] = ghosts[j]


def choose_half(up, down, *refs):
    for j in range(4):
        refs[j - 4][...] = jnp.where(lax.axis_index("gz") == 0, down[j], up[j])


def coefficients(refs):
    mids, rims = refs[:6], refs[7:13]
    return [lambda i, m=m, r=r: mid_and_rim(m.at[i], r.at[i]) for m, r in zip(mids, rims)]


def fill_sides(near, near_ghost, up, down, passed, side):
    core = lax.axis_index("gz")
    ny, narrow = up.shape[1], up.shape[2]
    outside, inside = core, 1 - core
    for j in range(4):
        side[j, outside, 0:ny, 0:narrow] = jnp.where(core == 0, up[j], passed[j][...])
        side[j, outside, 0:ny, narrow : 2 * narrow] = jnp.where(core == 0, passed[j][...], down[j])
        side[j, inside, 0:ny] = near[j]
        side[j, inside, ny : ny + TILE] = near_ghost[j]


def fill_side_ghosts(two, ny, off, side):
    place, outside = lax.axis_index("gy"), lax.axis_index("gz")
    first = ny // TILE
    if two:
        ghosts = {}
        for slot, parts in enumerate(PACKED):
            ghosts.update(unpack_ghosts(place, parts, off[at(first + slot)]))
    else:
        ghosts = {j: off[at(first + j)] for j in range(5)}
    for j in range(4):
        for which in range(2):
            place = (j, which, slice(ny, ny + TILE))
            side[place] = jnp.where(outside == which, ghosts[j], side[place])
    return ghosts[ONE]


def sweep(late, block, ghost, weights, side, edge, add, first, known, linear, adjoint, sa, b2, hot2, inward):
    kx, ky, kz, diag, part, back = weights
    half, ny = block.shape[1], block.shape[2]
    count, last = ny // TILE, half - 1
    own = lambda j, i: with_ghost(block.at[j, i], ghost.at[j, i])
    for which, i in ((0, 0), (1, last)):
        s, f, c = own(S, i), own(F, i), own(C, i)
        s_out, c_out, f_out = (whole(side.at[j, which]) for j in (S, C, F))
        for t in [count] if late else range(count):
            face = (c[t] + c_out[t]) * scale
            edge[which, at(t)] = face
            v, beyond = s[t], s_out[t]
            if which == 0:
                inner_add = (face + time_step * f[t]) * beyond - face * v
                outer_add = face * (v - beyond)
            else:
                inner_add = face * (beyond - v)
                outer_add = (face + time_step * f_out[t]) * v - face * beyond
            first[i, at(t)] = part(i)[t] + (0.5 + f[t]) * inner_add
            add[which, at(t)] = (0.5 + f_out[t]) * outer_add
    for i in range(1, last):
        for t in [] if late else range(count + 1):
            first[i, at(t)] = part(i)[t]
    for i in range(half):
        outer = i in (0, last)
        v, f, k, s, a = whole(first.at[i]), own(F, i), own(K, i), own(S, i), own(T, i)
        flow = Across(ky(i), kz(i), v)
        if outer:
            todo = [0, count - 1, count] if late else range(1, count - 1)
        else:
            todo = [count] if late else range(count)
        for t in todo:
            rc = 0.5 + f[t]
            sink = time_step * k[t]
            hot1 = jnp.tanh(v[t])
            full = diag(i)[t]
            if i == 0:
                full = full + edge[0, at(t)]
            if i == last:
                full = full + edge[1, at(t)]
            adjoint[i, at(t)] = full + sink * (1.0 - hot1 * hot1)
            rate = flow[t] - full * v[t] - sink * hot1
            if i > 0:
                rate = rate + (kx(i - 1)[t] + time_step * f[t]) * first[i - 1, at(t)]
            if i < last:
                rate = rate + kx(i)[t] * first[i + 1, at(t)]
            value = 0.75 * s[t] + 0.25 * (v[t] + rc * rate)
            b = a[t] * rc
            total = back(i)[t]
            if i == 0:
                total = total + edge[0, at(t)] * (side[T, 0, at(t)] * (0.5 + side[F, 0, at(t)]) - b)
            if i == last:
                high, high_f = edge[1, at(t)], side[F, 1, at(t)]
                total = total + ((high + time_step * high_f) * (side[T, 1, at(t)] * (0.5 + high_f)) - high * b)
            if outer:
                which = 0 if i == 0 else 1
                known[which, at(t)] = value
                linear[which, at(t)] = total
            else:
                hot = jnp.tanh(value)
                hot2[i, at(t)] = hot
                total = (2.0 / 3.0) * (total - sink * (1.0 - hot * hot) * b)
                sa[i, at(t)] = total
                b2[i, at(t)] = total * rc
    for t in [count] if late else range(count):
        inward[0, at(t)] = (kx(0)[t] + time_step * own(F, 1)[t]) * b2[1, at(t)]
        inward[1, at(t)] = kx(last - 1)[t] * b2[last - 1, at(t)]


def middle(block, ghost, near, near_ghost, up, down, *refs):
    passed, weights, outs = refs[:4], coefficients(refs[4:18]), refs[18:]
    fill_sides(near, near_ghost, up, down, passed, outs[0])
    sweep(False, block, ghost, weights, *outs)


def outward(two, block, ghost, off, *refs):
    weights, one_mid, one_rim = coefficients(refs[:14]), refs[6], refs[13]
    outs = [Draft(ref) for ref in refs[14 + SWEPT : 14 + 2 * SWEPT]]
    *ends, off_b = refs[14 + 2 * SWEPT :]
    hot2, sa, b2 = (Draft(ref) for ref in ends)
    side, edge, add, _, known, linear, *_ = outs
    core = lax.axis_index("gz")
    half, ny = block.shape[1], block.shape[2]
    count, last = ny // TILE, half - 1
    own = lambda j, i: with_ghost(block.at[j, i], ghost.at[j, i])
    one_ghost = fill_side_ghosts(two, ny, off, side)
    sweep(True, block, ghost, weights, *outs)
    for which, i in ((0, 0), (1, last)):
        f, k, a = own(F, i), own(K, i), own(T, i)
        mine = core == which
        for t in range(count + 1):
            one = off[at(t)] if t < count else one_ghost
            one = jnp.where(mine, one + add[which, at(t)], mid_and_rim(one_mid, one_rim)[t])
            face = edge[which, at(t)]
            if which == 0:
                face = face + time_step * f[t]
            rc = 0.5 + f[t]
            hot = jnp.tanh(known[which, at(t)] + 0.25 * rc * face * one)
            total = (2.0 / 3.0) * (linear[which, at(t)] - time_step * k[t] * (1.0 - hot * hot) * (a[t] * rc))
            hot2[which, at(t)] = hot
            sa[which, at(t)] = total
            b2[which, at(t)] = total * rc
    for t in range(count + 1):
        off_b[at(t)] = jnp.where(core == 0, b2[0, at(t)], b2[1, at(t)])
    for draft in (b2, sa, hot2, *outs):
        draft.flush()


def inside_adjoint(block, ghost, near, near_ghost, *refs):
    (kx, ky, kz, diag, part, back), on_b = coefficients(refs[:14]), refs[14]
    core = lax.axis_index("gz")
    half, ny = block.shape[1], block.shape[2]
    last = half - 1
    i = (1 - core) * last
    beside = i - 1 + 2 * core
    own = lambda j, plane: with_ghost(block.at[j, plane], ghost.at[j, plane])
    c_h, s_h, t_h, f_h = (with_ghost(near.at[j], near_ghost.at[j]) for j in (C, S, T, F))
    one = mid_and_rim(refs[6], refs[13])
    s, c, a, f, k = (own(j, i) for j in (S, C, T, F, K))
    above, below = jnp.where(core == 0, time_step, 0.0), jnp.where(core == 0, 0.0, time_step)
    step, next_first = kx((1 - core) * (last - 1)), part(beside)
    faces, first = [], []
    for t in range(ny // TILE + 1):
        faces.append((c[t] + c_h[t]) * scale)
        first.append(part(i)[t] + (0.5 + f[t]) * ((faces[t] + below * f[t]) * s_h[t] - faces[t] * s[t]))
    flow = Across(ky(i), kz(i), Made(first))
    out = []
    for t in range(ny // TILE + 1):
        rc, sink, face = 0.5 + f[t], time_step * k[t], faces[t]
        rate = flow[t] - (diag(i)[t] + face) * first[t] - sink * jnp.tanh(first[t])
        rate = rate + (step[t] + above * f[t]) * next_first[t] + (face + below * f[t]) * one[t]
        hot = jnp.tanh(0.75 * s[t] + 0.25 * (first[t] + rc * rate))
        b = a[t] * rc
        total = back(i)[t] + (face + above * f_h[t]) * (t_h[t] * (0.5 + f_h[t])) - face * b
        out.append((2.0 / 3.0) * (total - sink * (1.0 - hot * hot) * b) * rc)
    put(on_b, out)


def outward_first(ky_mid, kz_mid, ky_rim, kz_rim, adjoint, inward, sa, b2, fa, *parts):
    inside_keep, inside_give, along, cross = parts
    core = lax.axis_index("gz")
    half, ny = adjoint.shape[0], along.shape[0]
    values = []
    for which, i in ((0, 0), (1, half - 1)):
        b = whole(b2.at[which])
        flow = Across(mid_and_rim(ky_mid.at[i], ky_rim.at[i]), mid_and_rim(kz_mid.at[i], kz_rim.at[i]), b)
        total = lambda t: sa[which, at(t)] + flow[t] - adjoint[i, at(t)] * b[t] + inward[which, at(t)]
        values.append([0.25 * total(t) for t in range(len(b))])
    low, high = values
    for t in range(ny // TILE):
        along[at(t)], cross[at(t)] = halves(core, jnp.where(core == 0, low[t], high[t]))
        inside_keep[at(t)], inside_give[at(t)] = halves(core, jnp.where(core == 0, high[t], low[t]))
    for which in range(2):
        put(fa.at[which], values[which])


def inner(block, ghost, edge, side, first, adjoint, sa_in, b2_in, hot2_in, sa_out, b2_out, hot2_out, fa_out, *refs):
    kx, ky, kz, diag, _, _ = coefficients(refs[:14])
    value, term, adjoint0, hot0, fa, b3 = refs[14:]
    half, ny = block.shape[1], block.shape[2]
    count, last = ny // TILE, half - 1
    own = lambda j, i: with_ghost(block.at[j, i], ghost.at[j, i])
    pick = lambda i, inside, outside: inside.at[i] if 0 < i < last else outside.at[0 if i == 0 else 1]
    sa = lambda i: whole(pick(i, sa_in, sa_out))
    b2 = lambda i: whole(pick(i, b2_in, b2_out))
    hot2 = lambda i: whole(pick(i, hot2_in, hot2_out))
    for i in range(half):
        f = own(F, i)
        flow = Across(ky(i), kz(i), b2(i))
        for t in range(count + 1):
            if 0 < i < last:
                total = sa(i)[t] + flow[t] - adjoint[i, at(t)] * b2(i)[t]
                total = total + kx(i - 1)[t] * b2(i - 1)[t] + (kx(i)[t] + time_step * own(F, i + 1)[t]) * b2(i + 1)[t]
                total = 0.25 * total
            else:
                total = fa_out[0 if i == 0 else 1, at(t)]
            fa[i, at(t)] = total
            b3[i, at(t)] = total * (0.5 + f[t])
    for i in range(half):
        s, f, k, a = own(S, i), own(F, i), own(K, i), own(T, i)
        b = whole(b3.at[i])
        flow = Across(ky(i), kz(i), b)
        for t in range(count):
            hot = jnp.tanh(s[t])
            full = diag(i)[t]
            if i == 0:
                full = full + edge[0, at(t)]
            if i == last:
                full = full + edge[1, at(t)]
            full = full + time_step * k[t] * (1.0 - hot * hot)
            total = flow[t] - full * b[t] + fa[i, at(t)] + 0.75 * sa(i)[t] + a[t] * (1.0 / 3.0)
            if i > 0:
                total = total + kx(i - 1)[t] * b3[i - 1, at(t)]
            if i < last:
                total = total + (kx(i)[t] + time_step * own(F, i + 1)[t]) * b3[i + 1, at(t)]
            value[i, at(t)] = total
            first_hot = jnp.tanh(first[i, at(t)])
            total = (2.0 / 3.0) * hot2(i)[t] * a[t] + 0.25 * first_hot * sa(i)[t] + hot * fa[i, at(t)]
            term[i, at(t)] = -time_step * (0.5 + f[t]) * total
            if i == 0 or i == last:
                which = 0 if i == 0 else 1
                adjoint0[which, at(t)] = full
                hot0[which, at(t)] = -time_step * (0.5 + f[t]) * hot


def halves(core, value):
    narrow = value.shape[1] // 2
    left, right = value[:, :narrow], value[:, narrow:]
    return jnp.where(core == 0, left, right), jnp.where(core == 0, right, left)


def from_beyond(which, message, block, ghost, edge, side, b2_out, value, term, adjoint0, hot0, weights):
    kx, ky, kz = weights
    half, ny = block.shape[1], block.shape[2]
    count, last = ny // TILE, half - 1
    i = which * last
    beside = i + 1 - 2 * which
    wind = jnp.where(which == 1, time_step, 0.0)
    against = time_step - wind
    f = with_ghost(block.at[F, i], ghost.at[F, i])
    into, gains, late = [], [], []
    for t in range(count + 1):
        into.append(edge[which, at(t)] + wind * side[F, which, at(t)])
        gains.append(0.25 * into[t] * message[at(t)])
        late.append(gains[t] * (0.5 + f[t]))
    flow = Across(ky(i), kz(i), Made(late))
    step = kx(which * (last - 1))
    out = []
    for t in range(count):
        factor = into[t] * (0.5 + side[F, which, at(t)])
        known = 0.25 * (edge[which, at(t)] + against * f[t]) * b2_out[which, at(t)]
        total = value[i, at(t)] + gains[t] + flow[t] - adjoint0[which, at(t)] * late[t] + factor * known
        next_total = value[beside, at(t)] + (step[t] + wind * f[t]) * late[t]
        out.append((t, total, next_total, term[i, at(t)] + hot0[which, at(t)] * gains[t], factor))
    return out


def three(refs):
    return [lambda i, m=m, r=r: mid_and_rim(m.at[i], r.at[i]) for m, r in zip(refs[:3], refs[3:])]


def finish_inside(block, ghost, edge, side, b2_out, value, term, adjoint0, hot0, on_b, *refs):
    *six, keep, give = refs
    core = lax.axis_index("gz")
    half, ny = block.shape[1], block.shape[2]
    plane = lambda r: core * (half - 1) + r * (1 - 2 * core)

    def write(place, t, value):
        keep[place, at(t)], give[place, at(t)] = halves(core, value)

    parts = from_beyond(1 - core, on_b, block, ghost, edge, side, b2_out, value, term, adjoint0, hot0, three(six))
    for t, total, next_total, sink, factor in parts:
        write(half - 3, t, total)
        write(half - 4, t, next_total)
        write(2 * half - 4, t, sink)
        write(2 * half - 2, t, factor)
        for r in range(2, half - 2):
            write(r - 2, t, value[plane(r), at(t)])
        for r in range(1, half - 1):
            write(half - 3 + r, t, term[plane(r), at(t)])
        wind = jnp.where(core == 1, time_step, 0.0)
        f_out = side[F, core, at(t)]
        write(2 * half - 3, t, (edge[core, at(t)] + wind * f_out) * (0.5 + f_out))


def finish_outside(block, ghost, edge, side, b2_out, value, term, adjoint0, hot0, off_b, *refs):
    *six, _, keep, give = refs
    core = lax.axis_index("gz")
    parts = from_beyond(core, off_b, block, ghost, edge, side, b2_out, value, term, adjoint0, hot0, three(six))
    for t, total, next_total, sink, _ in parts:
        for place, value_here in enumerate((total, next_total, sink)):
            keep[place, at(t)], give[place, at(t)] = halves(core, value_here)


def take(cross, along, cross_out, along_out):
    cross_out[...] = cross[...]
    along_out[...] = along[...]


def assemble(labels, keep, got, keep_last, got_last, inside_keep, inside_got, along, cross, grad_state, grad_sink, *refs):
    masked, ends, sems = refs
    core = lax.axis_index("gz")
    count = grad_state.shape[0]
    half = count // 2
    copies = []

    def send(source, target):
        copies.append(pltpu.make_async_copy(source, target, sems.at[len(copies)]))
        copies[-1].start()

    sides = ((core, keep, keep_last, inside_got, cross), (1 - core, got, got_last, inside_keep, along))
    plane = lambda who, r: who * (count - 1) + r * (1 - 2 * who)
    for who, most, outermost, _, _ in sides:
        send(outermost.at[1], grad_state.at[plane(who, 1)])
        for r in range(2, half - 1):
            send(most.at[r - 2], grad_state.at[plane(who, r)])
    for slot, (who, most, outermost, inside, outside) in enumerate(sides):
        ends[slot, 0] = outermost[0] + most[2 * half - 3] * outside[...]
        send(ends.at[slot, 0], grad_state.at[plane(who, 0)])
        ends[slot, 1] = most[half - 3] + most[2 * half - 2] * inside[...]
        send(ends.at[slot, 1], grad_state.at[plane(who, half - 1)])
        for r in range(half):
            term = outermost[2] if r == 0 else most[half - 3 + r]
            place = plane(who, r)
            masked[slot, place - who * half] = jnp.where(touching(labels[place]), term, 0.0)
        send(masked.at[slot], grad_sink.at[pl.ds(who * half, half)])
    for copy in copies:
        copy.wait()


def on_device(state, conduct, sink, labels, cotangent):
    count, ny, nz = state.shape
    half, wide, rows = count // 2, 2 * nz, ny + TILE
    count_x, count_y = lax.axis_size("gx"), lax.axis_size("gy")
    assert lax.axis_size("gz") == 2 and half >= 4 and ny % TILE == 0 and ny >= 3 * TILE
    two = count_y == 2
    ahead = [(i, (i + 1) % count_x) for i in range(count_x)]
    behind = [(b, a) for a, b in ahead]
    chips = [(2 * i + 1, (2 * i + 2) % (2 * count_x)) for i in range(count_x)]
    chips = chips + [(b, a) for a, b in chips]

    def swap_cores(x):
        return lax.ppermute(x, "gz", [(0, 1), (1, 0)])

    def swap_chips(x):
        return lax.ppermute(x, ("gx", "gz"), chips)

    def to_slabs(x):
        route = [(2 * i + c, 2 * ((i + 2 * c - 1) % count_x) + c) for i in range(count_x) for c in range(2)]
        return lax.ppermute(x, ("gx", "gz"), route)

    def along_y(rims):
        forward = [(i, (i + 1) % count_y) for i in range(count_y)]
        backward = [(b, a) for a, b in forward]
        routes = [forward] if two else [backward, forward]
        return [lax.ppermute(rim, "gy", routes[i % len(routes)]) for i, rim in enumerate(rims)]

    ways = 1 if two else 2
    inputs = (state, conduct, sink, labels, cotangent)
    plane, span = (4, ny, nz), (5, half + 2, ny, nz)
    kinds = pltpu.VMEM((half + 2, ny, nz), jnp.int32)
    drains = pltpu.VMEM((half + 2, ny, nz), jnp.float32)
    sems = lambda many: pltpu.SemaphoreType.DMA((many,))
    up, down, trade = call(
        pack_inputs, [plane, plane, span], *inputs, given=HBM,
        scratch=[kinds, drains, pltpu.VMEM((2, ny, nz), jnp.int32), sems(5), sems(8)],
    )
    up = lax.ppermute(up, "gx", ahead)
    down = lax.ppermute(down, "gx", behind)
    traded = swap_cores(trade)
    (mine,) = call(own_planes, [span], *inputs, given=HBM, scratch=[kinds, drains, sems(5)])
    block, near = call(gather_planes, [(5, half, ny, wide), (7, ny, wide)], mine, traded)
    sizes = [4, (5 * half + 1) // 2]
    rims = call(functools.partial(pack_along_y, two), [(n, TILE, wide) for n in sizes for _ in range(ways)], block, near)
    rims = along_y(rims)
    split = lambda r: [(half - 1, r, wide)] + [(half, r, wide)] * 5 + [(r, wide)]
    mids = call(functools.partial(prepare_mid, count_y), split(ny - 2 * TILE), block, near)
    ghost, near_ghost, *edges = call(
        functools.partial(prepare_rim, two, count_y),
        [(5, half, TILE, wide), (7, TILE, wide)] + split(3 * TILE), block, near, *rims,
    )
    off, _ = call(
        functools.partial(pack_off, two, count_y), [(ny + (len(PACKED) if two else 5) * TILE, wide), (7, TILE, wide)],
        block, mids[4], *rims[:ways], flops=PACK_FLOPS,
    )
    passed = call(choose_half, [(ny, nz)] * 4, up, down, *rims)
    passed = [swap_cores(x) for x in passed]
    off = swap_chips(off)
    own, outer = (half, rows, wide), (2, rows, wide)
    (on_b,) = call(inside_adjoint, [(rows, wide)], block, ghost, near, near_ghost, *mids, *edges)
    on_b = swap_cores(on_b)
    swept_shapes = [(4, 2, rows, wide), outer, outer, own, outer, outer, own, own, own, own, outer]
    assert len(swept_shapes) == SWEPT
    swept = call(middle, swept_shapes, block, ghost, near, near_ghost, up, down, *passed, *mids, *edges)
    ends, mains = (rows, wide), (ny, wide)
    *swept, hot2_out, sa_out, b2_out, off_b = call(
        functools.partial(outward, two), swept_shapes + [outer] * 3 + [ends], block, ghost, off, *mids, *edges, *swept,
        aliases={17 + i: i for i in range(SWEPT)},
    )
    side, edge, add, first, known, linear, adjoint, sa, b2, hot2, inward = swept
    off_b = swap_chips(off_b)
    half_plane = (ny, nz)
    fa_out, inside_keep, inside_give, along, cross = call(
        outward_first, [outer] + [half_plane] * 4,
        mids[1], mids[2], edges[1], edges[2], adjoint, inward, sa_out, b2_out,
    )
    cross, along = swap_chips(cross), to_slabs(along)
    inside_got = swap_cores(inside_give)
    main = lambda planes: (planes, ny, wide)
    planes = lambda many: (many, ny, nz)
    value, term, adjoint0, hot0, _, _ = call(
        inner, [main(half), main(half), main(2), main(2), own, own],
        block, ghost, edge, side, first, adjoint, sa, b2, hot2, sa_out, b2_out, hot2_out, fa_out, *mids, *edges,
    )
    ready = (block, ghost, edge, side, b2_out, value, term, adjoint0, hot0)
    keep, give = call(finish_inside, [planes(2 * half - 1)] * 2, *ready, on_b, *mids[:3], *edges[:3])
    got = swap_cores(give)
    keep_last, give_last = call(finish_outside, [planes(3)] * 2, *ready, off_b, *mids[:3], *edges[:3], keep, flops=LAST_FLOPS)
    got_last = swap_cores(give_last)
    cross, along = call(take, [half_plane] * 2, cross, along, flops=FLOPS)
    grad_state, grad_sink = call(
        assemble, [state.shape, state.shape],
        labels, keep, got, keep_last, got_last, inside_keep, inside_got, along, cross, keep=False,
        scratch=[pltpu.VMEM((2, half, ny, nz), jnp.float32), pltpu.VMEM((2, 2, ny, nz), jnp.float32), pltpu.SemaphoreType.DMA((2 * half + 4,))],
    )
    return (grad_state, grad_sink)


def solution(mesh):
    block = P(("groups", "gx"), "gy", "gz")
    in_specs = (block, P("gx", "gy", "gz"), block, block, block)
    return jax.shard_map(on_device, mesh=mesh, in_specs=in_specs, out_specs=(block, block), check_vma=False)
```
